32 devices in a mesh: seq: 2 (over x), shard: 16 (over z, y, core).
Axes of the slice: x: 2, y: 2, z: 4, core: 2. Of those that a mesh axis runs over, the one named last changes fastest.
Arguments:
- features: bfloat16 [32, 768, 512], P('shard', 'seq'), may hold values from -6 to 6
- time_mask: int32 [32, 768], P('shard', 'seq'), may hold values from 0 to 1, as said below
- negatives: int32 [32, 768, 100], P('shard', 'seq'), may hold values from 0 to 767, as said below
- target_codes: int32 [32, 768, 2], P('shard', 'seq'), may hold values from 0 to 319
- feature_weight: float32 [512, 768], P('shard'), may hold values from -0.25 to 0.25
- feature_first: float32 [512, 768], P('shard')
- feature_second: float32 [512, 768], P('shard')
- conv_weight: float32 [6144, 768], P('shard'), may hold values from -0.15625 to 0.15625
- conv_first: float32 [6144, 768], P('shard')
- conv_second: float32 [6144, 768], P('shard')
- attention_weight: float32 [8, 768, 768], P(None, 'shard')
- attention_first: float32 [8, 768, 768], P(None, 'shard')
- attention_second: float32 [8, 768, 768], P(None, 'shard')
- left_basis_t: float32 [8, 768, 768], P(None, 'shard'), may hold values from -1 to 1, as said below
- right_orthogonal_basis: float32 [8, 768, 768], replicated, may hold values from -1 to 1
- expand_weight: float32 [2, 768, 3072], P(None, 'shard'), may hold values from -0.21875 to 0.21875
- expand_first: float32 [2, 768, 3072], P(None, 'shard')
- expand_second: float32 [2, 768, 3072], P(None, 'shard')
- shrink_weight: float32 [2, 3072, 768], P(None, 'shard'), may hold values from -0.109375 to 0.109375
- shrink_first: float32 [2, 3072, 768], P(None, 'shard')
- shrink_second: float32 [2, 3072, 768], P(None, 'shard')
- final_weight: float32 [768, 256], P('shard'), may hold values from -0.21875 to 0.21875
- final_first: float32 [768, 256], P('shard')
- final_second: float32 [768, 256], P('shard')
- target_weight: float32 [256, 256], P('shard'), may hold values from -0.375 to 0.375
- target_first: float32 [256, 256], P('shard')
- target_second: float32 [256, 256], P('shard')
- codebook_weight: float32 [256, 320], P('shard'), may hold values from -6 to 6
- codebook_first: float32 [256, 320], P('shard')
- codebook_second: float32 [256, 320], P('shard')
- vector_params: float32 [23808], P('shard')
- vector_first: float32 [23808], P('shard')
- vector_second: float32 [23808], P('shard')
Outputs:
- loss_total: float32 [2], replicated
- new_feature_weight: float32 [512, 768], P('shard')
- new_feature_first: float32 [512, 768], P('shard')
- new_feature_second: float32 [512, 768], P('shard')
- new_conv_weight: float32 [6144, 768], P('shard')
- new_conv_first: float32 [6144, 768], P('shard')
- new_conv_second: float32 [6144, 768], P('shard')
- new_attention_weight: float32 [8, 768, 768], P(None, 'shard')
- new_attention_first: float32 [8, 768, 768], P(None, 'shard')
- new_attention_second: float32 [8, 768, 768], P(None, 'shard')
- new_expand_weight: float32 [2, 768, 3072], P(None, 'shard')
- new_expand_first: float32 [2, 768, 3072], P(None, 'shard')
- new_expand_second: float32 [2, 768, 3072], P(None, 'shard')
- new_shrink_weight: float32 [2, 3072, 768], P(None, 'shard')
- new_shrink_first: float32 [2, 3072, 768], P(None, 'shard')
- new_shrink_second: float32 [2, 3072, 768], P(None, 'shard')
- new_final_weight: float32 [768, 256], P('shard')
- new_final_first: float32 [768, 256], P('shard')
- new_final_second: float32 [768, 256], P('shard')
- new_target_weight: float32 [256, 256], P('shard')
- new_target_first: float32 [256, 256], P('shard')
- new_target_second: float32 [256, 256], P('shard')
- new_codebook_weight: float32 [256, 320], P('shard')
- new_codebook_first: float32 [256, 320], P('shard')
- new_codebook_second: float32 [256, 320], P('shard')
- new_vector_params: float32 [23808], P('shard')
- new_vector_first: float32 [23808], P('shard')
- new_vector_second: float32 [23808], P('shard')
The draws below stay inside these ranges and needn't reach their ends.
Inputs may be any that keep to these rules, and one draw needn't show every extreme that they name: `time_mask`: masked frames come in runs of 10 that start at random; runs start more often late in a clip and in later clips. `negatives`: frame indices within the same clip, never the frame itself. `left_basis_t`: each matrix is orthogonal.
All inputs are finite; a program needn't handle non-finite values.
Results may differ from the reference program's by a relative error of at most 0.018.
Values may be sent and summed in bfloat16 or wider, within the bound.
A program may use at most 512 MiB of HBM per device.

```python
import math
import jax
import jax.numpy as jnp
from jax import lax

D = 768
HEADS = 12
HDIM = 64
FF = 3072
CIN = 512
KW = 128
GROUPS = 16
PROJ = 256
CODES = 320
QGROUPS = 2
NEG = 100
LAYERS = 2
LEN = 768
STEP = 10
CLIPS = 32
NV = 23808


def moment_draw(key, shape, decay, second, boost=1.0):
    grad_size = 0.012 / math.sqrt(CLIPS * LEN)
    share_fraction = (1.0 - decay) / decay
    if second:
        factor = jnp.exp(jax.random.uniform(key, shape, jnp.float32, math.log(0.5), math.log(8.0)))
        return boost * share_fraction * grad_size * grad_size * factor
    return boost * share_fraction * grad_size * jax.random.normal(key, shape, jnp.float32)


def basis_set(key):
    count = 4 * LAYERS
    orders = jax.vmap(lambda sub_key: jax.random.permutation(sub_key, D))(jax.random.split(key, count))
    flips = jnp.where(jax.random.uniform(jax.random.fold_in(key, 1), (count, D)) < 0.5, -1.0, 1.0)
    freq = jnp.arange(D)[:, None].astype(jnp.float32)
    place = jnp.arange(D)[None, :].astype(jnp.float32)
    table = jnp.cos(math.pi * (place + 0.5) * freq / D) * math.sqrt(2.0 / D)
    table = jnp.where(freq == 0.0, table * math.sqrt(0.5), table)
    rotated_gradient = jax.vmap(lambda order: table[:, order])(orders)
    return flips[:, :, None] * rotated_gradient


def draw_time_mask(key, part):
    key = jax.random.fold_in(key, 11)
    timestep_offsets = jnp.arange(LEN)[None, :]
    clip_ids = jnp.arange(CLIPS)[:, None]
    limit = 8 * (LEN + 2 * timestep_offsets) * (CLIPS + 2 * clip_ids) // (LEN * CLIPS)
    starts = (jax.random.randint(key, (CLIPS, LEN), 0, 1000) < limit).astype(jnp.int32)
    padded = jnp.pad(starts, ((0, 0), (9, 0)))
    spans = starts
    for offset in range(1, 10):
        spans = jnp.maximum(spans, padded[:, 9 - offset:9 - offset + LEN])
    return spans


def draw_negatives(key, part):
    key = jax.random.fold_in(key, 12)
    picks = jax.random.randint(key, (CLIPS, LEN, NEG), 0, LEN - 1)
    timestep_offsets = jnp.arange(LEN)[None, :, None]
    return picks + (picks >= timestep_offsets).astype(jnp.int32)


def draw_attention_weight(key, part):
    key = jax.random.fold_in(key, 13)
    base = jax.random.normal(key, (4 * LAYERS, D, D), jnp.float32) * D ** (-0.5)
    boost = jnp.where(jnp.arange(4 * LAYERS) % 4 == 3, math.sqrt(LEN) / 2.0, 1.0)
    return base * boost[:, None, None]


def draw_left_basis_t(key, part):
    return basis_set(jax.random.fold_in(key, 14))


def draw_right_orthogonal_basis(key, part):
    return basis_set(jax.random.fold_in(key, 15))


def draw_vector_params(key, part):
    key = jax.random.fold_in(key, 16)
    kinds = [(CIN, 1), (CIN, 0), (D, 0), (D, 2), (D, 0), (D, 1), (D, 0)]
    kinds = kinds + [(D, 0), (D, 0), (D, 0), (D, 1), (D, 0), (FF, 0), (D, 0), (D, 1), (D, 0)] * LAYERS
    kinds = kinds + [(PROJ, 0), (PROJ, 0)]
    scales = jnp.concatenate([jnp.full((width,), [0.1, 0.2, 1.0][kind], jnp.float32) for width, kind in kinds])
    shifts = jnp.concatenate([jnp.full((width,), 1.0 if kind == 1 else 0.0, jnp.float32) for width, kind in kinds])
    return shifts + scales * jax.random.normal(key, (NV,), jnp.float32)


def draw_feature_first(key, part):
    return moment_draw(jax.random.fold_in(key, 21), (CIN, D), 0.9, False)


def draw_feature_second(key, part):
    return moment_draw(jax.random.fold_in(key, 22), (CIN, D), 0.95, True)


def draw_conv_first(key, part):
    return moment_draw(jax.random.fold_in(key, 23), (KW * (D // GROUPS), D), 0.9, False)


def draw_conv_second(key, part):
    return moment_draw(jax.random.fold_in(key, 24), (KW * (D // GROUPS), D), 0.95, True)


def draw_attention_first(key, part):
    return moment_draw(jax.random.fold_in(key, 25), (4 * LAYERS, D, D), 0.5, False)


def draw_attention_second(key, part):
    return moment_draw(jax.random.fold_in(key, 26), (4 * LAYERS, D, D), 0.5, True, 3.0)


def draw_expand_first(key, part):
    return moment_draw(jax.random.fold_in(key, 27), (LAYERS, D, FF), 0.9, False)


def draw_expand_second(key, part):
    return moment_draw(jax.random.fold_in(key, 28), (LAYERS, D, FF), 0.95, True, 3.0)


def draw_shrink_first(key, part):
    return moment_draw(jax.random.fold_in(key, 29), (LAYERS, FF, D), 0.9, False)


def draw_shrink_second(key, part):
    return moment_draw(jax.random.fold_in(key, 30), (LAYERS, FF, D), 0.95, True, 4.0)


def draw_final_first(key, part):
    return moment_draw(jax.random.fold_in(key, 31), (D, PROJ), 0.9, False)


def draw_final_second(key, part):
    return moment_draw(jax.random.fold_in(key, 32), (D, PROJ), 0.95, True, 12.0)


def draw_target_first(key, part):
    return moment_draw(jax.random.fold_in(key, 33), (PROJ, PROJ), 0.9, False)


def draw_target_second(key, part):
    return moment_draw(jax.random.fold_in(key, 34), (PROJ, PROJ), 0.95, True, 30.0)


def draw_codebook_first(key, part):
    return moment_draw(jax.random.fold_in(key, 35), (PROJ, CODES), 0.9, False, 0.25)


def draw_codebook_second(key, part):
    return moment_draw(jax.random.fold_in(key, 36), (PROJ, CODES), 0.95, True, 0.05)


def draw_vector_first(key, part):
    return moment_draw(jax.random.fold_in(key, 37), (NV,), 0.9, False)


def draw_vector_second(key, part):
    return moment_draw(jax.random.fold_in(key, 38), (NV,), 0.95, True)


def place_ends(values, rng, smallest, top_value):
    index_at = [jax.random.randint(jax.random.fold_in(rng, axis), (), 0, length) for axis, length in enumerate(values.shape)]
    longest = values.shape.index(max(values.shape))
    neighbour = index_at[:longest] + [(index_at[longest] + 1) % values.shape[longest]] + index_at[longest + 1:]
    return values.at[tuple(index_at)].set(smallest).at[tuple(neighbour)].set(top_value)


def level_of(key, dims, shards, smallest, high):
    def one(position, parts):
        steps = jax.random.uniform(jax.random.fold_in(jax.random.fold_in(key, 6), position), (parts,), jnp.float32, smallest / len(shards), high / len(shards))
        return jnp.repeat(jnp.exp(steps), dims[position] // parts).reshape((-1,) + (1,) * (len(dims) - position - 1))

    loudness = one(*shards[0])
    for cut in shards[1:]:
        loudness = loudness * one(*cut)
    return loudness


def scatter_about(own_key, shape, scale, most, cuts=(), held_as=jnp.bfloat16):
    result = jax.random.normal(own_key, shape, jnp.float32) * scale
    if len(cuts) > 0:
        result = level_of(own_key, shape, cuts, -0.22, 0.18) * result
    return jnp.clip(result, min=-most, max=most).astype(held_as)


def setup_inputs(seed: int = 0) -> dict:
    splits = jax.random.split(jax.random.key(seed), 34)
    return {
        "features": scatter_about(splits[0], (CLIPS, LEN, CIN), 1.0, 6.0, ((0, 16), (1, 2))),
        "time_mask": draw_time_mask(jax.random.fold_in(splits[33], 71), 0),
        "negatives": draw_negatives(jax.random.fold_in(splits[33], 71), 0),
        "target_codes": place_ends(jax.random.randint(splits[3], (CLIPS, LEN, QGROUPS), 0, CODES), jax.random.fold_in(splits[3], 1), 0, CODES - 1).astype(jnp.int32),
        "feature_weight": scatter_about(splits[4], (CIN, D), CIN ** -0.5, 0.25, ((0, 16),), jnp.float32),
        "feature_first": draw_feature_first(jax.random.fold_in(splits[33], 71), 0),
        "feature_second": draw_feature_second(jax.random.fold_in(splits[33], 71), 0),
        "conv_weight": scatter_about(splits[7], (KW * (D // GROUPS), D), (KW * (D // GROUPS) // 4) ** -0.5, 0.15625, ((0, 16),), jnp.float32),
        "conv_first": draw_conv_first(jax.random.fold_in(splits[33], 71), 0),
        "conv_second": draw_conv_second(jax.random.fold_in(splits[33], 71), 0),
        "attention_weight": draw_attention_weight(jax.random.fold_in(splits[33], 71), 0),
        "attention_first": draw_attention_first(jax.random.fold_in(splits[33], 71), 0),
        "attention_second": draw_attention_second(jax.random.fold_in(splits[33], 71), 0),
        "left_basis_t": draw_left_basis_t(jax.random.fold_in(splits[33], 71), 0),
        "right_orthogonal_basis": draw_right_orthogonal_basis(jax.random.fold_in(splits[33], 71), 0),
        "expand_weight": scatter_about(splits[15], (LAYERS, D, FF), D ** -0.5, 0.21875, ((1, 16),), jnp.float32),
        "expand_first": draw_expand_first(jax.random.fold_in(splits[33], 71), 0),
        "expand_second": draw_expand_second(jax.random.fold_in(splits[33], 71), 0),
        "shrink_weight": scatter_about(splits[18], (LAYERS, FF, D), FF ** -0.5, 0.109375, ((1, 16),), jnp.float32),
        "shrink_first": draw_shrink_first(jax.random.fold_in(splits[33], 71), 0),
        "shrink_second": draw_shrink_second(jax.random.fold_in(splits[33], 71), 0),
        "final_weight": scatter_about(splits[21], (D, PROJ), D ** -0.5, 0.21875, ((0, 16),), jnp.float32),
        "final_first": draw_final_first(jax.random.fold_in(splits[33], 71), 0),
        "final_second": draw_final_second(jax.random.fold_in(splits[33], 71), 0),
        "target_weight": scatter_about(splits[24], (PROJ, PROJ), PROJ ** -0.5, 0.375, ((0, 16),), jnp.float32),
        "target_first": draw_target_first(jax.random.fold_in(splits[33], 71), 0),
        "target_second": draw_target_second(jax.random.fold_in(splits[33], 71), 0),
        "codebook_weight": scatter_about(splits[27], (PROJ, CODES), 1.0, 6.0, ((0, 16),), jnp.float32),
        "codebook_first": draw_codebook_first(jax.random.fold_in(splits[33], 71), 0),
        "codebook_second": draw_codebook_second(jax.random.fold_in(splits[33], 71), 0),
        "vector_params": draw_vector_params(jax.random.fold_in(splits[33], 71), 0),
        "vector_first": draw_vector_first(jax.random.fold_in(splits[33], 71), 0),
        "vector_second": draw_vector_second(jax.random.fold_in(splits[33], 71), 0),
    }


@jax.custom_vjp
def low(v):
    return lax.optimization_barrier(v.astype(jnp.bfloat16)).astype(jnp.float32)

@jax.custom_vjp
def low_back(v):
    return v

def low_keep(v):
    return (low(v), None)

def low_pass(kept, grad):
    return (grad,)

def back_keep(v):
    return (v, None)

def back_low(kept, grad):
    return (low(grad),)
low.defvjp(low_keep, low_pass)
low_back.defvjp(back_keep, back_low)
beta_one = 0.9
beta_two = 0.95
beta_rotated = 0.5
adam_epsilon = 1e-08
decay_rate = 0.01
rate_matrix = 0.02
rate_target = 0.08
rate_codebook = 0.6
rate_vector = 0.3
rate_rotated = 0.08
contrastive_sharpness = 0.1
norm_epsilon = 1e-05
unit_epsilon = 1e-06
maximum_score = lax.Precision.HIGHEST

def matmul(left_side, right_side):
    return jnp.dot(left_side, right_side, precision=maximum_score, preferred_element_type=jnp.float32)

def layer_norm(values, gain_row, bias_row):
    centred = values - lax.optimization_barrier(jnp.mean(values, -1, keepdims=True))
    spread = lax.optimization_barrier(jnp.mean(centred * centred, -1, keepdims=True))
    return centred * lax.rsqrt(spread + norm_epsilon) * gain_row + bias_row

def unit_rows(values):
    return values * lax.rsqrt(lax.optimization_barrier(jnp.sum(values * values, -1, keepdims=True)) + unit_epsilon)

def vector_pieces(vector):
    widths = [CIN, CIN, D, D, D, D, D] + [D, D, D, D, D, FF, D, D, D] * LAYERS + [PROJ, PROJ]
    pieces = []
    offset = 0
    for width in widths:
        pieces.append(vector[offset:offset + width])
        offset = offset + width
    return pieces

def grouped_conv(padded, kernel):
    window_index = jnp.arange(LEN)[:, None] + jnp.arange(KW)[None, :]
    window = padded[window_index].reshape(LEN, KW, GROUPS, D // GROUPS)
    shaped = kernel.reshape(KW, D // GROUPS, GROUPS, D // GROUPS)
    return jnp.einsum('tkgc,kcgo->tgo', window, shaped, precision=maximum_score).reshape(LEN, D)

def split_heads(rows):
    return rows.reshape(LEN, HEADS, HDIM).transpose(1, 0, 2)

def encoder_layer(hidden, attn_w, expand_w, shrink_w, pieces):
    q_bias, v_bias, o_bias, gain_one, bias_one, expand_bias, shrink_bias, gain_two, bias_two = pieces
    entry = low(hidden)
    query = low(low_back(matmul(entry, attn_w[0]) + q_bias))
    key_rows = low(low_back(matmul(entry, attn_w[1])))
    value_rows = low(low_back(matmul(entry, attn_w[2]) + v_bias))
    scores = jnp.einsum('hqd,hkd->hqk', split_heads(query), split_heads(key_rows), precision=maximum_score)
    scores = low_back(scores * HDIM ** (-0.5))
    probs = jax.nn.softmax(scores, axis=-1)
    mixed = jnp.einsum('hqk,hkd->hqd', low(probs), split_heads(value_rows), precision=maximum_score)
    mixed = low(low_back(mixed)).transpose(1, 0, 2).reshape(LEN, D)
    branch = low_back(matmul(mixed, attn_w[3]) + o_bias)
    middle = layer_norm(hidden + branch, gain_one, bias_one)
    inner = low_back(matmul(low(middle), expand_w) + expand_bias)
    outer = low_back(matmul(low(jax.nn.gelu(inner, approximate=False)), shrink_w) + shrink_bias)
    return layer_norm(middle + outer, gain_two, bias_two)

def clip_loss(params, feats, mask, distractor_draws, codes):
    feat_w, conv_w, attn_w, expand_w, shrink_w, final_w, target_w, code_w, vector = [low(item) for item in params]
    pieces = vector_pieces(vector)
    mask_on = (mask > 0)[:, None]
    normed = layer_norm(feats, pieces[0], pieces[1])
    projected = low_back(matmul(low(normed), feat_w) + pieces[2])
    masked = jnp.where(mask_on, pieces[3][None, :], projected)
    padded = jnp.pad(low(masked), ((KW // 2, KW // 2), (0, 0)))
    conv_out = low_back(grouped_conv(padded, conv_w) + pieces[4])
    hidden = layer_norm(masked + jax.nn.gelu(conv_out, approximate=False), pieces[5], pieces[6])
    for layer in range(LAYERS):
        hidden = encoder_layer(hidden, attn_w[4 * layer:4 * layer + 4], expand_w[layer], shrink_w[layer], pieces[7 + 9 * layer:16 + 9 * layer])
    context = unit_rows(low_back(matmul(low(hidden), final_w) + pieces[-2]))
    width = PROJ // QGROUPS
    chosen = []
    for group in range(QGROUPS):
        onehot = (codes[:, group][:, None] == jnp.arange(CODES)[None, :]).astype(jnp.float32)
        chosen.append(matmul(onehot, code_w[group * width:(group + 1) * width].T))
    targets = unit_rows(matmul(jnp.concatenate(chosen, 1), target_w) + pieces[-1])
    angular_agreement = low_back(matmul(low(context), low(targets).T))
    timestep_offsets = jnp.arange(LEN)
    true_target_agreement = angular_agreement[timestep_offsets, timestep_offsets] / contrastive_sharpness
    distractor_agreement = jnp.take_along_axis(angular_agreement, distractor_draws, axis=1) / contrastive_sharpness
    score_logits = jnp.concatenate([true_target_agreement[:, None], distractor_agreement], 1)
    largest = lax.optimization_barrier(jnp.max(score_logits, -1))
    total = largest + jnp.log(lax.optimization_barrier(jnp.sum(jnp.exp(score_logits - largest[:, None]), -1)))
    return jnp.sum(mask.astype(jnp.float32) * (total - true_target_agreement))

def adam_update(weight, grad, first, second, rate, decay):
    first = beta_one * first + (1 - beta_one) * grad
    second = beta_two * second + (1 - beta_two) * grad * grad
    share_fraction = first / (1 - beta_one ** STEP) / (jnp.sqrt(second / (1 - beta_two ** STEP)) + adam_epsilon)
    return (weight - rate * (share_fraction + decay * weight), first, second)

def rotate_one(inputs):
    weight, grad, first, second, left_t, right_side = inputs
    rotated_gradient = matmul(matmul(left_t, grad), right_side)
    first = beta_rotated * first + (1 - beta_rotated) * rotated_gradient
    second = beta_rotated * second + (1 - beta_rotated) * rotated_gradient * rotated_gradient
    share_fraction = first / (1 - beta_rotated ** STEP) / (jnp.sqrt(second / (1 - beta_rotated ** STEP)) + adam_epsilon)
    update = matmul(matmul(left_t.T, share_fraction), right_side.T)
    return (weight - rate_rotated * update, first, second)

def reference(features, time_mask, negatives, target_codes, feature_weight, feature_first, feature_second, conv_weight, conv_first, conv_second, attention_weight, attention_first, attention_second, left_basis_t, right_orthogonal_basis, expand_weight, expand_first, expand_second, shrink_weight, shrink_first, shrink_second, final_weight, final_first, final_second, target_weight, target_first, target_second, codebook_weight, codebook_first, codebook_second, vector_params, vector_first, vector_second):
    params = (feature_weight, conv_weight, attention_weight, expand_weight, shrink_weight, final_weight, target_weight, codebook_weight, vector_params)
    derivative_multiplier = 1.0 / (CLIPS * LEN)

    def one_clip(carry, inputs):
        grads, loss_sum, count = carry
        feats, mask, distractor_draws, codes = inputs
        value, pullback = jax.vjp(lambda items: clip_loss(items, feats.astype(jnp.float32), mask, distractor_draws, codes), params)
        clip_grads, = pullback(jnp.ones((), jnp.float32) * derivative_multiplier)
        grads = jax.tree.map(jnp.add, grads, clip_grads)
        return ((grads, loss_sum + value, count + jnp.sum(mask.astype(jnp.float32))), None)
    zeros = jax.tree.map(jnp.zeros_like, params)
    start = (zeros, jnp.zeros((), jnp.float32), jnp.zeros((), jnp.float32))
    (grads, loss_sum, count), _ = lax.scan(one_clip, start, (features, time_mask, negatives, target_codes))
    feature_new = adam_update(feature_weight, grads[0], feature_first, feature_second, rate_matrix, decay_rate)
    conv_new = adam_update(conv_weight, grads[1], conv_first, conv_second, rate_matrix, decay_rate)
    attention_new = lax.map(rotate_one, (attention_weight, grads[2], attention_first, attention_second, left_basis_t, right_orthogonal_basis))
    expand_new = adam_update(expand_weight, grads[3], expand_first, expand_second, rate_matrix, decay_rate)
    shrink_new = adam_update(shrink_weight, grads[4], shrink_first, shrink_second, rate_matrix, decay_rate)
    final_new = adam_update(final_weight, grads[5], final_first, final_second, rate_matrix, decay_rate)
    target_new = adam_update(target_weight, grads[6], target_first, target_second, rate_target, decay_rate)
    codebook_new = adam_update(codebook_weight, grads[7], codebook_first, codebook_second, rate_codebook, decay_rate)
    vector_new = adam_update(vector_params, grads[8], vector_first, vector_second, rate_vector, 0.0)
    return (jnp.stack([loss_sum, count]), feature_new[0], feature_new[1], feature_new[2], conv_new[0], conv_new[1], conv_new[2], attention_new[0], attention_new[1], attention_new[2], expand_new[0], expand_new[1], expand_new[2], shrink_new[0], shrink_new[1], shrink_new[2], final_new[0], final_new[1], final_new[2], target_new[0], target_new[1], target_new[2], codebook_new[0], codebook_new[1], codebook_new[2], vector_new[0], vector_new[1], vector_new[2])
```

```python
import functools

import jax
import jax.numpy as jnp
from jax import lax
from jax.experimental import pallas as pl
from jax.experimental.pallas import tpu as pltpu
from jax.sharding import PartitionSpec as P

D = 768
HEADS = 12
HDIM = 64
FF = 3072
CIN = 512
PROJ = 256
CODES = 320
QGROUPS = 2
LAYERS = 2
STEP = 10
SMALL_LANES = 1536


beta_one = 0.9
beta_two = 0.95
beta_rotated = 0.5
adam_epsilon = 1e-08
decay_rate = 0.01
rate_matrix = 0.02
rate_target = 0.08
rate_codebook = 0.6
rate_vector = 0.3
rate_rotated = 0.08
contrastive_sharpness = 0.1
norm_epsilon = 1e-05
unit_epsilon = 1e-06

KW = 128
GROUPS = 16
GC = D // GROUPS
LANE = 64
PACK = 4
PADW = GROUPS * LANE
HALF = KW // PACK
STEPS = HALF + 1
VMEM = 56 * 1024 * 1024
NT = (((1,), (1,)), ((), ()))
NN = (((1,), (0,)), ((), ()))


def mm(a, b, dims=NN):
    return lax.dot_general(a, b, dims, preferred_element_type=jnp.float32)


def spread_matrix(rows, out_cols, block, wide):
    i = lax.broadcasted_iota(jnp.int32, (rows, out_cols), 0)
    j = lax.broadcasted_iota(jnp.int32, (rows, out_cols), 1)
    return ((i // block) * wide + i % block == j).astype(jnp.bfloat16)


def pack_pair(x_ref, even_ref, odd_ref, rows):
    low = lax.broadcasted_iota(jnp.int32, (rows * 16, 128), 1) < LANE
    x = x_ref[...].reshape(rows, PACK, 16, 128)
    for half in range(2):
        first = x[:, 2 * half].reshape(rows * 16, 128).astype(jnp.float32)
        second = x[:, 2 * half + 1].reshape(rows * 16, 128).astype(jnp.float32)
        even_ref[:, half * 128:half * 128 + 128] = jnp.where(low, first, pltpu.roll(second, LANE, 1)).astype(jnp.bfloat16)
        odd_ref[:, half * 128:half * 128 + 128] = jnp.where(low, pltpu.roll(first, LANE, 1), second).astype(jnp.bfloat16)


def unpack_pair(even, odd, out_ref, rows):
    low = lax.broadcasted_iota(jnp.int32, (rows * 16, 128), 1) < LANE
    parts = []
    for half in range(2):
        e = even[:, half * 128:half * 128 + 128]
        o = odd[:, half * 128:half * 128 + 128]
        parts.append(jnp.where(low, e, pltpu.roll(o, LANE, 1)).reshape(rows, 1, 16, 128))
        parts.append(jnp.where(low, pltpu.roll(e, LANE, 1), o).reshape(rows, 1, 16, 128))
    out_ref[...] = jnp.concatenate(parts, axis=1).reshape(PACK * rows, 16, 128)


def widen_taps(w_ref, wide_ref, shards):
    per = KW // shards
    sel = spread_matrix(per * GC, per * LANE, GC, LANE)
    block = mm(w_ref[...].reshape(shards * 2 * GC, per * GC), sel).astype(jnp.bfloat16)
    for group in range(2):
        wide_ref[group, GC:, :] = jnp.zeros((LANE - GC, STEPS * 256), jnp.bfloat16)
        wide_ref[group, 0:GC, KW * LANE:] = jnp.zeros((GC, STEPS * 256 - KW * LANE), jnp.bfloat16)
        for s in range(shards):
            start = (2 * s + group) * GC
            wide_ref[group, 0:GC, s * per * LANE:(s + 1) * per * LANE] = block[start:start + GC]


def build_taps(wide_ref, taps_ref, group):
    wide = wide_ref[group]
    shifted = pltpu.roll(wide.astype(jnp.float32), LANE, 1).astype(jnp.bfloat16)
    total = STEPS * 256
    taps_ref[0:64, :] = wide
    taps_ref[64:128, :] = shifted
    taps_ref[128:192, 0:128] = jnp.zeros((64, 128), jnp.bfloat16)
    taps_ref[128:192, 128:total] = wide[:, 0:total - 128]
    taps_ref[192:256, 0:128] = jnp.zeros((64, 128), jnp.bfloat16)
    taps_ref[192:256, 128:total] = shifted[:, 0:total - 128]


def conv_forward_kernel(rows, shards, x_ref, w_ref, y_ref, even_ref, odd_ref, taps_ref, wide_ref):
    m = rows * 16
    pack_pair(x_ref, even_ref, odd_ref, rows + HALF)
    widen_taps(w_ref, wide_ref, shards)
    results = []
    for group, packed in enumerate((even_ref, odd_ref)):
        build_taps(wide_ref, taps_ref, group)
        left = jnp.concatenate([packed[q * 16:q * 16 + m, :] for q in range(STEPS)], axis=1)
        results.append(mm(left, taps_ref[...], NT))
    unpack_pair(results[0], results[1], y_ref, rows)


def conv_forward(x, w, rows, shards):
    frames = PACK * (rows + HALF)
    return pl.pallas_call(
        functools.partial(conv_forward_kernel, rows, shards),
        grid=(GROUPS // 2,),
        in_specs=[
            pl.BlockSpec((frames, 16, 128), lambda g: (0, 0, g)),
            pl.BlockSpec((shards, 2 * GC, w.shape[2]), lambda g: (0, g, 0)),
        ],
        out_specs=pl.BlockSpec((PACK * rows, 16, 128), lambda g: (0, 0, g)),
        out_shape=jax.ShapeDtypeStruct((PACK * rows, 16, PADW), jnp.float32),
        scratch_shapes=[pltpu.VMEM(((rows + HALF) * 16, 256), jnp.bfloat16)] * 2 + [
            pltpu.VMEM((256, STEPS * 256), jnp.bfloat16),
            pltpu.VMEM((2, LANE, STEPS * 256), jnp.bfloat16),
        ],
        compiler_params=pltpu.CompilerParams(vmem_limit_bytes=VMEM, dimension_semantics=("arbitrary",)),
        name="conv_forward",
    )(x, w)


def conv_backward_kernel(rows, shards, x_ref, d_ref, w_ref, dx_ref, dw_ref,
                         xe_ref, xo_ref, de_ref, do_ref, taps_ref, wide_ref, prod_ref, grad_ref):
    m = rows * 16
    per = KW // shards
    pack_pair(x_ref, xe_ref, xo_ref, rows + HALF)
    pack_pair(d_ref, de_ref, do_ref, rows + HALF)
    widen_taps(w_ref, wide_ref, shards)
    results = []
    for group, (x_packed, d_packed) in enumerate(((xe_ref, de_ref), (xo_ref, do_ref))):
        build_taps(wide_ref, taps_ref, group)
        d_turned = d_packed[HALF // 2 * 16:HALF // 2 * 16 + m, :].astype(jnp.float32).T.astype(jnp.bfloat16)
        acc = jnp.zeros((m, 256), jnp.float32)
        for q in range(STEPS):
            left = d_packed[(HALF - q) * 16:(HALF - q) * 16 + m, :]
            acc = acc + mm(left, taps_ref[:, q * 256:q * 256 + 256])
            prod_ref[:, q * 256:q * 256 + 256] = mm(d_turned, x_packed[q * 16:q * 16 + m, :])
        results.append(acc)
        width = KW * LANE
        straight = prod_ref[0:GC, 0:width] + prod_ref[128:128 + GC, 128:128 + width]
        turned = prod_ref[64:64 + GC, :] + pltpu.roll(prod_ref[192:192 + GC, :], STEPS * 256 - 128, 1)
        grad = straight + pltpu.roll(turned, STEPS * 256 - 64, 1)[:, 0:width]
        grad = grad.astype(jnp.bfloat16)
        for s in range(shards):
            start = (2 * s + group) * GC
            grad_ref[start:start + GC, :] = grad[:, s * per * LANE:(s + 1) * per * LANE]
    sel = spread_matrix(per * GC, per * LANE, GC, LANE)
    dw_ref[...] = mm(grad_ref[...], sel, NT).astype(jnp.bfloat16).reshape(shards, 2 * GC, per * GC)
    unpack_pair(results[0], results[1], dx_ref, rows)


def conv_backward(x, d, w, rows, shards):
    frames = PACK * (rows + HALF)
    return pl.pallas_call(
        functools.partial(conv_backward_kernel, rows, shards),
        grid=(GROUPS // 2,),
        in_specs=[
            pl.BlockSpec((frames, 16, 128), lambda g: (0, 0, g)),
            pl.BlockSpec((frames, 16, 128), lambda g: (0, 0, g)),
            pl.BlockSpec((shards, 2 * GC, w.shape[2]), lambda g: (0, g, 0)),
        ],
        out_specs=[
            pl.BlockSpec((PACK * rows, 16, 128), lambda g: (0, 0, g)),
            pl.BlockSpec((shards, 2 * GC, w.shape[2]), lambda g: (0, g, 0)),
        ],
        out_shape=[
            jax.ShapeDtypeStruct((PACK * rows, 16, PADW), jnp.float32),
            jax.ShapeDtypeStruct(w.shape, jnp.bfloat16),
        ],
        scratch_shapes=[pltpu.VMEM(((rows + HALF) * 16, 256), jnp.bfloat16)] * 4 + [
            pltpu.VMEM((256, STEPS * 256), jnp.bfloat16),
            pltpu.VMEM((2, LANE, STEPS * 256), jnp.bfloat16),
            pltpu.VMEM((256, STEPS * 256), jnp.float32),
            pltpu.VMEM((shards * 2 * GC, KW // shards * LANE), jnp.bfloat16),
        ],
        compiler_params=pltpu.CompilerParams(vmem_limit_bytes=VMEM, dimension_semantics=("arbitrary",)),
        name="conv_backward",
    )(x, d, w)


def to_strips(padded, frame_count):
    clips = padded.shape[0]
    strips = 16 // clips
    length = frame_count // strips
    sel = spread_matrix(D, PADW, GC, LANE)
    wide = mm(padded.reshape(-1, D), sel).astype(jnp.bfloat16).reshape(clips, -1, PADW)
    parts = jnp.stack([wide[:, s * length:s * length + length + KW] for s in range(strips)], 1)
    return parts.reshape(16, length + KW, PADW).transpose(1, 0, 2)


def from_strips(y, clips):
    rows = y.transpose(1, 0, 2).reshape(-1, PADW)
    high = lax.reduce_precision(rows, 8, 7)
    rest = (rows - high).astype(jnp.bfloat16)
    high = high.astype(jnp.bfloat16)
    sel = spread_matrix(D, PADW, GC, LANE)
    return mm(high, sel, NT) + mm(rest, sel, NT)


SCALE = HDIM ** (-0.5)


def turned(block):
    return block.astype(jnp.float32).T.astype(jnp.bfloat16)


def attend_kernel(blocks, q_ref, *refs):
    keys = [refs[2 * j] for j in range(blocks)]
    values = [refs[2 * j + 1] for j in range(blocks)]
    mixed_ref, stat_ref = refs[2 * blocks:]
    frames = q_ref.shape[0]
    low = lax.broadcasted_iota(jnp.int32, (frames, 128), 1) < HDIM
    scaled = q_ref[...] * jnp.bfloat16(SCALE)
    none = jnp.zeros_like(scaled)
    turned_keys = [turned(k[...]) for k in keys]
    parts = []
    stats = []
    for head in range(2):
        query = jnp.where(low, scaled, none) if head == 0 else jnp.where(low, none, scaled)
        scores = [mm(query, k) for k in turned_keys]
        largest = functools.reduce(jnp.maximum, [jnp.max(s, 1, keepdims=True) for s in scores])
        powers = [jnp.exp(s - largest) for s in scores]
        total = functools.reduce(jnp.add, [jnp.sum(p, 1, keepdims=True) for p in powers])
        out = functools.reduce(jnp.add, [mm(p.astype(jnp.bfloat16), v[...]) for p, v in zip(powers, values)])
        parts.append(out * (1.0 / total))
        stats.append(jnp.broadcast_to(largest + jnp.log(total), (frames, 128)))
    mixed_ref[...] = jnp.where(low, parts[0], parts[1]).astype(jnp.bfloat16)
    rows = jnp.where(low, stats[0], stats[1]).T
    stat_ref[0, 0, 0:1, :] = rows[0:1, :]
    stat_ref[0, 0, 1:2, :] = rows[HDIM:HDIM + 1, :]


def attend(query, keys, values, clips):
    blocks = len(keys)
    rows = query.shape[0]
    frames = rows // clips
    spec = pl.BlockSpec((frames, 128), lambda c, h: (c, h))
    operands = [query]
    for k, v in zip(keys, values):
        operands += [k, v]
    return pl.pallas_call(
        functools.partial(attend_kernel, blocks),
        grid=(clips, HEADS // 2),
        in_specs=[spec] * len(operands),
        out_specs=[spec, pl.BlockSpec((1, 1, 2, frames), lambda c, h: (c, h, 0, 0))],
        out_shape=[
            jax.ShapeDtypeStruct((rows, D), jnp.bfloat16),
            jax.ShapeDtypeStruct((clips, HEADS // 2, 2, frames), jnp.float32),
        ],
        compiler_params=pltpu.CompilerParams(vmem_limit_bytes=VMEM, dimension_semantics=("arbitrary", "arbitrary")),
        name="attend",
    )(*operands)


def attend_back_kernel(blocks, q_ref, d_ref, stat_ref, *refs):
    keys = [refs[2 * j] for j in range(blocks)]
    values = [refs[2 * j + 1] for j in range(blocks)]
    dq_ref = refs[2 * blocks]
    dk = [refs[2 * blocks + 1 + 2 * j] for j in range(blocks)]
    dv = [refs[2 * blocks + 2 + 2 * j] for j in range(blocks)]
    frames = q_ref.shape[0]
    low = lax.broadcasted_iota(jnp.int32, (frames, 128), 1) < HDIM
    scaled = q_ref[...] * jnp.bfloat16(SCALE)
    grad = d_ref[...]
    none = jnp.zeros_like(scaled)
    q_turned = turned(scaled)
    d_turned = turned(grad)
    gap = jnp.zeros((HDIM, frames), jnp.bfloat16)
    k_turned = [turned(k[...]) for k in keys]
    dq_rows = []
    dk_sum = [None] * blocks
    dv_sum = [None] * blocks
    for head in range(2):
        pick = slice(head * HDIM, head * HDIM + HDIM)
        if head == 0:
            query, grad_head = jnp.where(low, scaled, none), jnp.where(low, grad, none)
            q_side = jnp.concatenate([q_turned[pick], gap], 0)
            d_side = jnp.concatenate([d_turned[pick], gap], 0)
        else:
            query, grad_head = jnp.where(low, none, scaled), jnp.where(low, none, grad)
            q_side = jnp.concatenate([gap, q_turned[pick]], 0)
            d_side = jnp.concatenate([gap, d_turned[pick]], 0)
        stat = stat_ref[0, 0, head:head + 1, :]
        probs = [jnp.exp(mm(k[...], q_side) - stat) for k in keys]
        weighted = [p * mm(v[...], d_side) for p, v in zip(probs, values)]
        delta = functools.reduce(jnp.add, [jnp.sum(w, 0, keepdims=True) for w in weighted])
        dq = None
        for j in range(blocks):
            ds = (weighted[j] - probs[j] * delta).astype(jnp.bfloat16)
            grad_v = mm(probs[j].astype(jnp.bfloat16), grad_head)
            grad_k = mm(ds, query)
            part = mm(k_turned[j][pick], ds)
            dq = part if dq is None else dq + part
            dv_sum[j] = grad_v if dv_sum[j] is None else dv_sum[j] + grad_v
            dk_sum[j] = grad_k if dk_sum[j] is None else dk_sum[j] + grad_k
        dq_rows.append(dq)
    dq_ref[...] = (jnp.concatenate(dq_rows, 0) * SCALE).T.astype(jnp.bfloat16)
    for j in range(blocks):
        dk[j][...] = dk_sum[j].astype(jnp.bfloat16)
        dv[j][...] = dv_sum[j].astype(jnp.bfloat16)


def attend_back(query, grad, stat, keys, values, clips):
    blocks = len(keys)
    rows = query.shape[0]
    frames = rows // clips
    spec = pl.BlockSpec((frames, 128), lambda c, h: (c, h))
    operands = []
    for k, v in zip(keys, values):
        operands += [k, v]
    shape = jax.ShapeDtypeStruct((rows, D), jnp.bfloat16)
    return pl.pallas_call(
        functools.partial(attend_back_kernel, blocks),
        grid=(clips, HEADS // 2),
        in_specs=[spec, spec, pl.BlockSpec((1, 1, 2, frames), lambda c, h: (c, h, 0, 0))] + [spec] * len(operands),
        out_specs=[spec] * (1 + 2 * blocks),
        out_shape=[shape] * (1 + 2 * blocks),
        compiler_params=pltpu.CompilerParams(vmem_limit_bytes=VMEM, dimension_semantics=("arbitrary", "arbitrary")),
        name="attend_back",
    )(query, grad, stat, *operands)


def count_kernel(draws, n_ref, out_ref):
    length, frames = out_ref.shape[1:]
    place = lax.broadcasted_iota(jnp.int32, (length // 8, 8, frames), 0) * 8 + lax.broadcasted_iota(
        jnp.int32, (length // 8, 8, frames), 1)
    total = jnp.zeros((length // 8, 8, frames), jnp.float32)
    for n in range(draws):
        row = n_ref[0, n:n + 1, :]
        total = total + jnp.where(place == row[None], 1.0, 0.0)
    out_ref[0] = total.reshape(length, frames).astype(jnp.bfloat16)


def count_draws(negatives, length):
    clips, draws, frames = negatives.shape
    tile = 128 if frames % 128 == 0 else frames
    return pl.pallas_call(
        functools.partial(count_kernel, draws),
        grid=(clips, frames // tile),
        in_specs=[pl.BlockSpec((1, draws, tile), lambda c, f: (c, 0, f))],
        out_specs=pl.BlockSpec((1, length, tile), lambda c, f: (c, 0, f)),
        out_shape=jax.ShapeDtypeStruct((clips, length, frames), jnp.bfloat16),
        compiler_params=pltpu.CompilerParams(vmem_limit_bytes=VMEM, dimension_semantics=("arbitrary", "arbitrary")),
        name="count_draws",
    )(negatives)


def swap_moves(count, step):
    return [(i, (i - step) % count) for i in range(count)]


def gather_ring(block):
    count = lax.axis_size("seq")
    return [block] + [lax.ppermute(block, "seq", swap_moves(count, step)) for step in range(1, count)]


def return_ring(blocks):
    count = lax.axis_size("seq")
    return [lax.ppermute(block, "seq", swap_moves(count, -step)) for step, block in enumerate(blocks) if step > 0]


def seq_sum(values):
    if lax.axis_size("seq") > 2:
        return lax.psum(values, "seq").astype(jnp.float32)
    other = lax.ppermute(values, "seq", [(0, 1), (1, 0)])
    return values.astype(jnp.float32) + other.astype(jnp.float32)


def lowered(values):
    return values.astype(jnp.bfloat16)


def bdot(left_side, right_side):
    return jnp.dot(left_side, right_side, preferred_element_type=jnp.float32)


def turned_dot(left_side, right_side):
    return lax.dot_general(left_side, right_side, NT, preferred_element_type=jnp.float32)


def rows_dot(left_side, right_side):
    return lax.dot_general(left_side, right_side, (((0,), (0,)), ((), ())), preferred_element_type=jnp.float32)


def fdot(left_side, right_side):
    return jnp.dot(left_side, right_side, precision=lax.Precision.HIGHEST, preferred_element_type=jnp.float32)


def column_sum(values):
    return jnp.sum(values.astype(jnp.float32), 0)


def gelu_parts(values):
    half = 0.5 * (1.0 + lax.erf(values * 0.5**0.5))
    density = jnp.exp(-0.5 * values * values) * (2.0 * jnp.pi) ** -0.5
    return values * half, half + values * density


def layer_norm(values, gain_row, bias_row):
    centred = values - jnp.mean(values, -1, keepdims=True)
    spread = jnp.mean(centred * centred, -1, keepdims=True)
    return centred * lax.rsqrt(spread + norm_epsilon) * gain_row + bias_row


def unit_rows(values):
    return values * lax.rsqrt(jnp.sum(values * values, -1, keepdims=True) + unit_epsilon)


def vector_pieces(vector):
    widths = [CIN, CIN, D, D, D, D, D] + [D, D, D, D, D, FF, D, D, D] * LAYERS + [PROJ, PROJ]
    pieces = []
    offset = 0
    for width in widths:
        pieces.append(vector[offset : offset + width])
        offset = offset + width
    return pieces


def with_halo(block, width):
    count = lax.axis_size("seq")
    forward = [(i, i + 1) for i in range(count - 1)]
    backward = [(i + 1, i) for i in range(count - 1)]
    low = lax.ppermute(block[:, block.shape[1] - width :], "seq", forward)
    high = lax.ppermute(block[:, :width], "seq", backward)
    return jnp.concatenate([low, block, high], axis=1)


def layer_forward(hidden, attn_w, expand_w, shrink_w, pieces, clip_count):
    q_bias, v_bias, o_bias, gain_one, bias_one, expand_bias, shrink_bias, gain_two, bias_two = pieces
    entries = gather_ring(lowered(hidden))
    query = lowered(bdot(entries[0], attn_w[:, :D]) + q_bias)
    keys = [lowered(bdot(entry, attn_w[:, D : 2 * D])) for entry in entries]
    values = [lowered(bdot(entry, attn_w[:, 2 * D : 3 * D]) + v_bias) for entry in entries]
    mixed, stat = attend(query, keys, values, clip_count)
    branch = bdot(mixed, attn_w[:, 3 * D :]) + o_bias
    middle, middle_pull = jax.vjp(layer_norm, hidden + branch, gain_one, bias_one)
    middle_low = lowered(middle)
    inner = bdot(middle_low, expand_w) + expand_bias
    activated, slope = gelu_parts(inner)
    active_low = lowered(activated)
    slope_low = lowered(slope)
    outer = bdot(active_low, shrink_w) + shrink_bias
    result, final_pull = jax.vjp(layer_norm, middle + outer, gain_two, bias_two)
    cache = (entries, query, keys, values, mixed, stat, middle_pull, middle_low, slope_low, active_low, final_pull)
    return result, cache


def feed_backward(grad_out, cache, expand_w, shrink_w):
    middle_low, slope_low, active_low, final_pull = cache[7:]
    grad_sum, grad_gain, grad_bias = final_pull(grad_out)
    grad_outer = lowered(grad_sum)
    grad_shrink = lowered(rows_dot(active_low, grad_outer))
    grad_inner = lowered(slope_low.astype(jnp.float32) * turned_dot(grad_outer, shrink_w))
    grad_expand = lowered(rows_dot(middle_low, grad_inner))
    grad_middle = grad_sum + turned_dot(grad_inner, expand_w)
    vectors = [column_sum(grad_inner), column_sum(grad_outer), grad_gain, grad_bias]
    return grad_middle, grad_expand, grad_shrink, vectors


def attend_backward(grad_middle, cache, attn_w, clip_count):
    entries, query, keys, values, mixed, stat, middle_pull = cache[:7]
    grad_sum, grad_gain, grad_bias = middle_pull(grad_middle)
    grad_branch = lowered(grad_sum)
    grad_out_proj = lowered(rows_dot(mixed, grad_branch))
    grad_mixed = lowered(turned_dot(grad_branch, attn_w[:, 3 * D :]))
    results = attend_back(query, grad_mixed, stat, keys, values, clip_count)
    grad_query, grad_keys, grad_values = results[0], results[1::2], results[2::2]
    back = [
        turned_dot(dk, attn_w[:, D : 2 * D]) + turned_dot(dv, attn_w[:, 2 * D : 3 * D])
        for dk, dv in zip(grad_keys, grad_values)
    ]
    arrived = return_ring([lowered(block) for block in back])
    grad_hidden = grad_sum + turned_dot(grad_query, attn_w[:, :D]) + back[0]
    for block in arrived:
        grad_hidden = grad_hidden + block.astype(jnp.float32)
    grads = [
        lowered(rows_dot(entries[0], grad_query)),
        lowered(sum(rows_dot(entry, dk) for entry, dk in zip(entries, grad_keys))),
        lowered(sum(rows_dot(entry, dv) for entry, dv in zip(entries, grad_values))),
        grad_out_proj,
    ]
    vectors = [
        column_sum(grad_query),
        sum(column_sum(dv) for dv in grad_values),
        column_sum(grad_branch),
        grad_gain,
        grad_bias,
    ]
    return grad_hidden, grads, vectors


def adam_update(weight, grad, first, second, rate, decay):
    first = beta_one * first + (1 - beta_one) * grad
    second = beta_two * second + (1 - beta_two) * grad * grad
    share_fraction = (
        first / (1 - beta_one**STEP) / (jnp.sqrt(second / (1 - beta_two**STEP)) + adam_epsilon)
    )
    return (weight - rate * (share_fraction + decay * weight), first, second)


def gather_rows(block):
    return lax.all_gather(block, "shard", axis=0, tiled=True)


def scatter_chunks(chunks):
    return lax.psum_scatter(chunks, "shard", scatter_dimension=0, tiled=False)


def trade(chunks):
    return lax.all_to_all(chunks, "shard", split_axis=0, concat_axis=0, tiled=True)


def on_device(
    features,
    time_mask,
    negatives,
    target_codes,
    feature_weight,
    feature_first,
    feature_second,
    conv_weight,
    conv_first,
    conv_second,
    attention_weight,
    attention_first,
    attention_second,
    left_basis_t,
    right_orthogonal_basis,
    expand_weight,
    expand_first,
    expand_second,
    shrink_weight,
    shrink_first,
    shrink_second,
    final_weight,
    final_first,
    final_second,
    target_weight,
    target_first,
    target_second,
    codebook_weight,
    codebook_first,
    codebook_second,
    vector_params,
    vector_first,
    vector_second,
):
    clip_count, frame_count = (features.shape[0], features.shape[1])
    row_count = clip_count * frame_count
    seq_count = lax.axis_size("seq")
    shards = lax.axis_size("shard")
    clip_frames = frame_count * seq_count
    small_items = [feature_weight, final_weight, target_weight, codebook_weight, vector_params]
    small_sizes = [item.size for item in small_items]
    small_total = sum(small_sizes)
    small_width = -(-(small_total + 2) // SMALL_LANES) * SMALL_LANES

    def split_small(flat):
        parts = []
        offset = 0
        for item, size in zip(small_items, small_sizes):
            parts.append(flat[:, offset : offset + size].reshape((-1,) + item.shape[1:]))
            offset = offset + size
        return parts

    small = jnp.concatenate([lowered(item).reshape(-1) for item in small_items])
    small = jnp.pad(small, (0, small_width - small_total))
    small_all = lax.all_gather(small, "shard", axis=0, tiled=False)
    feat_w, final_w, target_w, code_w, vector_low = split_small(small_all)
    conv_w = lax.all_gather(lowered(conv_weight).T, "shard", axis=0, tiled=False)
    attn_w, expand_w, shrink_w = [], [], []
    for layer in range(LAYERS):
        own = lowered(attention_weight[4 * layer : 4 * layer + 4]).transpose(1, 0, 2).reshape(-1, 4 * D)
        attn_w.append(gather_rows(own))
        expand_w.append(gather_rows(lowered(expand_weight[layer])))
        shrink_w.append(gather_rows(lowered(shrink_weight[layer])))
    parts = shards // (4 * LAYERS)
    left_low = trade(jnp.repeat(lowered(left_basis_t), parts, axis=0)).reshape(D, D)

    pieces = vector_pieces(vector_low.astype(jnp.float32))
    mask_on = (time_mask > 0).reshape(row_count, 1)
    feats = features.reshape(row_count, CIN).astype(jnp.float32)
    normed, norm_pull = jax.vjp(layer_norm, feats, pieces[0], pieces[1])
    normed_low = lowered(normed)
    projected = bdot(normed_low, feat_w) + pieces[2]
    masked = jnp.where(mask_on, pieces[3][None, :], projected)
    padded = with_halo(lowered(masked).reshape(clip_count, frame_count, D), KW // 2)
    strip_rows = frame_count * clip_count // 16 // PACK
    strips = to_strips(padded, frame_count)
    conv_out = from_strips(conv_forward(strips, conv_w, strip_rows, shards), clip_count) + pieces[4]
    conv_active, conv_slope = gelu_parts(conv_out)
    hidden, front_pull = jax.vjp(layer_norm, masked + conv_active, pieces[5], pieces[6])

    caches = []
    for layer in range(LAYERS):
        hidden, cache = layer_forward(
            hidden, attn_w[layer], expand_w[layer], shrink_w[layer], pieces[7 + 9 * layer : 16 + 9 * layer], clip_count
        )
        caches.append(cache)
    top_low = lowered(hidden)
    context, context_pull = jax.vjp(unit_rows, bdot(top_low, final_w) + pieces[-2])
    context_low = lowered(context).reshape(clip_count, frame_count, PROJ)

    first_frame = lax.axis_index("seq") * frame_count
    ring_draws = (negatives - first_frame + clip_frames) % clip_frames
    counts = count_draws(ring_draws.transpose(0, 2, 1), clip_frames).astype(jnp.float32)
    codes = jnp.concatenate(gather_ring(target_codes), 1).reshape(clip_count * clip_frames, QGROUPS)
    width = PROJ // QGROUPS
    code_f = code_w.astype(jnp.float32)
    target_f = target_w.astype(jnp.float32)
    table = jnp.concatenate(
        [fdot(code_f[g * width : (g + 1) * width].T, target_f[g * width : (g + 1) * width]) for g in range(QGROUPS)]
    )
    choice = jnp.concatenate(
        [(codes[:, g : g + 1] == jnp.arange(CODES)[None, :]).astype(jnp.float32) for g in range(QGROUPS)], 1
    )
    targets, target_pull = jax.vjp(unit_rows, fdot(choice, table) + pieces[-1])
    targets_low = lowered(targets).reshape(clip_count, clip_frames, PROJ)
    similar = jnp.einsum("clp,cfp->clf", targets_low, context_low, preferred_element_type=jnp.float32)
    logits = similar / contrastive_sharpness
    place = jnp.arange(clip_frames)[:, None] == jnp.arange(frame_count)[None, :]
    own = place.astype(jnp.float32)[None]
    weight = counts + own
    largest = jnp.max(jnp.where(weight > 0, logits, -jnp.inf), 1, keepdims=True)
    power = weight * jnp.exp(jnp.where(weight > 0, logits - largest, 0.0))
    running_totals = jnp.sum(power, 1, keepdims=True)
    mask_as_floats = time_mask.astype(jnp.float32)
    own_logit = jnp.sum(own * logits, 1)
    row_loss = largest[:, 0] + jnp.log(running_totals[:, 0]) - own_logit
    loss_sum = jnp.sum(mask_as_floats * row_loss)
    mask_count = jnp.sum(mask_as_floats)
    derivative_multiplier = 1.0 / (clip_count * shards * clip_frames)
    grad_similar = lowered(
        mask_as_floats[:, None, :]
        * (power / running_totals - own)
        * (derivative_multiplier / contrastive_sharpness)
    )
    grad_context = jnp.einsum("clf,clp->cfp", grad_similar, targets_low, preferred_element_type=jnp.float32)
    grad_targets = jnp.einsum("clf,cfp->clp", grad_similar, context_low, preferred_element_type=jnp.float32)
    (grad_raw,) = target_pull(grad_targets.reshape(-1, PROJ))
    grad_table = fdot(choice.T, grad_raw)
    tables = [grad_table[g * CODES : (g + 1) * CODES] for g in range(QGROUPS)]
    grad_target_w = jnp.concatenate([fdot(code_f[g * width : (g + 1) * width], tables[g]) for g in range(QGROUPS)])
    grad_codebook = jnp.concatenate(
        [fdot(target_f[g * width : (g + 1) * width], tables[g].T) for g in range(QGROUPS)]
    )
    grad_target_bias = column_sum(grad_raw)
    (grad_context_raw,) = context_pull(grad_context.reshape(row_count, PROJ))
    grad_context_low = lowered(grad_context_raw)
    grad_final_w = rows_dot(top_low, grad_context_low)
    grad_final_bias = column_sum(grad_context_low)
    grad_hidden = turned_dot(grad_context_low, final_w)

    attn_grads = [None] * LAYERS
    feed_sums = [None] * LAYERS
    layer_pieces = [None] * LAYERS
    for layer in reversed(range(LAYERS)):
        grad_middle, grad_expand, grad_shrink, feed_vectors = feed_backward(
            grad_hidden, caches[layer], expand_w[layer], shrink_w[layer]
        )
        chunks = jnp.concatenate(
            [grad_expand[:, j * D : (j + 1) * D].reshape(shards, -1, D) for j in range(FF // D)]
            + [grad_shrink.reshape(shards, -1, D)],
            1,
        )
        feed_sums[layer] = seq_sum(scatter_chunks(chunks))
        grad_hidden, attn_grads[layer], attn_vectors = attend_backward(
            grad_middle, caches[layer], attn_w[layer], clip_count
        )
        layer_pieces[layer] = attn_vectors + feed_vectors
    attn_chunks = jnp.stack(attn_grads[0] + attn_grads[1]).reshape(4 * LAYERS, D, parts, D // parts)
    attn_chunks = attn_chunks.transpose(0, 2, 1, 3).reshape(shards, D, D // parts)
    attn_sum = seq_sum(scatter_chunks(attn_chunks))

    grad_sum, grad_gain_enc, grad_bias_enc = front_pull(grad_hidden)
    grad_conv_low = lowered(grad_sum * conv_slope)
    grad_strips = to_strips(with_halo(grad_conv_low.reshape(clip_count, frame_count, D), KW // 2), frame_count)
    grad_back, conv_chunks = conv_backward(strips, grad_strips, conv_w, strip_rows, shards)
    grad_masked = grad_sum + from_strips(grad_back, clip_count)
    grad_embedding = jnp.sum(jnp.where(mask_on, grad_masked, 0.0), 0)
    grad_projected = lowered(jnp.where(mask_on, 0.0, grad_masked))
    grad_feat_w = rows_dot(normed_low, grad_projected)
    _, grad_gain_feat, grad_bias_feat = norm_pull(turned_dot(grad_projected, feat_w))
    vector_grads = [
        grad_gain_feat,
        grad_bias_feat,
        column_sum(grad_projected),
        grad_embedding,
        column_sum(grad_conv_low),
        grad_gain_enc,
        grad_bias_enc,
    ]
    for layer in range(LAYERS):
        vector_grads = vector_grads + layer_pieces[layer]
    vector_grads = jnp.concatenate(vector_grads + [grad_final_bias, grad_target_bias])
    small_grads = [
        lowered(item).reshape(shards, -1)
        for item in (grad_feat_w, grad_final_w, grad_target_w, grad_codebook, vector_grads)
    ]
    loss_tile = jnp.broadcast_to(lowered(jnp.stack([loss_sum, mask_count]))[None], (shards, 2))
    gap = jnp.zeros((shards, small_width - small_total - 2), jnp.bfloat16)
    small_chunks = jnp.concatenate(small_grads + [loss_tile, gap], 1)
    taps = conv_chunks.shape[2]
    last_chunks = jnp.concatenate([conv_chunks, small_chunks.reshape(shards, -1, taps)], 1)
    last_sum = seq_sum(scatter_chunks(last_chunks))
    sum_conv = last_sum[:D].T
    small_sum = last_sum[D:].reshape(1, -1)
    sum_loss = small_sum[0, small_total : small_total + 2]
    sum_feat, sum_final, sum_target, sum_code, sum_vector = split_small(small_sum)

    rows = D // shards
    columns = D // parts

    def to_rows(block):
        shaped = trade(lowered(block).reshape(shards, rows, columns)).reshape(4 * LAYERS, parts, rows, columns)
        return shaped.transpose(0, 2, 1, 3).reshape(4 * LAYERS, rows, D)

    def to_columns(block):
        shaped = lowered(block).reshape(4 * LAYERS, rows, parts, columns).transpose(0, 2, 1, 3)
        return trade(shaped.reshape(shards, rows, columns)).reshape(D, columns)

    right_low = lowered(right_orthogonal_basis)
    left_grad = to_rows(bdot(left_low, lowered(attn_sum)))
    rotated = jnp.einsum("mrd,mde->mre", left_grad, right_low, preferred_element_type=jnp.float32)
    rot_first = beta_rotated * attention_first + (1 - beta_rotated) * rotated
    rot_second = beta_rotated * attention_second + (1 - beta_rotated) * rotated * rotated
    share_fraction = (
        rot_first
        / (1 - beta_rotated**STEP)
        / (jnp.sqrt(rot_second / (1 - beta_rotated**STEP)) + adam_epsilon)
    )
    half_back = jnp.einsum("mre,mde->mrd", lowered(share_fraction), right_low, preferred_element_type=jnp.float32)
    update = to_rows(rows_dot(left_low, to_columns(half_back)))
    new_attention = attention_weight - rate_rotated * update.astype(jnp.float32)

    sum_expand = jnp.stack(
        [s[: -shrink_weight.shape[1]].reshape(FF // D, -1, D).transpose(1, 0, 2).reshape(-1, FF) for s in feed_sums]
    )
    sum_shrink = jnp.stack([s[-shrink_weight.shape[1] :] for s in feed_sums])
    feature_new = adam_update(feature_weight, sum_feat, feature_first, feature_second, rate_matrix, decay_rate)
    conv_new = adam_update(conv_weight, sum_conv, conv_first, conv_second, rate_matrix, decay_rate)
    expand_new = adam_update(expand_weight, sum_expand, expand_first, expand_second, rate_matrix, decay_rate)
    shrink_new = adam_update(shrink_weight, sum_shrink, shrink_first, shrink_second, rate_matrix, decay_rate)
    final_new = adam_update(final_weight, sum_final, final_first, final_second, rate_matrix, decay_rate)
    target_new = adam_update(target_weight, sum_target, target_first, target_second, rate_target, decay_rate)
    codebook_new = adam_update(codebook_weight, sum_code, codebook_first, codebook_second, rate_codebook, decay_rate)
    vector_new = adam_update(vector_params, sum_vector, vector_first, vector_second, rate_vector, 0.0)
    return (
        (sum_loss,)
        + feature_new
        + conv_new
        + (new_attention, rot_first, rot_second)
        + expand_new
        + shrink_new
        + final_new
        + target_new
        + codebook_new
        + vector_new
    )


def solution(mesh):
    return jax.shard_map(
        on_device,
        mesh=mesh,
        in_specs=(
            P("shard", "seq", None),
            P("shard", "seq"),
            P("shard", "seq", None),
            P("shard", "seq", None),
            P("shard", None),
            P("shard", None),
            P("shard", None),
            P("shard", None),
            P("shard", None),
            P("shard", None),
            P(None, "shard", None),
            P(None, "shard", None),
            P(None, "shard", None),
            P(None, "shard", None),
            P(),
            P(None, "shard", None),
            P(None, "shard", None),
            P(None, "shard", None),
            P(None, "shard", None),
            P(None, "shard", None),
            P(None, "shard", None),
            P("shard", None),
            P("shard", None),
            P("shard", None),
            P("shard", None),
            P("shard", None),
            P("shard", None),
            P("shard", None),
            P("shard", None),
            P("shard", None),
            P("shard"),
            P("shard"),
            P("shard"),
        ),
        out_specs=(
            P(),
            P("shard", None),
            P("shard", None),
            P("shard", None),
            P("shard", None),
            P("shard", None),
            P("shard", None),
            P(None, "shard", None),
            P(None, "shard", None),
            P(None, "shard", None),
            P(None, "shard", None),
            P(None, "shard", None),
            P(None, "shard", None),
            P(None, "shard", None),
            P(None, "shard", None),
            P(None, "shard", None),
            P("shard", None),
            P("shard", None),
            P("shard", None),
            P("shard", None),
            P("shard", None),
            P("shard", None),
            P("shard", None),
            P("shard", None),
            P("shard", None),
            P("shard"),
            P("shard"),
            P("shard"),
        ),
        check_vma=False,
    )
```

```python
import functools

import jax
import jax.numpy as jnp
from jax import lax
from jax.experimental import pallas as pl
from jax.experimental.pallas import tpu as pltpu
from jax.sharding import PartitionSpec as P

D = 768
HEADS = 12
HDIM = 64
FF = 3072
CIN = 512
PROJ = 256
CODES = 320
QGROUPS = 2
LAYERS = 2
STEP = 10
SMALL_LANES = 6144


beta_one = 0.9
beta_two = 0.95
beta_rotated = 0.5
adam_epsilon = 1e-08
decay_rate = 0.01
rate_matrix = 0.02
rate_target = 0.08
rate_codebook = 0.6
rate_vector = 0.3
rate_rotated = 0.08
contrastive_sharpness = 0.1
norm_epsilon = 1e-05
unit_epsilon = 1e-06

KW = 128
GROUPS = 16
GC = D // GROUPS
LANE = 64
PACK = 4
PADW = GROUPS * LANE
HALF = KW // PACK
STEPS = HALF + 1
VMEM = 56 * 1024 * 1024
SMALL_COST = pl.CostEstimate(flops=1024, bytes_accessed=1024, transcendentals=0)
NT = (((1,), (1,)), ((), ()))
NN = (((1,), (0,)), ((), ()))


def mm(a, b, dims=NN):
    return lax.dot_general(a, b, dims, preferred_element_type=jnp.float32)


def spread_matrix(rows, out_cols, block, wide):
    i = lax.broadcasted_iota(jnp.int32, (rows, out_cols), 0)
    j = lax.broadcasted_iota(jnp.int32, (rows, out_cols), 1)
    return ((i // block) * wide + i % block == j).astype(jnp.bfloat16)


def pack_pair(x_ref, even_ref, odd_ref, rows):
    low = lax.broadcasted_iota(jnp.int32, (rows * 16, 128), 1) < LANE
    x = x_ref[...].reshape(rows, PACK, 16, 128)
    for half in range(2):
        first = x[:, 2 * half].reshape(rows * 16, 128).astype(jnp.float32)
        second = x[:, 2 * half + 1].reshape(rows * 16, 128).astype(jnp.float32)
        even_ref[:, half * 128:half * 128 + 128] = jnp.where(low, first, pltpu.roll(second, LANE, 1)).astype(jnp.bfloat16)
        odd_ref[:, half * 128:half * 128 + 128] = jnp.where(low, pltpu.roll(first, LANE, 1), second).astype(jnp.bfloat16)


def unpack_pair(even, odd, out_ref, rows):
    low = lax.broadcasted_iota(jnp.int32, (rows * 16, 128), 1) < LANE
    parts = []
    for half in range(2):
        e = even[:, half * 128:half * 128 + 128]
        o = odd[:, half * 128:half * 128 + 128]
        parts.append(jnp.where(low, e, pltpu.roll(o, LANE, 1)).reshape(rows, 1, 16, 128))
        parts.append(jnp.where(low, pltpu.roll(e, LANE, 1), o).reshape(rows, 1, 16, 128))
    out_ref[...] = jnp.concatenate(parts, axis=1).reshape(PACK * rows, 16, 128)


def widen_taps(w_ref, wide_ref, shards):
    per = KW // shards
    sel = spread_matrix(per * GC, per * LANE, GC, LANE)
    block = mm(w_ref[...].reshape(shards * 2 * GC, per * GC), sel).astype(jnp.bfloat16)
    for group in range(2):
        wide_ref[group, GC:, :] = jnp.zeros((LANE - GC, STEPS * 256), jnp.bfloat16)
        wide_ref[group, 0:GC, KW * LANE:] = jnp.zeros((GC, STEPS * 256 - KW * LANE), jnp.bfloat16)
        for s in range(shards):
            start = (2 * s + group) * GC
            wide_ref[group, 0:GC, s * per * LANE:(s + 1) * per * LANE] = block[start:start + GC]


def build_taps(wide_ref, taps_ref, group):
    wide = wide_ref[group]
    shifted = pltpu.roll(wide.astype(jnp.float32), LANE, 1).astype(jnp.bfloat16)
    total = STEPS * 256
    taps_ref[0:64, :] = wide
    taps_ref[64:128, :] = shifted
    taps_ref[128:192, 0:128] = jnp.zeros((64, 128), jnp.bfloat16)
    taps_ref[128:192, 128:total] = wide[:, 0:total - 128]
    taps_ref[192:256, 0:128] = jnp.zeros((64, 128), jnp.bfloat16)
    taps_ref[192:256, 128:total] = shifted[:, 0:total - 128]


def conv_forward_kernel(rows, shards, x_ref, w_ref, y_ref, even_ref, odd_ref, taps_ref, wide_ref):
    m = rows * 16
    pack_pair(x_ref, even_ref, odd_ref, rows + HALF)
    widen_taps(w_ref, wide_ref, shards)
    results = []
    for group, packed in enumerate((even_ref, odd_ref)):
        build_taps(wide_ref, taps_ref, group)
        left = jnp.concatenate([packed[q * 16:q * 16 + m, :] for q in range(STEPS)], axis=1)
        results.append(mm(left, taps_ref[...], NT))
    unpack_pair(results[0], results[1], y_ref, rows)


def conv_forward(x, w, rows, shards):
    frames = PACK * (rows + HALF)
    return pl.pallas_call(
        functools.partial(conv_forward_kernel, rows, shards),
        grid=(GROUPS // 2,),
        in_specs=[
            pl.BlockSpec((frames, 16, 128), lambda g: (0, 0, g)),
            pl.BlockSpec((shards, 2 * GC, w.shape[2]), lambda g: (0, g, 0)),
        ],
        out_specs=pl.BlockSpec((PACK * rows, 16, 128), lambda g: (0, 0, g)),
        out_shape=jax.ShapeDtypeStruct((PACK * rows, 16, PADW), jnp.float32),
        scratch_shapes=[pltpu.VMEM(((rows + HALF) * 16, 256), jnp.bfloat16)] * 2 + [
            pltpu.VMEM((256, STEPS * 256), jnp.bfloat16),
            pltpu.VMEM((2, LANE, STEPS * 256), jnp.bfloat16),
        ],
        cost_estimate=SMALL_COST,
        compiler_params=pltpu.CompilerParams(vmem_limit_bytes=VMEM, dimension_semantics=("arbitrary",)),
        name="conv_forward",
    )(x, w)


def conv_input_kernel(rows, shards, d_ref, w_ref, dx_ref, even_ref, odd_ref, taps_ref, wide_ref):
    m = rows * 16
    pack_pair(d_ref, even_ref, odd_ref, rows + HALF)
    widen_taps(w_ref, wide_ref, shards)
    results = []
    for group, packed in enumerate((even_ref, odd_ref)):
        build_taps(wide_ref, taps_ref, group)
        acc = jnp.zeros((m, 256), jnp.float32)
        for q in range(STEPS):
            left = packed[(HALF - q) * 16:(HALF - q) * 16 + m, :]
            acc = acc + mm(left, taps_ref[:, q * 256:q * 256 + 256])
        results.append(acc)
    unpack_pair(results[0], results[1], dx_ref, rows)


def conv_input_grad(d, w, rows, shards):
    frames = PACK * (rows + HALF)
    return pl.pallas_call(
        functools.partial(conv_input_kernel, rows, shards),
        grid=(GROUPS // 2,),
        in_specs=[
            pl.BlockSpec((frames, 16, 128), lambda g: (0, 0, g)),
            pl.BlockSpec((shards, 2 * GC, w.shape[2]), lambda g: (0, g, 0)),
        ],
        out_specs=pl.BlockSpec((PACK * rows, 16, 128), lambda g: (0, 0, g)),
        out_shape=jax.ShapeDtypeStruct((PACK * rows, 16, PADW), jnp.float32),
        scratch_shapes=[pltpu.VMEM(((rows + HALF) * 16, 256), jnp.bfloat16)] * 2 + [
            pltpu.VMEM((256, STEPS * 256), jnp.bfloat16),
            pltpu.VMEM((2, LANE, STEPS * 256), jnp.bfloat16),
        ],
        cost_estimate=SMALL_COST,
        compiler_params=pltpu.CompilerParams(vmem_limit_bytes=VMEM, dimension_semantics=("arbitrary",)),
        name="conv_input_grad",
    )(d, w)


def conv_weight_kernel(rows, shards, x_ref, d_ref, dw_ref, xe_ref, xo_ref, de_ref, do_ref, prod_ref, grad_ref):
    m = rows * 16
    per = KW // shards
    width = KW * LANE
    pack_pair(x_ref, xe_ref, xo_ref, rows + HALF)
    pack_pair(d_ref, de_ref, do_ref, rows)
    for group, (x_packed, d_packed) in enumerate(((xe_ref, de_ref), (xo_ref, do_ref))):
        d_turned = d_packed[...].astype(jnp.float32).T.astype(jnp.bfloat16)
        for q in range(STEPS):
            prod_ref[:, q * 256:q * 256 + 256] = mm(d_turned, x_packed[q * 16:q * 16 + m, :])
        straight = prod_ref[0:GC, 0:width] + prod_ref[128:128 + GC, 128:128 + width]
        turned_part = prod_ref[64:64 + GC, :] + pltpu.roll(prod_ref[192:192 + GC, :], STEPS * 256 - 128, 1)
        grad = straight + pltpu.roll(turned_part, STEPS * 256 - 64, 1)[:, 0:width]
        grad = grad.astype(jnp.bfloat16)
        for s in range(shards):
            start = (2 * s + group) * GC
            grad_ref[start:start + GC, :] = grad[:, s * per * LANE:(s + 1) * per * LANE]
    sel = spread_matrix(per * GC, per * LANE, GC, LANE)
    dw_ref[...] = mm(grad_ref[...], sel, NT).astype(jnp.bfloat16).reshape(shards, 2 * GC, per * GC)


def conv_weight_grad(x, d, rows, shards):
    per = KW // shards
    first = HALF * PACK // 2
    d = d[first:first + PACK * rows]
    return pl.pallas_call(
        functools.partial(conv_weight_kernel, rows, shards),
        grid=(GROUPS // 2,),
        in_specs=[
            pl.BlockSpec((PACK * (rows + HALF), 16, 128), lambda g: (0, 0, g)),
            pl.BlockSpec((PACK * rows, 16, 128), lambda g: (0, 0, g)),
        ],
        out_specs=pl.BlockSpec((shards, 2 * GC, per * GC), lambda g: (0, g, 0)),
        out_shape=jax.ShapeDtypeStruct((shards, D, per * GC), jnp.bfloat16),
        scratch_shapes=[
            pltpu.VMEM(((rows + HALF) * 16, 256), jnp.bfloat16),
            pltpu.VMEM(((rows + HALF) * 16, 256), jnp.bfloat16),
            pltpu.VMEM((rows * 16, 256), jnp.bfloat16),
            pltpu.VMEM((rows * 16, 256), jnp.bfloat16),
            pltpu.VMEM((256, STEPS * 256), jnp.float32),
            pltpu.VMEM((shards * 2 * GC, per * LANE), jnp.bfloat16),
        ],
        cost_estimate=SMALL_COST,
        compiler_params=pltpu.CompilerParams(vmem_limit_bytes=VMEM, dimension_semantics=("arbitrary",)),
        name="conv_weight_grad",
    )(x, d)


def line_up_kernel(*refs):
    out_ref = refs[-1]
    row = 0
    for ref in refs[:-1]:
        for j in range(ref.shape[1] // 256):
            out_ref[row:row + 1, :] = ref[:, j * 256:j * 256 + 256]
            row += 1


def line_up(vectors):
    vectors = [v.reshape(1, -1) for v in vectors]
    total = sum(v.shape[1] for v in vectors)
    return pl.pallas_call(
        line_up_kernel,
        out_shape=jax.ShapeDtypeStruct((total // 256, 256), jnp.float32),
        name="line_up",
    )(*vectors)


def to_strips(padded, frame_count):
    clips = padded.shape[0]
    strips = 16 // clips
    length = frame_count // strips
    sel = spread_matrix(D, PADW, GC, LANE)
    wide = mm(padded.reshape(-1, D), sel).astype(jnp.bfloat16).reshape(clips, -1, PADW)
    parts = jnp.stack([wide[:, s * length:s * length + length + KW] for s in range(strips)], 1)
    return parts.reshape(16, length + KW, PADW).transpose(1, 0, 2)


def from_strips(y, clips):
    rows = y.transpose(1, 0, 2).reshape(-1, PADW)
    high = lax.reduce_precision(rows, 8, 7)
    rest = (rows - high).astype(jnp.bfloat16)
    high = high.astype(jnp.bfloat16)
    sel = spread_matrix(D, PADW, GC, LANE)
    return mm(high, sel, NT) + mm(rest, sel, NT)


SCALE = HDIM ** (-0.5)


def turned(block):
    return block.astype(jnp.float32).T.astype(jnp.bfloat16)


def attend_kernel(blocks, q_ref, *refs):
    keys = [refs[2 * j] for j in range(blocks)]
    values = [refs[2 * j + 1] for j in range(blocks)]
    mixed_ref, stat_ref = refs[2 * blocks:]
    frames = q_ref.shape[0]
    low = lax.broadcasted_iota(jnp.int32, (frames, 128), 1) < HDIM
    scaled = q_ref[...] * jnp.bfloat16(SCALE)
    none = jnp.zeros_like(scaled)
    turned_keys = [turned(k[...]) for k in keys]
    parts = []
    stats = []
    for head in range(2):
        query = jnp.where(low, scaled, none) if head == 0 else jnp.where(low, none, scaled)
        scores = [mm(query, k) for k in turned_keys]
        largest = functools.reduce(jnp.maximum, [jnp.max(s, 1, keepdims=True) for s in scores])
        powers = [jnp.exp(s - largest) for s in scores]
        total = functools.reduce(jnp.add, [jnp.sum(p, 1, keepdims=True) for p in powers])
        out = functools.reduce(jnp.add, [mm(p.astype(jnp.bfloat16), v[...]) for p, v in zip(powers, values)])
        parts.append(out * (1.0 / total))
        stats.append(jnp.broadcast_to(largest + jnp.log(total), (frames, 128)))
    mixed_ref[...] = jnp.where(low, parts[0], parts[1]).astype(jnp.bfloat16)
    rows = jnp.where(low, stats[0], stats[1]).T
    stat_ref[0, 0, 0:1, :] = rows[0:1, :]
    stat_ref[0, 0, 1:2, :] = rows[HDIM:HDIM + 1, :]


def attend(query, keys, values, clips):
    blocks = len(keys)
    rows = query.shape[0]
    frames = rows // clips
    spec = pl.BlockSpec((frames, 128), lambda c, h: (c, h))
    operands = [query]
    for k, v in zip(keys, values):
        operands += [k, v]
    return pl.pallas_call(
        functools.partial(attend_kernel, blocks),
        grid=(clips, HEADS // 2),
        in_specs=[spec] * len(operands),
        out_specs=[spec, pl.BlockSpec((1, 1, 2, frames), lambda c, h: (c, h, 0, 0))],
        out_shape=[
            jax.ShapeDtypeStruct((rows, D), jnp.bfloat16),
            jax.ShapeDtypeStruct((clips, HEADS // 2, 2, frames), jnp.float32),
        ],
        cost_estimate=SMALL_COST,
        compiler_params=pltpu.CompilerParams(vmem_limit_bytes=VMEM, dimension_semantics=("arbitrary", "arbitrary")),
        name="attend",
    )(*operands)


def attend_back_kernel(blocks, q_ref, d_ref, stat_ref, *refs):
    keys = [refs[2 * j] for j in range(blocks)]
    values = [refs[2 * j + 1] for j in range(blocks)]
    dq_ref = refs[2 * blocks]
    dk = [refs[2 * blocks + 1 + 2 * j] for j in range(blocks)]
    dv = [refs[2 * blocks + 2 + 2 * j] for j in range(blocks)]
    frames = q_ref.shape[0]
    low = lax.broadcasted_iota(jnp.int32, (frames, 128), 1) < HDIM
    scaled = q_ref[...] * jnp.bfloat16(SCALE)
    grad = d_ref[...]
    none = jnp.zeros_like(scaled)
    q_turned = turned(scaled)
    d_turned = turned(grad)
    gap = jnp.zeros((HDIM, frames), jnp.bfloat16)
    k_turned = [turned(k[...]) for k in keys]
    dq_rows = []
    dk_sum = [None] * blocks
    dv_sum = [None] * blocks
    for head in range(2):
        pick = slice(head * HDIM, head * HDIM + HDIM)
        if head == 0:
            query, grad_head = jnp.where(low, scaled, none), jnp.where(low, grad, none)
            q_side = jnp.concatenate([q_turned[pick], gap], 0)
            d_side = jnp.concatenate([d_turned[pick], gap], 0)
        else:
            query, grad_head = jnp.where(low, none, scaled), jnp.where(low, none, grad)
            q_side = jnp.concatenate([gap, q_turned[pick]], 0)
            d_side = jnp.concatenate([gap, d_turned[pick]], 0)
        stat = stat_ref[0, 0, head:head + 1, :]
        probs = [jnp.exp(mm(k[...], q_side) - stat) for k in keys]
        weighted = [p * mm(v[...], d_side) for p, v in zip(probs, values)]
        delta = functools.reduce(jnp.add, [jnp.sum(w, 0, keepdims=True) for w in weighted])
        dq = None
        for j in range(blocks):
            ds = (weighted[j] - probs[j] * delta).astype(jnp.bfloat16)
            grad_v = mm(probs[j].astype(jnp.bfloat16), grad_head)
            grad_k = mm(ds, query)
            part = mm(k_turned[j][pick], ds)
            dq = part if dq is None else dq + part
            dv_sum[j] = grad_v if dv_sum[j] is None else dv_sum[j] + grad_v
            dk_sum[j] = grad_k if dk_sum[j] is None else dk_sum[j] + grad_k
        dq_rows.append(dq)
    dq_ref[...] = (jnp.concatenate(dq_rows, 0) * SCALE).T.astype(jnp.bfloat16)
    for j in range(blocks):
        dk[j][...] = dk_sum[j].astype(jnp.bfloat16)
        dv[j][...] = dv_sum[j].astype(jnp.bfloat16)


def attend_back(query, grad, stat, keys, values, clips):
    blocks = len(keys)
    rows = query.shape[0]
    frames = rows // clips
    spec = pl.BlockSpec((frames, 128), lambda c, h: (c, h))
    operands = []
    for k, v in zip(keys, values):
        operands += [k, v]
    shape = jax.ShapeDtypeStruct((rows, D), jnp.bfloat16)
    return pl.pallas_call(
        functools.partial(attend_back_kernel, blocks),
        grid=(clips, HEADS // 2),
        in_specs=[spec, spec, pl.BlockSpec((1, 1, 2, frames), lambda c, h: (c, h, 0, 0))] + [spec] * len(operands),
        out_specs=[spec] * (1 + 2 * blocks),
        out_shape=[shape] * (1 + 2 * blocks),
        cost_estimate=SMALL_COST,
        compiler_params=pltpu.CompilerParams(vmem_limit_bytes=VMEM, dimension_semantics=("arbitrary", "arbitrary")),
        name="attend_back",
    )(query, grad, stat, *operands)


def count_kernel(draws, n_ref, out_ref):
    length, frames = out_ref.shape[1:]
    place = lax.broadcasted_iota(jnp.int32, (length // 8, 8, frames), 0) * 8 + lax.broadcasted_iota(
        jnp.int32, (length // 8, 8, frames), 1)
    total = jnp.zeros((length // 8, 8, frames), jnp.float32)
    for n in range(draws):
        row = n_ref[0, n:n + 1, :]
        total = total + jnp.where(place == row[None], 1.0, 0.0)
    out_ref[0] = total.reshape(length, frames).astype(jnp.bfloat16)


def count_draws(negatives, length):
    clips, draws, frames = negatives.shape
    tile = 128 if frames % 128 == 0 else frames
    return pl.pallas_call(
        functools.partial(count_kernel, draws),
        grid=(clips, frames // tile),
        in_specs=[pl.BlockSpec((1, draws, tile), lambda c, f: (c, 0, f))],
        out_specs=pl.BlockSpec((1, length, tile), lambda c, f: (c, 0, f)),
        out_shape=jax.ShapeDtypeStruct((clips, length, frames), jnp.bfloat16),
        cost_estimate=SMALL_COST,
        compiler_params=pltpu.CompilerParams(vmem_limit_bytes=VMEM, dimension_semantics=("arbitrary", "arbitrary")),
        name="count_draws",
    )(negatives)


MESH = pl.DeviceIdType.MESH
AHEAD = 3
OTHER = 2


def reduce_kernel(count, seqs, sizes, *refs):
    number = len(sizes)
    sources = refs[:number]
    outs = refs[number : 2 * number]
    bits = count.bit_length() - 1
    turns = seqs.bit_length() - 1
    levels = bits + turns
    held = refs[2 * number : 2 * number + levels]
    send_sem, recv_sem = refs[2 * number + levels :]
    me = lax.axis_index("shard")
    place = lax.axis_index("seq")

    def across(index, bit):
        return index + (1 - 2 * ((index // 2**bit) % 2)) * 2**bit

    partners = [{"shard": across(me, b)} for b in range(bits)] + [{"seq": across(place, t)} for t in range(turns)]
    barrier = pltpu.get_barrier_semaphore()
    for partner in partners:
        pl.semaphore_signal(barrier, inc=1, device_id=partner, device_id_type=MESH)
    pl.semaphore_wait(barrier, len(partners))

    pieces = []
    offset = 0
    for source, out, (rows, cut) in zip(sources, outs, sizes):
        for start in range(0, rows, cut):
            pieces.append((source, out, start, offset + start, cut))
        offset += rows
    orders = [list(range(bits)), list(range(bits))]
    if bits > 2:
        orders[1] = [0] + list(range(2, bits)) + [1]
    flights = {}

    def moves(piece, level):
        order = orders[1 if piece % 5 == OTHER else 0]
        if level >= bits:
            return [(0, 0)], partners[level]
        bit = order[level]
        left = sorted(order[level:])
        low = 2 ** left.index(bit)
        side = (me // 2**bit) % 2
        pairs = []
        for j in range(2 ** (bits - level - 1)):
            base = (j // low) * 2 * low + j % low
            pairs.append((base + side * low, base + (1 - side) * low))
        return pairs, partners[bit]

    def data(piece, level, index):
        source, _, start, spot, cut = pieces[piece]
        if level == 0:
            return source.at[index, pl.ds(start, cut)]
        return held[level - 1].at[index, pl.ds(spot, cut)]

    def launch(piece, level):
        pairs, partner = moves(piece, level)
        _, _, _, spot, cut = pieces[piece]
        copies = []
        for j, (_, sent) in enumerate(pairs):
            copies.append(
                pltpu.make_async_remote_copy(
                    src_ref=data(piece, level, sent),
                    dst_ref=held[level].at[j, pl.ds(spot, cut)],
                    send_sem=send_sem.at[piece, level, j],
                    recv_sem=recv_sem.at[piece, level, j],
                    device_id=partner,
                    device_id_type=MESH,
                )
            )
        for copy in copies:
            copy.start()
        flights[piece, level] = copies

    def absorb(piece, level):
        pairs, _ = moves(piece, level)
        _, out, start, spot, cut = pieces[piece]
        for j, (kept, _) in enumerate(pairs):
            flights[piece, level][j].wait()
            mine, other = data(piece, level, kept)[...], held[level][j, pl.ds(spot, cut)]
            if level == levels - 1:
                out[pl.ds(start, cut)] = mine.astype(jnp.float32) + other.astype(jnp.float32)
            else:
                held[level][j, pl.ds(spot, cut)] = mine + other

    delay = [0, 1] + [1 + AHEAD * level for level in range(1, levels)]
    for wave in range(len(pieces) + delay[-1]):
        for level in range(levels, -1, -1):
            piece = wave - delay[level]
            if 0 <= piece < len(pieces):
                if level > 0:
                    absorb(piece, level - 1)
                if level < levels:
                    launch(piece, level)


def reduce_chunks(call, mesh_sizes, cuts, *chunks):
    count, seqs = mesh_sizes
    bits, turns = count.bit_length() - 1, seqs.bit_length() - 1
    lanes = chunks[0].shape[2]
    sizes = [(c.shape[1], cut) for c, cut in zip(chunks, cuts)]
    total = sum(rows for rows, _ in sizes)
    number = sum(rows // cut for rows, cut in sizes)
    slots = [2 ** (bits - 1 - level) for level in range(bits)] + [1] * turns
    return pl.pallas_call(
        functools.partial(reduce_kernel, count, seqs, sizes),
        in_specs=[pl.BlockSpec(memory_space=pltpu.VMEM)] * len(chunks),
        out_specs=[pl.BlockSpec(memory_space=pltpu.VMEM)] * len(chunks),
        out_shape=[jax.ShapeDtypeStruct(c.shape[1:], jnp.float32) for c in chunks],
        scratch_shapes=[pltpu.VMEM((n, total, lanes), jnp.bfloat16) for n in slots]
        + [pltpu.SemaphoreType.DMA((number, bits + turns, count // 2))] * 2,
        cost_estimate=SMALL_COST,
        compiler_params=pltpu.CompilerParams(collective_id=call, has_side_effects=True, vmem_limit_bytes=VMEM),
        name="reduce_chunks",
    )(*chunks)


def swap_moves(count, step):
    return [(i, (i - step) % count) for i in range(count)]


def gather_ring(block):
    count = lax.axis_size("seq")
    return [block] + [lax.ppermute(block, "seq", swap_moves(count, step)) for step in range(1, count)]


def return_ring(blocks):
    count = lax.axis_size("seq")
    return [lax.ppermute(block, "seq", swap_moves(count, -step)) for step, block in enumerate(blocks) if step > 0]


def seq_sum(values):
    if lax.axis_size("seq") > 2:
        return lax.psum(values, "seq").astype(jnp.float32)
    other = lax.ppermute(values, "seq", [(0, 1), (1, 0)])
    return values.astype(jnp.float32) + other.astype(jnp.float32)


def lowered(values):
    return values.astype(jnp.bfloat16)


def bdot(left_side, right_side):
    return jnp.dot(left_side, right_side, preferred_element_type=jnp.float32)


def turned_dot(left_side, right_side):
    return lax.dot_general(left_side, right_side, NT, preferred_element_type=jnp.float32)


def rows_dot(left_side, right_side):
    return lax.dot_general(left_side, right_side, (((0,), (0,)), ((), ())), preferred_element_type=jnp.float32)


def fdot(left_side, right_side):
    return jnp.dot(left_side, right_side, precision=lax.Precision.HIGHEST, preferred_element_type=jnp.float32)


def column_sum(values):
    return jnp.sum(values.astype(jnp.float32), 0, keepdims=True)


def gelu_parts(values):
    half = 0.5 * (1.0 + lax.erf(values * 0.5**0.5))
    density = jnp.exp(-0.5 * values * values) * (2.0 * jnp.pi) ** -0.5
    return values * half, half + values * density


def norm_forward(values, gain_row, bias_row):
    centred = values - jnp.mean(values, -1, keepdims=True)
    spread = jnp.mean(centred * centred, -1, keepdims=True)
    scale = lax.rsqrt(spread + norm_epsilon)
    level = centred * scale
    return level * gain_row + bias_row, (level, scale, gain_row)


def norm_vectors(grad, kept):
    level = kept[0]
    return jnp.sum(grad * level, 0, keepdims=True), jnp.sum(grad, 0, keepdims=True)


def norm_backward(grad, kept):
    level, scale, gain_row = kept
    inside = grad * gain_row
    centred = inside - jnp.mean(inside, -1, keepdims=True) - level * jnp.mean(inside * level, -1, keepdims=True)
    return (scale * centred,) + norm_vectors(grad, kept)


def unit_rows(values):
    return values * lax.rsqrt(jnp.sum(values * values, -1, keepdims=True) + unit_epsilon)


def vector_pieces(vector):
    widths = [CIN, CIN, D, D, D, D, D] + [D, D, D, D, D, FF, D, D, D] * LAYERS + [PROJ, PROJ]
    pieces = []
    offset = 0
    for width in widths:
        pieces.append(vector[offset : offset + width])
        offset = offset + width
    return pieces


def with_halo(block, width):
    count = lax.axis_size("seq")
    forward = [(i, i + 1) for i in range(count - 1)]
    backward = [(i + 1, i) for i in range(count - 1)]
    low = lax.ppermute(block[:, block.shape[1] - width :], "seq", forward)
    high = lax.ppermute(block[:, :width], "seq", backward)
    return jnp.concatenate([low, block, high], axis=1)


def layer_forward(hidden, attn_w, expand_w, shrink_w, pieces, clip_count, *waiting):
    q_bias, v_bias, o_bias, gain_one, bias_one, expand_bias, shrink_bias, gain_two, bias_two = pieces
    entries = gather_ring(lowered(hidden))
    query = lowered(bdot(entries[0], attn_w[:, :D]) + q_bias)
    keys = [lowered(bdot(entry, attn_w[:, D : 2 * D])) for entry in entries]
    values = [lowered(bdot(entry, attn_w[:, 2 * D : 3 * D]) + v_bias) for entry in entries]
    mixed, stat = attend(query, keys, values, clip_count)
    if waiting:
        mixed, *waiting = fence(mixed, *waiting)
    branch = bdot(mixed, attn_w[:, 3 * D :]) + o_bias
    middle, middle_kept = norm_forward(hidden + branch, gain_one, bias_one)
    middle_low = lowered(middle)
    inner = bdot(middle_low, expand_w) + expand_bias
    activated, slope = gelu_parts(inner)
    active_low = lowered(activated)
    slope_low = lowered(slope)
    outer = bdot(active_low, shrink_w) + shrink_bias
    result, final_kept = norm_forward(middle + outer, gain_two, bias_two)
    cache = (entries, query, keys, values, mixed, stat, middle_kept, middle_low, slope_low, active_low, final_kept)
    return (result, cache) + tuple(waiting or [None])


def feed_backward(grad_out, cache, expand_w, shrink_w):
    middle_low, slope_low, active_low, final_kept = cache[7:]
    grad_sum, grad_gain, grad_bias = norm_backward(grad_out, final_kept)
    grad_outer = lowered(grad_sum)
    grad_shrink = lowered(rows_dot(active_low, grad_outer))
    grad_inner = lowered(slope_low.astype(jnp.float32) * turned_dot(grad_outer, shrink_w))
    grad_expand = lowered(rows_dot(middle_low, grad_inner))
    grad_middle = grad_sum + turned_dot(grad_inner, expand_w)
    vectors = [column_sum(grad_inner), column_sum(grad_outer), grad_gain, grad_bias]
    return grad_middle, grad_expand, grad_shrink, vectors


def attend_backward(grad_middle, cache, attn_w, clip_count, *waiting):
    entries, query, keys, values, mixed, stat, middle_kept = cache[:7]
    grad_sum, grad_gain, grad_bias = norm_backward(grad_middle, middle_kept)
    grad_branch = lowered(grad_sum)
    grad_mixed = lowered(turned_dot(grad_branch, attn_w[:, 3 * D :]))
    results = attend_back(query, grad_mixed, stat, keys, values, clip_count)
    results, grad_branch, *waiting = fence(results, grad_branch, *waiting)
    grad_query, grad_keys, grad_values = results[0], results[1::2], results[2::2]
    back = [
        turned_dot(dk, attn_w[:, D : 2 * D]) + turned_dot(dv, attn_w[:, 2 * D : 3 * D])
        for dk, dv in zip(grad_keys, grad_values)
    ]
    arrived = return_ring([lowered(block) for block in back])
    grad_hidden = grad_sum + turned_dot(grad_query, attn_w[:, :D]) + back[0]
    for block in arrived:
        grad_hidden = grad_hidden + block.astype(jnp.float32)
    grads = [
        lowered(rows_dot(entries[0], grad_query)),
        lowered(sum(rows_dot(entry, dk) for entry, dk in zip(entries, grad_keys))),
        lowered(sum(rows_dot(entry, dv) for entry, dv in zip(entries, grad_values))),
        lowered(rows_dot(mixed, grad_branch)),
    ]
    vectors = [
        column_sum(grad_query),
        sum(column_sum(dv) for dv in grad_values),
        column_sum(grad_branch),
        grad_gain,
        grad_bias,
    ]
    return grad_hidden, grads, vectors, waiting


def adam_update(weight, grad, first, second, rate, decay):
    first = beta_one * first + (1 - beta_one) * grad
    second = beta_two * second + (1 - beta_two) * grad * grad
    share_fraction = (
        first / (1 - beta_one**STEP) / (jnp.sqrt(second / (1 - beta_two**STEP)) + adam_epsilon)
    )
    return (weight - rate * (share_fraction + decay * weight), first, second)


def gather_rows(block):
    whole = lax.all_gather(block, "shard", axis=0, tiled=True)
    return whole.reshape((-1,) + block.shape)


def pass_kernel(*refs):
    pass


def fence(*values):
    flat, tree = jax.tree.flatten(values)
    spec = pl.BlockSpec(memory_space=pl.ANY)
    flat = pl.pallas_call(
        pass_kernel,
        in_specs=[spec] * len(flat),
        out_specs=[spec] * len(flat),
        out_shape=[jax.ShapeDtypeStruct(v.shape, v.dtype) for v in flat],
        input_output_aliases={i: i for i in range(len(flat))},
        cost_estimate=SMALL_COST,
        name="fence",
    )(*flat)
    return jax.tree.unflatten(tree, flat)


def scatter_chunks(chunks):
    return lax.psum_scatter(chunks, "shard", scatter_dimension=0, tiled=False)


def trade(chunks):
    return lax.all_to_all(chunks, "shard", split_axis=0, concat_axis=0, tiled=True)


def on_device(
    features,
    time_mask,
    negatives,
    target_codes,
    feature_weight,
    feature_first,
    feature_second,
    conv_weight,
    conv_first,
    conv_second,
    attention_weight,
    attention_first,
    attention_second,
    left_basis_t,
    right_orthogonal_basis,
    expand_weight,
    expand_first,
    expand_second,
    shrink_weight,
    shrink_first,
    shrink_second,
    final_weight,
    final_first,
    final_second,
    target_weight,
    target_first,
    target_second,
    codebook_weight,
    codebook_first,
    codebook_second,
    vector_params,
    vector_first,
    vector_second,
):
    clip_count, frame_count = (features.shape[0], features.shape[1])
    row_count = clip_count * frame_count
    seq_count = lax.axis_size("seq")
    shards = lax.axis_size("shard")
    clip_frames = frame_count * seq_count
    small_items = [feature_weight, final_weight, target_weight, codebook_weight, vector_params]
    small_sizes = [item.size for item in small_items]
    small_total = sum(small_sizes)
    small_width = -(-(small_total + 2) // SMALL_LANES) * SMALL_LANES

    def split_small(flat):
        parts = []
        offset = 0
        for item, size in zip(small_items, small_sizes):
            parts.append(flat[:, offset : offset + size].reshape((-1,) + item.shape[1:]))
            offset = offset + size
        return parts

    small = jnp.concatenate([lowered(item).reshape(-1) for item in small_items])
    small = jnp.pad(small, (0, small_width - small_total))
    taps = conv_weight.shape[0]
    (own_first,) = fence(jnp.concatenate([lowered(conv_weight).T, small.reshape(-1, taps)]))
    first_all = gather_rows(own_first)
    conv_w = first_all
    feat_w, final_w, target_w, code_w, vector_low = split_small(first_all[:, D:].reshape(shards, -1))
    attn_w, expand_w, shrink_w = [], [], []
    rows = D // shards

    def own_attn(layer):
        return jnp.concatenate([lowered(attention_weight[4 * layer + i]) for i in range(4)])

    def own_feed(layer):
        expand_own = lowered(expand_weight[layer])
        return jnp.concatenate(
            [expand_own[:, j * D : (j + 1) * D] for j in range(FF // D)] + [lowered(shrink_weight[layer])]
        )

    def use_attn(whole):
        attn_w.append(jnp.concatenate([whole[:, j * rows : (j + 1) * rows].reshape(D, D) for j in range(4)], 1))

    def use_feed(whole):
        blocks = [whole[:, j * rows : (j + 1) * rows].reshape(D, D) for j in range(FF // D)]
        expand_w.append(jnp.concatenate(blocks, 1))
        shrink_w.append(whole[:, FF // D * rows :].reshape(FF, D))

    first_frame = lax.axis_index("seq") * frame_count
    ring_draws = (negatives - first_frame + clip_frames) % clip_frames
    counts = count_draws(ring_draws.transpose(0, 2, 1), clip_frames)
    counts, own_0 = fence(counts, jnp.concatenate([own_attn(0), own_feed(0)]))
    whole = gather_rows(own_0)
    use_attn(whole[:, : 4 * rows])
    use_feed(whole[:, 4 * rows :])
    parts = shards // (4 * LAYERS)

    pieces = vector_pieces(vector_low.astype(jnp.float32))
    mask_on = (time_mask > 0).reshape(row_count, 1)
    feats = features.reshape(row_count, CIN).astype(jnp.float32)
    normed, norm_kept = norm_forward(feats, pieces[0], pieces[1])
    normed_low = lowered(normed)
    projected = bdot(normed_low, feat_w) + pieces[2]
    masked = jnp.where(mask_on, pieces[3][None, :], projected)
    padded = with_halo(lowered(masked).reshape(clip_count, frame_count, D), KW // 2)
    strip_rows = frame_count * clip_count // 16 // PACK
    strips = to_strips(padded, frame_count)
    conv_out = from_strips(conv_forward(strips, conv_w, strip_rows, shards), clip_count) + pieces[4]
    conv_active, conv_slope = gelu_parts(conv_out)
    hidden, front_kept = norm_forward(masked + conv_active, pieces[5], pieces[6])

    hidden, own_1 = fence(hidden, own_attn(1))
    use_attn(gather_rows(own_1))
    hidden, cache, own_1 = layer_forward(
        hidden, attn_w[0], expand_w[0], shrink_w[0], pieces[7:16], clip_count, own_feed(1)
    )
    caches = [cache]
    use_feed(gather_rows(own_1))
    hidden, cache, _ = layer_forward(hidden, attn_w[1], expand_w[1], shrink_w[1], pieces[16:25], clip_count)
    caches.append(cache)
    top_low = lowered(hidden)
    context, context_pull = jax.vjp(unit_rows, bdot(top_low, final_w) + pieces[-2])
    context_low = lowered(context).reshape(clip_count, frame_count, PROJ)
    held = jnp.stack([lowered(left_basis_t), lowered(attention_first), lowered(attention_second)], 1)
    context_low, held = fence(context_low, held)
    traded = trade(jnp.repeat(held, parts, axis=0))

    counts = counts.astype(jnp.float32)
    codes = jnp.concatenate(gather_ring(target_codes), 1).reshape(clip_count * clip_frames, QGROUPS)
    width = PROJ // QGROUPS
    code_f = code_w.astype(jnp.float32)
    target_f = target_w.astype(jnp.float32)
    table = jnp.concatenate(
        [fdot(code_f[g * width : (g + 1) * width].T, target_f[g * width : (g + 1) * width]) for g in range(QGROUPS)]
    )
    choice = jnp.concatenate(
        [(codes[:, g : g + 1] == jnp.arange(CODES)[None, :]).astype(jnp.float32) for g in range(QGROUPS)], 1
    )
    targets, target_pull = jax.vjp(unit_rows, fdot(choice, table) + pieces[-1])
    targets_low = lowered(targets).reshape(clip_count, clip_frames, PROJ)
    similar = jnp.einsum("clp,cfp->clf", targets_low, context_low, preferred_element_type=jnp.float32)
    logits = similar / contrastive_sharpness
    place = jnp.arange(clip_frames)[:, None] == jnp.arange(frame_count)[None, :]
    own = place.astype(jnp.float32)[None]
    weight = counts + own
    largest = jnp.max(jnp.where(weight > 0, logits, -jnp.inf), 1, keepdims=True)
    power = weight * jnp.exp(jnp.where(weight > 0, logits - largest, 0.0))
    running_totals = jnp.sum(power, 1, keepdims=True)
    mask_as_floats = time_mask.astype(jnp.float32)
    own_logit = jnp.sum(own * logits, 1)
    row_loss = largest[:, 0] + jnp.log(running_totals[:, 0]) - own_logit
    loss_sum = jnp.sum(mask_as_floats * row_loss)
    mask_count = jnp.sum(mask_as_floats)
    derivative_multiplier = 1.0 / (clip_count * shards * clip_frames)
    grad_similar = lowered(
        mask_as_floats[:, None, :]
        * (power / running_totals - own)
        * (derivative_multiplier / contrastive_sharpness)
    )
    grad_context = jnp.einsum("clf,clp->cfp", grad_similar, targets_low, preferred_element_type=jnp.float32)
    grad_targets = jnp.einsum("clf,cfp->clp", grad_similar, context_low, preferred_element_type=jnp.float32)
    (grad_raw,) = target_pull(grad_targets.reshape(-1, PROJ))
    grad_table = fdot(choice.T, grad_raw)
    tables = [grad_table[g * CODES : (g + 1) * CODES] for g in range(QGROUPS)]
    grad_target_w = jnp.concatenate([fdot(code_f[g * width : (g + 1) * width], tables[g]) for g in range(QGROUPS)])
    grad_codebook = jnp.concatenate(
        [fdot(target_f[g * width : (g + 1) * width], tables[g].T) for g in range(QGROUPS)]
    )
    grad_target_bias = column_sum(grad_raw)
    (grad_context_raw,) = context_pull(grad_context.reshape(row_count, PROJ))
    grad_context_low = lowered(grad_context_raw)
    grad_final_w = rows_dot(top_low, grad_context_low)
    grad_final_bias = column_sum(grad_context_low)
    grad_hidden = turned_dot(grad_context_low, final_w)

    columns = D // parts
    def rotated_adam(first, second, grad):
        first = beta_rotated * first + (1 - beta_rotated) * grad
        second = beta_rotated * second + (1 - beta_rotated) * grad * grad
        share = first / (1 - beta_rotated**STEP) / (jnp.sqrt(second / (1 - beta_rotated**STEP)) + adam_epsilon)
        return share, first, second

    def rotate(whole_grad):
        left_low, first_low, second_low = [traded[:, i].reshape(D, D) for i in range(3)]
        group = lax.axis_index("shard") // parts
        right_low = lowered(lax.dynamic_index_in_dim(right_orthogonal_basis, group, 0, keepdims=False))
        rotated = bdot(lowered(bdot(left_low, whole_grad)), right_low)
        direction = rotated_adam(first_low.astype(jnp.float32), second_low.astype(jnp.float32), rotated)[0]
        half_back = lowered(turned_dot(lowered(direction), right_low))
        part_start = (lax.axis_index("shard") % parts) * columns
        rotated_part = lax.dynamic_slice_in_dim(lowered(rotated), part_start, columns, 1)
        update_part = lowered(rows_dot(left_low, lax.dynamic_slice_in_dim(half_back, part_start, columns, 1)))
        sent = jnp.stack([rotated_part.reshape(shards, rows, columns), update_part.reshape(shards, rows, columns)], 1)
        return sent

    def feed_blocks(grad_expand, grad_shrink):
        blocks = [grad_expand[:, j * D : (j + 1) * D].reshape(shards, -1, D) for j in range(FF // D)]
        return blocks + [grad_shrink.reshape(shards, -1, D)]

    def attn_blocks(grads):
        return [grad.reshape(shards, -1, D) for grad in grads]

    grad_middle, grad_expand, grad_shrink, feed_vectors_1 = feed_backward(
        grad_hidden, caches[1], expand_w[1], shrink_w[1]
    )
    grad_hidden, grads, attn_vectors_1, (traded,) = attend_backward(
        grad_middle, caches[1], attn_w[1], clip_count, traded
    )
    chunks = jnp.concatenate(attn_blocks(grads) + feed_blocks(grad_expand, grad_shrink), 1)
    grad_hidden, chunks = fence(grad_hidden, chunks)
    sum_1 = scatter_chunks(chunks)
    grad_middle, grad_expand, grad_shrink, feed_vectors_0 = feed_backward(
        grad_hidden, caches[0], expand_w[0], shrink_w[0]
    )
    feed_grads = feed_blocks(grad_expand, grad_shrink)
    grad_hidden, grads, attn_vectors_0, _ = attend_backward(grad_middle, caches[0], attn_w[0], clip_count)
    grad_hidden, chunks = fence(grad_hidden, jnp.concatenate(attn_blocks(grads) + feed_grads, 1))
    sum_0 = scatter_chunks(chunks)
    mesh_sizes = (shards, seq_count)
    grad_sum, grad_gain_enc, grad_bias_enc = norm_backward(grad_hidden, front_kept)
    grad_conv_low = lowered(grad_sum * conv_slope)
    grad_strips = to_strips(with_halo(grad_conv_low.reshape(clip_count, frame_count, D), KW // 2), frame_count)
    conv_chunks = conv_weight_grad(strips, grad_strips, strip_rows, shards)
    grad_strips, conv_chunks, sum_1 = fence(grad_strips, conv_chunks, sum_1)
    sum_1 = seq_sum(sum_1)
    grad_back = conv_input_grad(grad_strips, conv_w, strip_rows, shards)
    grad_back, sum_1 = fence(grad_back, sum_1)
    grad_masked = grad_sum + from_strips(grad_back, clip_count)
    grad_embedding = jnp.sum(jnp.where(mask_on, grad_masked, 0.0), 0, keepdims=True)
    grad_projected = lowered(jnp.where(mask_on, 0.0, grad_masked))
    grad_feat_w = rows_dot(normed_low, grad_projected)
    grad_gain_feat, grad_bias_feat = norm_vectors(turned_dot(grad_projected, feat_w), norm_kept)
    vector_grads = [
        grad_gain_feat,
        grad_bias_feat,
        column_sum(grad_projected),
        grad_embedding,
        column_sum(grad_conv_low),
        grad_gain_enc,
        grad_bias_enc,
    ]
    vector_grads += attn_vectors_0 + feed_vectors_0 + attn_vectors_1 + feed_vectors_1
    vector_grads = line_up(vector_grads + [grad_final_bias, grad_target_bias])
    small_grads = [
        lowered(item).reshape(shards, -1)
        for item in (grad_feat_w, grad_final_w, grad_target_w, grad_codebook, vector_grads)
    ]
    loss_tile = jnp.broadcast_to(lowered(jnp.stack([loss_sum, mask_count]))[None], (shards, 2))
    gap = jnp.zeros((shards, small_width - small_total - 2), jnp.bfloat16)
    small_chunks = jnp.concatenate(small_grads + [loss_tile, gap], 1)
    small_chunks, sum_0 = fence(small_chunks.reshape(shards, -1, taps), sum_0)
    sum_0 = seq_sum(sum_0)
    attn_rows = jnp.concatenate([sum_0[: 4 * rows], sum_1[: 4 * rows]]).reshape(4 * LAYERS, rows, D)
    whole_grad = trade(jnp.repeat(lowered(attn_rows), parts, axis=0)).reshape(D, D)
    sent = rotate(whole_grad)
    sent, small_chunks = fence(sent, small_chunks)
    rotation = trade(sent)
    small_sum, sum_conv = reduce_chunks(0, mesh_sizes, (128, 96), small_chunks, conv_chunks)
    small_sum = small_sum.reshape(1, -1)
    sum_conv = sum_conv.T
    arrived = rotation.reshape(4 * LAYERS, parts, 2, rows, columns).transpose(2, 0, 3, 1, 4)
    arrived = arrived.reshape(2, 4 * LAYERS, rows, D).astype(jnp.float32)
    _, rot_first, rot_second = rotated_adam(attention_first, attention_second, arrived[0])
    new_attention = attention_weight - rate_rotated * arrived[1]
    feed_sums = [sum_0[4 * rows :], sum_1[4 * rows :]]
    sum_loss = small_sum[0, small_total : small_total + 2]
    sum_feat, sum_final, sum_target, sum_code, sum_vector = split_small(small_sum)
    sum_expand = jnp.stack(
        [s[: -shrink_weight.shape[1]].reshape(FF // D, -1, D).transpose(1, 0, 2).reshape(-1, FF) for s in feed_sums]
    )
    sum_shrink = jnp.stack([s[-shrink_weight.shape[1] :] for s in feed_sums])
    feature_new = adam_update(feature_weight, sum_feat, feature_first, feature_second, rate_matrix, decay_rate)
    conv_new = adam_update(conv_weight, sum_conv, conv_first, conv_second, rate_matrix, decay_rate)
    expand_new = adam_update(expand_weight, sum_expand, expand_first, expand_second, rate_matrix, decay_rate)
    shrink_new = adam_update(shrink_weight, sum_shrink, shrink_first, shrink_second, rate_matrix, decay_rate)
    final_new = adam_update(final_weight, sum_final, final_first, final_second, rate_matrix, decay_rate)
    target_new = adam_update(target_weight, sum_target, target_first, target_second, rate_target, decay_rate)
    codebook_new = adam_update(codebook_weight, sum_code, codebook_first, codebook_second, rate_codebook, decay_rate)
    vector_new = adam_update(vector_params, sum_vector, vector_first, vector_second, rate_vector, 0.0)
    return (
        (sum_loss,)
        + feature_new
        + conv_new
        + (new_attention, rot_first, rot_second)
        + expand_new
        + shrink_new
        + final_new
        + target_new
        + codebook_new
        + vector_new
    )


def solution(mesh):
    return jax.shard_map(
        on_device,
        mesh=mesh,
        in_specs=(
            P("shard", "seq", None),
            P("shard", "seq"),
            P("shard", "seq", None),
            P("shard", "seq", None),
            P("shard", None),
            P("shard", None),
            P("shard", None),
            P("shard", None),
            P("shard", None),
            P("shard", None),
            P(None, "shard", None),
            P(None, "shard", None),
            P(None, "shard", None),
            P(None, "shard", None),
            P(),
            P(None, "shard", None),
            P(None, "shard", None),
            P(None, "shard", None),
            P(None, "shard", None),
            P(None, "shard", None),
            P(None, "shard", None),
            P("shard", None),
            P("shard", None),
            P("shard", None),
            P("shard", None),
            P("shard", None),
            P("shard", None),
            P("shard", None),
            P("shard", None),
            P("shard", None),
            P("shard"),
            P("shard"),
            P("shard"),
        ),
        out_specs=(
            P(),
            P("shard", None),
            P("shard", None),
            P("shard", None),
            P("shard", None),
            P("shard", None),
            P("shard", None),
            P(None, "shard", None),
            P(None, "shard", None),
            P(None, "shard", None),
            P(None, "shard", None),
            P(None, "shard", None),
            P(None, "shard", None),
            P(None, "shard", None),
            P(None, "shard", None),
            P(None, "shard", None),
            P("shard", None),
            P("shard", None),
            P("shard", None),
            P("shard", None),
            P("shard", None),
            P("shard", None),
            P("shard", None),
            P("shard", None),
            P("shard", None),
            P("shard"),
            P("shard"),
            P("shard"),
        ),
        check_vma=False,
    )
```

```python
import functools

import jax
import jax.numpy as jnp
from jax import lax
from jax.experimental import pallas as pl
from jax.experimental.pallas import tpu as pltpu
from jax.sharding import PartitionSpec as P

D = 768
HEADS = 12
HDIM = 64
FF = 3072
CIN = 512
PROJ = 256
CODES = 320
QGROUPS = 2
LAYERS = 2
STEP = 10
SMALL_ROWS = 160


beta_one = 0.9
beta_two = 0.95
beta_rotated = 0.5
adam_epsilon = 1e-08
decay_rate = 0.01
rate_matrix = 0.02
rate_target = 0.08
rate_codebook = 0.6
rate_vector = 0.3
rate_rotated = 0.08
contrastive_sharpness = 0.1
norm_epsilon = 1e-05
unit_epsilon = 1e-06

KW = 128
GROUPS = 16
GC = D // GROUPS
LANE = 64
PACK = 4
PADW = GROUPS * LANE
HALF = KW // PACK
STEPS = HALF + 1
VMEM = 56 * 1024 * 1024
SMALL_COST = pl.CostEstimate(flops=1024, bytes_accessed=1024, transcendentals=0)
CONV_COST = pl.CostEstimate(flops=35 * 10**9, bytes_accessed=10**7, transcendentals=0)
NT = (((1,), (1,)), ((), ()))
NN = (((1,), (0,)), ((), ()))


def mm(a, b, dims=NN):
    return lax.dot_general(a, b, dims, preferred_element_type=jnp.float32)


def spread_matrix(rows, out_cols, block, wide):
    i = lax.broadcasted_iota(jnp.int32, (rows, out_cols), 0)
    j = lax.broadcasted_iota(jnp.int32, (rows, out_cols), 1)
    return ((i // block) * wide + i % block == j).astype(jnp.bfloat16)


def pack_pair(x_ref, even_ref, odd_ref, rows):
    low = lax.broadcasted_iota(jnp.int32, (rows * 16, 128), 1) < LANE
    x = x_ref[...].reshape(rows, PACK, 16, 128)
    for half in range(2):
        first = x[:, 2 * half].reshape(rows * 16, 128).astype(jnp.float32)
        second = x[:, 2 * half + 1].reshape(rows * 16, 128).astype(jnp.float32)
        even_ref[:, half * 128:half * 128 + 128] = jnp.where(low, first, pltpu.roll(second, LANE, 1)).astype(jnp.bfloat16)
        odd_ref[:, half * 128:half * 128 + 128] = jnp.where(low, pltpu.roll(first, LANE, 1), second).astype(jnp.bfloat16)


def unpack_pair(even, odd, out_ref, rows):
    low = lax.broadcasted_iota(jnp.int32, (rows * 16, 128), 1) < LANE
    parts = []
    for half in range(2):
        e = even[:, half * 128:half * 128 + 128]
        o = odd[:, half * 128:half * 128 + 128]
        parts.append(jnp.where(low, e, pltpu.roll(o, LANE, 1)).reshape(rows, 1, 16, 128))
        parts.append(jnp.where(low, pltpu.roll(e, LANE, 1), o).reshape(rows, 1, 16, 128))
    out_ref[...] = jnp.concatenate(parts, axis=1).reshape(PACK * rows, 16, 128)


def widen_taps(w_ref, wide_ref, shards):
    per = KW // shards
    sel = spread_matrix(per * GC, per * LANE, GC, LANE)
    block = mm(w_ref[...].reshape(shards * 2 * GC, per * GC), sel).astype(jnp.bfloat16)
    for group in range(2):
        wide_ref[group, GC:, :] = jnp.zeros((LANE - GC, STEPS * 256), jnp.bfloat16)
        wide_ref[group, 0:GC, KW * LANE:] = jnp.zeros((GC, STEPS * 256 - KW * LANE), jnp.bfloat16)
        for s in range(shards):
            start = (2 * s + group) * GC
            wide_ref[group, 0:GC, s * per * LANE:(s + 1) * per * LANE] = block[start:start + GC]


def build_taps(wide_ref, taps_ref, group):
    wide = wide_ref[group]
    shifted = pltpu.roll(wide.astype(jnp.float32), LANE, 1).astype(jnp.bfloat16)
    total = STEPS * 256
    taps_ref[0:64, :] = wide
    taps_ref[64:128, :] = shifted
    taps_ref[128:192, 0:128] = jnp.zeros((64, 128), jnp.bfloat16)
    taps_ref[128:192, 128:total] = wide[:, 0:total - 128]
    taps_ref[192:256, 0:128] = jnp.zeros((64, 128), jnp.bfloat16)
    taps_ref[192:256, 128:total] = shifted[:, 0:total - 128]


def conv_forward_kernel(rows, shards, x_ref, w_ref, y_ref, even_ref, odd_ref, taps_ref, wide_ref):
    m = rows * 16
    pack_pair(x_ref, even_ref, odd_ref, rows + HALF)
    widen_taps(w_ref, wide_ref, shards)
    results = []
    for group, packed in enumerate((even_ref, odd_ref)):
        build_taps(wide_ref, taps_ref, group)
        left = jnp.concatenate([packed[q * 16:q * 16 + m, :] for q in range(STEPS)], axis=1)
        results.append(mm(left, taps_ref[...], NT))
    unpack_pair(results[0], results[1], y_ref, rows)


def conv_forward(x, w, first, rows, shards):
    frames = PACK * (rows + HALF)
    return pl.pallas_call(
        functools.partial(conv_forward_kernel, rows, shards),
        grid=(GROUPS // 2,),
        in_specs=[
            pl.BlockSpec((frames, 16, 128), lambda g: (0, 0, g)),
            pl.BlockSpec((shards, 2 * GC, w.shape[2]), lambda g: (0, first + g, 0)),
        ],
        out_specs=pl.BlockSpec((PACK * rows, 16, 128), lambda g: (0, 0, g)),
        out_shape=jax.ShapeDtypeStruct((PACK * rows, 16, PADW), jnp.float32),
        scratch_shapes=[pltpu.VMEM(((rows + HALF) * 16, 256), jnp.bfloat16)] * 2 + [
            pltpu.VMEM((256, STEPS * 256), jnp.bfloat16),
            pltpu.VMEM((2, LANE, STEPS * 256), jnp.bfloat16),
        ],
        cost_estimate=SMALL_COST,
        compiler_params=pltpu.CompilerParams(vmem_limit_bytes=VMEM, dimension_semantics=("arbitrary",)),
        name="conv_forward",
    )(x, w)


def conv_input_kernel(rows, shards, d_ref, w_ref, dx_ref, even_ref, odd_ref, taps_ref, wide_ref):
    m = rows * 16
    pack_pair(d_ref, even_ref, odd_ref, rows + HALF)
    widen_taps(w_ref, wide_ref, shards)
    results = []
    for group, packed in enumerate((even_ref, odd_ref)):
        build_taps(wide_ref, taps_ref, group)
        acc = jnp.zeros((m, 256), jnp.float32)
        for q in range(STEPS):
            left = packed[(HALF - q) * 16:(HALF - q) * 16 + m, :]
            acc = acc + mm(left, taps_ref[:, q * 256:q * 256 + 256])
        results.append(acc)
    unpack_pair(results[0], results[1], dx_ref, rows)


def conv_input_grad(d, w, first, rows, shards):
    frames = PACK * (rows + HALF)
    return pl.pallas_call(
        functools.partial(conv_input_kernel, rows, shards),
        grid=(GROUPS // 2,),
        in_specs=[
            pl.BlockSpec((frames, 16, 128), lambda g: (0, 0, g)),
            pl.BlockSpec((shards, 2 * GC, w.shape[2]), lambda g: (0, first + g, 0)),
        ],
        out_specs=pl.BlockSpec((PACK * rows, 16, 128), lambda g: (0, 0, g)),
        out_shape=jax.ShapeDtypeStruct((PACK * rows, 16, PADW), jnp.float32),
        scratch_shapes=[pltpu.VMEM(((rows + HALF) * 16, 256), jnp.bfloat16)] * 2 + [
            pltpu.VMEM((256, STEPS * 256), jnp.bfloat16),
            pltpu.VMEM((2, LANE, STEPS * 256), jnp.bfloat16),
        ],
        cost_estimate=CONV_COST,
        compiler_params=pltpu.CompilerParams(vmem_limit_bytes=VMEM, dimension_semantics=("arbitrary",)),
        name="conv_input_grad",
    )(d, w)


def conv_weight_kernel(rows, shards, x_ref, d_ref, dw_ref, xe_ref, xo_ref, de_ref, do_ref, prod_ref, grad_ref):
    m = rows * 16
    per = KW // shards
    width = KW * LANE
    pack_pair(x_ref, xe_ref, xo_ref, rows + HALF)
    pack_pair(d_ref, de_ref, do_ref, rows)
    for group, (x_packed, d_packed) in enumerate(((xe_ref, de_ref), (xo_ref, do_ref))):
        d_turned = d_packed[...].astype(jnp.float32).T.astype(jnp.bfloat16)
        for q in range(STEPS):
            prod_ref[:, q * 256:q * 256 + 256] = mm(d_turned, x_packed[q * 16:q * 16 + m, :])
        straight = prod_ref[0:GC, 0:width] + prod_ref[128:128 + GC, 128:128 + width]
        turned_part = prod_ref[64:64 + GC, :] + pltpu.roll(prod_ref[192:192 + GC, :], STEPS * 256 - 128, 1)
        grad = straight + pltpu.roll(turned_part, STEPS * 256 - 64, 1)[:, 0:width]
        grad = grad.astype(jnp.bfloat16)
        for s in range(shards):
            start = (2 * s + group) * GC
            grad_ref[start:start + GC, :] = grad[:, s * per * LANE:(s + 1) * per * LANE]
    sel = spread_matrix(per * GC, per * LANE, GC, LANE)
    dw_ref[...] = mm(grad_ref[...], sel, NT).astype(jnp.bfloat16).reshape(shards, 2 * GC, per * GC)


def conv_weight_grad(x, d, rows, shards):
    per = KW // shards
    first = HALF * PACK // 2
    d = d[first:first + PACK * rows]
    return pl.pallas_call(
        functools.partial(conv_weight_kernel, rows, shards),
        grid=(GROUPS // 2,),
        in_specs=[
            pl.BlockSpec((PACK * (rows + HALF), 16, 128), lambda g: (0, 0, g)),
            pl.BlockSpec((PACK * rows, 16, 128), lambda g: (0, 0, g)),
        ],
        out_specs=pl.BlockSpec((shards, 2 * GC, per * GC), lambda g: (0, g, 0)),
        out_shape=jax.ShapeDtypeStruct((shards, D, per * GC), jnp.bfloat16),
        scratch_shapes=[
            pltpu.VMEM(((rows + HALF) * 16, 256), jnp.bfloat16),
            pltpu.VMEM(((rows + HALF) * 16, 256), jnp.bfloat16),
            pltpu.VMEM((rows * 16, 256), jnp.bfloat16),
            pltpu.VMEM((rows * 16, 256), jnp.bfloat16),
            pltpu.VMEM((256, STEPS * 256), jnp.float32),
            pltpu.VMEM((shards * 2 * GC, per * LANE), jnp.bfloat16),
        ],
        cost_estimate=CONV_COST,
        compiler_params=pltpu.CompilerParams(vmem_limit_bytes=VMEM, dimension_semantics=("arbitrary",)),
        name="conv_weight_grad",
    )(x, d)


def turned_adam_kernel(rule, grad_ref, weight_ref, first_ref, second_ref, new_ref, new_first_ref, new_second_ref):
    new, first, second = rule(weight_ref[...], grad_ref[...].T, first_ref[...], second_ref[...])
    new_ref[...] = new
    new_first_ref[...] = first
    new_second_ref[...] = second


def turned_adam(rule, weight, grad, first, second):
    return tuple(
        pl.pallas_call(
            functools.partial(turned_adam_kernel, rule),
            out_shape=[jax.ShapeDtypeStruct(weight.shape, jnp.float32)] * 3,
            cost_estimate=SMALL_COST,
            compiler_params=pltpu.CompilerParams(vmem_limit_bytes=VMEM),
            name="turned_adam",
        )(grad, weight, first, second)
    )


def put_pieces(out_ref, start, block, taps):
    depth, width = block.shape[-2:]
    for at in range(0, width, taps):
        size = min(taps, width - at)
        out_ref[..., start:start + depth, 0:size] = block[..., at:at + size]
        start += depth
    return start


def pack_weights_kernel(conv_ref, *refs):
    vector_ref, out_ref, held = refs[-3:]
    taps = conv_ref.shape[0]
    out_ref[0:D, :] = conv_ref[...].T.astype(jnp.bfloat16)
    held[...] = jnp.zeros_like(held)
    start = 0
    for ref in refs[:-3]:
        start = put_pieces(held, start, ref[...], taps)
    size = vector_ref.shape[1]
    for at in range(0, size, taps):
        width = min(taps, size - at)
        held[start:start + 1, 0:width] = vector_ref[:, at:at + width]
        start += 1
    out_ref[D:, :] = held[...].astype(jnp.bfloat16)


def pack_weights(conv, blocks, vector, rows):
    taps = conv.shape[0]
    return pl.pallas_call(
        pack_weights_kernel,
        out_shape=jax.ShapeDtypeStruct((D + rows, taps), jnp.bfloat16),
        scratch_shapes=[pltpu.VMEM((rows, taps), jnp.float32)],
        cost_estimate=SMALL_COST,
        compiler_params=pltpu.CompilerParams(vmem_limit_bytes=VMEM),
        name="pack_weights",
    )(conv, *blocks, vector.reshape(1, -1))


def pack_grads_kernel(blocks, *refs):
    extra_ref, out_ref, held, flat = refs[-4:]
    shards, _, taps = out_ref.shape
    held[...] = jnp.zeros_like(held)
    start = 0
    for ref in refs[:blocks]:
        start = put_pieces(held, start, ref[...], taps)
    place = 0
    for ref in refs[blocks:-4]:
        flat[:, place:place + ref.shape[1]] = ref[...]
        place += ref.shape[1]
    size = place // shards
    for s in range(shards):
        for row, at in enumerate(range(0, size, taps)):
            width = min(taps, size - at)
            held[s, start + row:start + row + 1, 0:width] = flat[:, s * size + at:s * size + at + width]
    start += -(-size // taps)
    held[:, start:start + 1, 0:128] = jnp.broadcast_to(extra_ref[...][None], (shards, 1, 128))
    out_ref[...] = held[...].astype(jnp.bfloat16)


def pack_grads(blocks, vectors, extra, shards, rows, taps):
    blocks = [block.reshape(shards, -1, block.shape[-1]) for block in blocks]
    vectors = [v.reshape(1, -1) for v in vectors]
    total = sum(v.shape[1] for v in vectors)
    return pl.pallas_call(
        functools.partial(pack_grads_kernel, len(blocks)),
        out_shape=jax.ShapeDtypeStruct((shards, rows, taps), jnp.bfloat16),
        scratch_shapes=[pltpu.VMEM((shards, rows, taps), jnp.float32), pltpu.VMEM((1, total), jnp.float32)],
        cost_estimate=SMALL_COST,
        compiler_params=pltpu.CompilerParams(vmem_limit_bytes=VMEM),
        name="pack_grads",
    )(*blocks, *vectors, extra)


def to_strips(padded, frame_count):
    clips = padded.shape[0]
    strips = 16 // clips
    length = frame_count // strips
    sel = spread_matrix(D, PADW, GC, LANE)
    wide = mm(padded.reshape(-1, D), sel).astype(jnp.bfloat16).reshape(clips, -1, PADW)
    parts = jnp.stack([wide[:, s * length:s * length + length + KW] for s in range(strips)], 1)
    return parts.reshape(16, length + KW, PADW).transpose(1, 0, 2)


def from_strips(y, clips):
    rows = y.transpose(1, 0, 2).reshape(-1, PADW)
    high = lax.reduce_precision(rows, 8, 7)
    rest = (rows - high).astype(jnp.bfloat16)
    high = high.astype(jnp.bfloat16)
    sel = spread_matrix(D, PADW, GC, LANE)
    return mm(high, sel, NT) + mm(rest, sel, NT)


SCALE = HDIM ** (-0.5)


def turned(block):
    return block.astype(jnp.float32).T.astype(jnp.bfloat16)


def attend_kernel(blocks, q_ref, *refs):
    keys = [refs[2 * j] for j in range(blocks)]
    values = [refs[2 * j + 1] for j in range(blocks)]
    mixed_ref, stat_ref = refs[2 * blocks:]
    frames = q_ref.shape[0]
    low = lax.broadcasted_iota(jnp.int32, (frames, 128), 1) < HDIM
    scaled = q_ref[...] * jnp.bfloat16(SCALE)
    none = jnp.zeros_like(scaled)
    turned_keys = [turned(k[...]) for k in keys]
    parts = []
    stats = []
    for head in range(2):
        query = jnp.where(low, scaled, none) if head == 0 else jnp.where(low, none, scaled)
        scores = [mm(query, k) for k in turned_keys]
        largest = functools.reduce(jnp.maximum, [jnp.max(s, 1, keepdims=True) for s in scores])
        powers = [jnp.exp(s - largest) for s in scores]
        total = functools.reduce(jnp.add, [jnp.sum(p, 1, keepdims=True) for p in powers])
        out = functools.reduce(jnp.add, [mm(p.astype(jnp.bfloat16), v[...]) for p, v in zip(powers, values)])
        parts.append(out * (1.0 / total))
        stats.append(jnp.broadcast_to(largest + jnp.log(total), (frames, 128)))
    mixed_ref[...] = jnp.where(low, parts[0], parts[1]).astype(jnp.bfloat16)
    rows = jnp.where(low, stats[0], stats[1]).T
    stat_ref[0, 0, 0:1, :] = rows[0:1, :]
    stat_ref[0, 0, 1:2, :] = rows[HDIM:HDIM + 1, :]


def head_spec(item, frames):
    if isinstance(item, tuple):
        return pl.BlockSpec((None, frames, 128), lambda c, h: (item[1], c, h))
    return pl.BlockSpec((frames, 128), lambda c, h: (c, h))


def head_array(item):
    return item[0] if isinstance(item, tuple) else item


def attend(query, keys, values, clips):
    blocks = len(keys)
    rows = head_array(query).shape[-2]
    frames = rows // clips
    spec = pl.BlockSpec((frames, 128), lambda c, h: (c, h))
    operands = [query]
    for k, v in zip(keys, values):
        operands += [k, v]
    return pl.pallas_call(
        functools.partial(attend_kernel, blocks),
        grid=(clips, HEADS // 2),
        in_specs=[head_spec(item, frames) for item in operands],
        out_specs=[spec, pl.BlockSpec((1, 1, 2, frames), lambda c, h: (c, h, 0, 0))],
        out_shape=[
            jax.ShapeDtypeStruct((rows, D), jnp.bfloat16),
            jax.ShapeDtypeStruct((clips, HEADS // 2, 2, frames), jnp.float32),
        ],
        cost_estimate=SMALL_COST,
        compiler_params=pltpu.CompilerParams(vmem_limit_bytes=VMEM, dimension_semantics=("arbitrary", "arbitrary")),
        name="attend",
    )(*[head_array(item) for item in operands])


def attend_back_kernel(blocks, q_ref, d_ref, stat_ref, *refs):
    keys = [refs[2 * j] for j in range(blocks)]
    values = [refs[2 * j + 1] for j in range(blocks)]
    dq_ref = refs[2 * blocks]
    dk = [refs[2 * blocks + 1 + 2 * j] for j in range(blocks)]
    dv = [refs[2 * blocks + 2 + 2 * j] for j in range(blocks)]
    frames = q_ref.shape[0]
    low = lax.broadcasted_iota(jnp.int32, (frames, 128), 1) < HDIM
    scaled = q_ref[...] * jnp.bfloat16(SCALE)
    grad = d_ref[...]
    none = jnp.zeros_like(scaled)
    q_turned = turned(scaled)
    d_turned = turned(grad)
    gap = jnp.zeros((HDIM, frames), jnp.bfloat16)
    k_turned = [turned(k[...]) for k in keys]
    dq_rows = []
    dk_sum = [None] * blocks
    dv_sum = [None] * blocks
    for head in range(2):
        pick = slice(head * HDIM, head * HDIM + HDIM)
        if head == 0:
            query, grad_head = jnp.where(low, scaled, none), jnp.where(low, grad, none)
            q_side = jnp.concatenate([q_turned[pick], gap], 0)
            d_side = jnp.concatenate([d_turned[pick], gap], 0)
        else:
            query, grad_head = jnp.where(low, none, scaled), jnp.where(low, none, grad)
            q_side = jnp.concatenate([gap, q_turned[pick]], 0)
            d_side = jnp.concatenate([gap, d_turned[pick]], 0)
        stat = stat_ref[0, 0, head:head + 1, :]
        probs = [jnp.exp(mm(k[...], q_side) - stat) for k in keys]
        weighted = [p * mm(v[...], d_side) for p, v in zip(probs, values)]
        delta = functools.reduce(jnp.add, [jnp.sum(w, 0, keepdims=True) for w in weighted])
        dq = None
        for j in range(blocks):
            ds = (weighted[j] - probs[j] * delta).astype(jnp.bfloat16)
            grad_v = mm(probs[j].astype(jnp.bfloat16), grad_head)
            grad_k = mm(ds, query)
            part = mm(k_turned[j][pick], ds)
            dq = part if dq is None else dq + part
            dv_sum[j] = grad_v if dv_sum[j] is None else dv_sum[j] + grad_v
            dk_sum[j] = grad_k if dk_sum[j] is None else dk_sum[j] + grad_k
        dq_rows.append(dq)
    dq_ref[...] = (jnp.concatenate(dq_rows, 0) * SCALE).T.astype(jnp.bfloat16)
    for j in range(blocks):
        dk[j][...] = dk_sum[j].astype(jnp.bfloat16)
        dv[j][...] = dv_sum[j].astype(jnp.bfloat16)


def attend_back(query, grad, stat, keys, values, clips):
    blocks = len(keys)
    rows = grad.shape[0]
    frames = rows // clips
    spec = pl.BlockSpec((frames, 128), lambda c, h: (c, h))
    operands = []
    for k, v in zip(keys, values):
        operands += [k, v]
    shape = jax.ShapeDtypeStruct((rows, D), jnp.bfloat16)
    return pl.pallas_call(
        functools.partial(attend_back_kernel, blocks),
        grid=(clips, HEADS // 2),
        in_specs=[head_spec(query, frames), spec, pl.BlockSpec((1, 1, 2, frames), lambda c, h: (c, h, 0, 0))]
        + [head_spec(item, frames) for item in operands],
        out_specs=[spec] * (1 + 2 * blocks),
        out_shape=[shape] * (1 + 2 * blocks),
        cost_estimate=SMALL_COST,
        compiler_params=pltpu.CompilerParams(vmem_limit_bytes=VMEM, dimension_semantics=("arbitrary", "arbitrary")),
        name="attend_back",
    )(head_array(query), grad, stat, *[head_array(item) for item in operands])


def count_kernel(draws, n_ref, out_ref):
    length, frames = out_ref.shape[1:]
    place = lax.broadcasted_iota(jnp.int32, (length // 8, 8, frames), 0) * 8 + lax.broadcasted_iota(
        jnp.int32, (length // 8, 8, frames), 1)
    total = jnp.zeros((length // 8, 8, frames), jnp.float32)
    for n in range(draws):
        row = n_ref[0, n:n + 1, :]
        total = total + jnp.where(place == row[None], 1.0, 0.0)
    out_ref[0] = total.reshape(length, frames).astype(jnp.bfloat16)


def count_draws(negatives, length):
    clips, draws, frames = negatives.shape
    tile = 128 if frames % 128 == 0 else frames
    return pl.pallas_call(
        functools.partial(count_kernel, draws),
        grid=(clips, frames // tile),
        in_specs=[pl.BlockSpec((1, draws, tile), lambda c, f: (c, 0, f))],
        out_specs=pl.BlockSpec((1, length, tile), lambda c, f: (c, 0, f)),
        out_shape=jax.ShapeDtypeStruct((clips, length, frames), jnp.bfloat16),
        cost_estimate=SMALL_COST,
        compiler_params=pltpu.CompilerParams(vmem_limit_bytes=VMEM, dimension_semantics=("arbitrary", "arbitrary")),
        name="count_draws",
    )(negatives)


def square(ref):
    return ref[...].reshape(D, D)


def project_kernel(x_ref, w_ref, b_ref, out_ref):
    out_ref[0] = (mm(x_ref[...], square(w_ref)) + b_ref[0]).astype(jnp.bfloat16)


def project(entry, whole, first, biases):
    count = len(biases)
    rows = entry.shape[0]
    shards, _, _ = whole.shape
    depth = D // shards
    return pl.pallas_call(
        project_kernel,
        grid=(count,),
        in_specs=[
            pl.BlockSpec((rows, D), lambda i: (0, 0)),
            pl.BlockSpec((shards, depth, D), lambda i: (0, first + i, 0)),
            pl.BlockSpec((1, 1, D), lambda i: (i, 0, 0)),
        ],
        out_specs=pl.BlockSpec((1, rows, D), lambda i: (i, 0, 0)),
        out_shape=jax.ShapeDtypeStruct((count, rows, D), jnp.bfloat16),
        cost_estimate=SMALL_COST,
        compiler_params=pltpu.CompilerParams(vmem_limit_bytes=VMEM, dimension_semantics=("arbitrary",)),
        name="project",
    )(entry, whole, jnp.stack(biases).reshape(count, 1, D))


def norm_rows(values, gain_row, bias_row):
    centred = values - jnp.mean(values, -1, keepdims=True)
    scale = lax.rsqrt(jnp.mean(centred * centred, -1, keepdims=True) + norm_epsilon)
    level = centred * scale
    return level * gain_row + bias_row, level, scale


def norm_rows_back(grad, level, scale, gain_row):
    inside = grad * gain_row
    centred = inside - jnp.mean(inside, -1, keepdims=True) - level * jnp.mean(inside * level, -1, keepdims=True)
    return scale * centred


def gelu_parts(values):
    half = 0.5 * (1.0 + lax.erf(values * 0.5**0.5))
    density = jnp.exp(-0.5 * values * values) * (2.0 * jnp.pi) ** -0.5
    return values * half, half + values * density


def feed_kernel(
    hidden_ref, mixed_ref, wo_ref, e_ref, s_ref, ob_ref, g1_ref, b1_ref, eb_ref, sb_ref, g2_ref, b2_ref,
    low_ref, level1_ref, scale1_ref, active_ref, slope_ref, result_ref, result_low_ref, level2_ref, scale2_ref,
    middle_ref, total_ref,
):
    step = pl.program_id(0)

    @pl.when(step == 0)
    def _():
        branch = mm(mixed_ref[...], square(wo_ref)) + ob_ref[...]
        middle, level, scale = norm_rows(hidden_ref[...] + branch, g1_ref[...], b1_ref[...])
        middle_ref[...] = middle
        low_ref[...] = middle.astype(jnp.bfloat16)
        level1_ref[...] = level
        scale1_ref[...] = scale
        total_ref[...] = jnp.zeros_like(total_ref)

    inner = mm(low_ref[...], square(e_ref)) + eb_ref[...]
    active, slope = gelu_parts(inner)
    active = active.astype(jnp.bfloat16)
    active_ref[...] = active
    slope_ref[...] = slope.astype(jnp.bfloat16)
    total_ref[...] += mm(active, square(s_ref))

    @pl.when(step == pl.num_programs(0) - 1)
    def _():
        result, level, scale = norm_rows(middle_ref[...] + (total_ref[...] + sb_ref[...]), g2_ref[...], b2_ref[...])
        result_ref[...] = result
        result_low_ref[...] = result.astype(jnp.bfloat16)
        level2_ref[...] = level
        scale2_ref[...] = scale


def feed_forward(hidden, mixed, attn_whole, feed_whole, first, place, vectors):
    rows = hidden.shape[0]
    shards = attn_whole.shape[0]
    depth = D // shards
    parts = FF // D
    row = pl.BlockSpec((1, D), lambda j: (0, 0))
    flat = pl.BlockSpec((rows, D), lambda j: (0, 0))
    column = pl.BlockSpec((rows, 1), lambda j: (0, 0))
    tile = pl.BlockSpec((rows, D), lambda j: (0, j))
    o_bias, gain_one, bias_one, expand_bias, shrink_bias, gain_two, bias_two = [v.reshape(1, -1) for v in vectors]

    def shape(width, dtype):
        return jax.ShapeDtypeStruct((rows, width), dtype)

    return pl.pallas_call(
        feed_kernel,
        grid=(parts,),
        in_specs=[
            flat,
            flat,
            pl.BlockSpec((shards, depth, D), lambda j: (0, place + 3, 0)),
            pl.BlockSpec((shards, depth, D), lambda j: (0, first + j, 0)),
            pl.BlockSpec((shards // parts, parts * depth, D), lambda j: (j, first // parts + 1, 0)),
            row, row, row,
            pl.BlockSpec((1, D), lambda j: (0, j)),
            row, row, row,
        ],
        out_specs=[flat, flat, column, tile, tile, flat, flat, flat, column],
        out_shape=[
            shape(D, jnp.bfloat16), shape(D, jnp.float32), shape(1, jnp.float32),
            shape(FF, jnp.bfloat16), shape(FF, jnp.bfloat16),
            shape(D, jnp.float32), shape(D, jnp.bfloat16), shape(D, jnp.float32), shape(1, jnp.float32),
        ],
        scratch_shapes=[pltpu.VMEM((rows, D), jnp.float32)] * 2,
        cost_estimate=SMALL_COST,
        compiler_params=pltpu.CompilerParams(vmem_limit_bytes=VMEM, dimension_semantics=("arbitrary",)),
        name="feed_forward",
    )(hidden, mixed, attn_whole, feed_whole, feed_whole, o_bias, gain_one, bias_one, expand_bias, shrink_bias, gain_two, bias_two)


def row_sum(values):
    return jnp.sum(values, 0, keepdims=True)


def feed_back_kernel(arrivals, base, *refs):
    if base:
        refs = refs[1:]
    grad_ref = refs[0]
    extra = refs[1 : 1 + arrivals]
    (
        level2_ref, scale2_ref, g2_ref, slope_ref, active_ref, low_ref, e_ref, s_ref, level1_ref, scale1_ref, g1_ref, wo_ref,
        sum_ref, branch_ref, mixed_ref, vec_ref, eb_ref, chunk_ref,
        outer_ref, turned_ref, total_ref, e_slot, s_slot, e_sem, s_sem,
    ) = refs[1 + arrivals :]
    step = pl.program_id(0)
    last = pl.num_programs(0) - 1
    slot = lax.rem(step, 2)
    shards, depth = e_slot.shape[1:3]
    group = s_slot.shape[1]

    @pl.when(step == 0)
    def _():
        grad = grad_ref[...]
        for ref in extra:
            grad = grad + ref[...].astype(jnp.float32)
        level = level2_ref[...]
        total = norm_rows_back(grad, level, scale2_ref[...], g2_ref[...])
        outer = total.astype(jnp.bfloat16)
        outer_ref[...] = outer
        total_ref[...] = total
        vec_ref[3:4, :] = row_sum(outer.astype(jnp.float32))
        vec_ref[4:5, :] = row_sum(grad * level)
        vec_ref[5:6, :] = row_sum(grad)
        turned_ref[...] = turned(low_ref[...])

    def copies(at, index):
        e_copy = pltpu.make_async_copy(
            e_slot.at[at], chunk_ref.at[:, pl.ds(base + index * depth, depth), :], e_sem.at[at]
        )
        s_copy = pltpu.make_async_copy(
            s_slot.at[at],
            chunk_ref.at[pl.ds(index * group, group), pl.ds(base + (last + 1) * depth, (last + 1) * depth), :],
            s_sem.at[at],
        )
        return e_copy, s_copy

    @pl.when(step >= 2)
    def _():
        for copy in copies(slot, step - 2):
            copy.wait()

    outer = outer_ref[...]
    inner = (mm(outer, square(s_ref), NT) * slope_ref[...].astype(jnp.float32)).astype(jnp.bfloat16)
    eb_ref[...] = row_sum(inner.astype(jnp.float32))
    total_ref[...] += mm(inner, square(e_ref), NT)
    e_slot[slot] = mm(turned_ref[...], inner).astype(jnp.bfloat16).reshape(shards, depth, D)
    s_slot[slot] = mm(turned(active_ref[...]), outer).astype(jnp.bfloat16).reshape(group, (last + 1) * depth, D)
    for copy in copies(slot, step):
        copy.start()

    @pl.when(step == last)
    def _():
        grad = total_ref[...]
        level = level1_ref[...]
        total = norm_rows_back(grad, level, scale1_ref[...], g1_ref[...])
        branch = total.astype(jnp.bfloat16)
        sum_ref[...] = total
        branch_ref[...] = branch
        vec_ref[0:1, :] = row_sum(branch.astype(jnp.float32))
        vec_ref[1:2, :] = row_sum(grad * level)
        vec_ref[2:3, :] = row_sum(grad)
        vec_ref[6:8, :] = jnp.zeros((2, D), jnp.float32)
        mixed_ref[...] = mm(branch, square(wo_ref), NT).astype(jnp.bfloat16)
        for index in (last - 1, last):
            for copy in copies(lax.rem(index, 2), index):
                copy.wait()


def feed_back(grads, cache, attn_whole, feed_whole, first, place, gain_one, gain_two, chunks):
    level1, scale1, low, slope, active, level2, scale2 = cache
    rows = low.shape[0]
    shards = attn_whole.shape[0]
    depth = D // shards
    parts = FF // D
    flat = pl.BlockSpec((rows, D), lambda j: (0, 0))
    row = pl.BlockSpec((1, D), lambda j: (0, 0))
    column = pl.BlockSpec((rows, 1), lambda j: (0, 0))
    tile = pl.BlockSpec((rows, D), lambda j: (0, j))
    return pl.pallas_call(
        functools.partial(feed_back_kernel, len(grads) - 1, 0 if chunks is None else 4 * depth),
        grid=(parts,),
        in_specs=[pl.BlockSpec(memory_space=pl.ANY)] * (chunks is not None)
        + [flat] * len(grads)
        + [
            flat, column, row, tile, tile, flat,
            pl.BlockSpec((shards, depth, D), lambda j: (0, first + j, 0)),
            pl.BlockSpec((shards // parts, parts * depth, D), lambda j: (j, first // parts + 1, 0)),
            flat, column, row,
            pl.BlockSpec((shards, depth, D), lambda j: (0, place + 3, 0)),
        ],
        out_specs=[
            flat, flat, flat,
            pl.BlockSpec((8, D), lambda j: (0, 0)),
            pl.BlockSpec((1, D), lambda j: (0, j)),
            pl.BlockSpec(memory_space=pl.ANY),
        ],
        out_shape=[
            jax.ShapeDtypeStruct((rows, D), jnp.float32),
            jax.ShapeDtypeStruct((rows, D), jnp.bfloat16),
            jax.ShapeDtypeStruct((rows, D), jnp.bfloat16),
            jax.ShapeDtypeStruct((8, D), jnp.float32),
            jax.ShapeDtypeStruct((1, FF), jnp.float32),
            jax.ShapeDtypeStruct((shards, (4 * (chunks is not None) + 2 * parts) * depth, D), jnp.bfloat16),
        ],
        input_output_aliases={} if chunks is None else {0: 5},
        scratch_shapes=[
            pltpu.VMEM((rows, D), jnp.bfloat16),
            pltpu.VMEM((D, rows), jnp.bfloat16),
            pltpu.VMEM((rows, D), jnp.float32),
            pltpu.VMEM((2, shards, depth, D), jnp.bfloat16),
            pltpu.VMEM((2, shards // parts, parts * depth, D), jnp.bfloat16),
            pltpu.SemaphoreType.DMA((2,)),
            pltpu.SemaphoreType.DMA((2,)),
        ],
        cost_estimate=SMALL_COST,
        compiler_params=pltpu.CompilerParams(vmem_limit_bytes=VMEM, dimension_semantics=("arbitrary",)),
        name="feed_back",
    )(
        *([] if chunks is None else [chunks]), *grads, level2, scale2, gain_two.reshape(1, D), slope, active, low, feed_whole, feed_whole,
        level1, scale1, gain_one.reshape(1, D), attn_whole,
    )


def entry_back_kernel(blocks, sum_ref, dq_ref, *refs):
    keys, values = refs[0 : 2 * blocks : 2], refs[1 : 2 * blocks : 2]
    wq_ref, wk_ref, wv_ref = refs[2 * blocks : 2 * blocks + 3]
    outs = refs[2 * blocks + 3 :]
    key_w, value_w = square(wk_ref), square(wv_ref)
    for j in range(blocks):
        back = mm(keys[j][...], key_w, NT) + mm(values[j][...], value_w, NT)
        if j == 0:
            outs[0][...] = sum_ref[...] + mm(dq_ref[...], square(wq_ref), NT) + back
        else:
            outs[j][...] = back.astype(jnp.bfloat16)


def entry_back(grad_sum, dq, pairs, attn_whole, place):
    rows = dq.shape[0]
    shards = attn_whole.shape[0]
    flat = pl.BlockSpec((rows, D), lambda i: (0, 0))
    weights = [pl.BlockSpec((shards, D // shards, D), lambda i, m=m: (0, place + m, 0)) for m in range(3)]
    return pl.pallas_call(
        functools.partial(entry_back_kernel, len(pairs) // 2),
        grid=(1,),
        in_specs=[flat] * (2 + len(pairs)) + weights,
        out_specs=[flat] * (len(pairs) // 2),
        out_shape=[
            jax.ShapeDtypeStruct((rows, D), jnp.float32 if j == 0 else jnp.bfloat16) for j in range(len(pairs) // 2)
        ],
        cost_estimate=SMALL_COST,
        compiler_params=pltpu.CompilerParams(vmem_limit_bytes=VMEM, dimension_semantics=("arbitrary",)),
        name="entry_back",
    )(grad_sum, dq, *pairs, attn_whole, attn_whole, attn_whole)


def attn_grads_kernel(blocks, *refs):
    entries = refs[:blocks]
    dq_ref, mixed_ref, branch_ref = refs[blocks : blocks + 3]
    pairs = refs[blocks + 3 : 3 * blocks + 3]
    out_ref, vec_ref, slots, sem = refs[3 * blocks + 3 :]
    shards, depth = slots.shape[1:3]
    entry_turned = [turned(e[...]) for e in entries]

    def put(i, value):
        slots[i] = value.astype(jnp.bfloat16).reshape(shards, depth, D)
        pltpu.make_async_copy(slots.at[i], out_ref.at[:, pl.ds(i * depth, depth), :], sem.at[i]).start()

    put(0, mm(entry_turned[0], dq_ref[...]))
    put(1, functools.reduce(jnp.add, [mm(e, k[...]) for e, k in zip(entry_turned, pairs[0::2])]))
    put(2, functools.reduce(jnp.add, [mm(e, v[...]) for e, v in zip(entry_turned, pairs[1::2])]))
    put(3, mm(turned(mixed_ref[...]), branch_ref[...]))
    vec_ref[0:1, :] = row_sum(dq_ref[...].astype(jnp.float32))
    vec_ref[1:2, :] = functools.reduce(jnp.add, [row_sum(v[...].astype(jnp.float32)) for v in pairs[1::2]])
    vec_ref[2:8, :] = jnp.zeros((6, D), jnp.float32)
    for i in range(4):
        pltpu.make_async_copy(slots.at[i], out_ref.at[:, pl.ds(i * depth, depth), :], sem.at[i]).wait()


def attn_grads(entries, dq, mixed, branch, pairs, shards, room):
    blocks = len(entries)
    rows = dq.shape[0]
    flat = pl.BlockSpec((rows, D), lambda i: (0, 0))
    operands = list(entries) + [dq, mixed, branch] + list(pairs)
    return pl.pallas_call(
        functools.partial(attn_grads_kernel, blocks),
        grid=(1,),
        in_specs=[flat] * len(operands),
        out_specs=[pl.BlockSpec(memory_space=pl.ANY), pl.BlockSpec((8, D), lambda i: (0, 0))],
        out_shape=[
            jax.ShapeDtypeStruct((shards, room, D), jnp.bfloat16),
            jax.ShapeDtypeStruct((8, D), jnp.float32),
        ],
        scratch_shapes=[
            pltpu.VMEM((4, shards, D // shards, D), jnp.bfloat16),
            pltpu.SemaphoreType.DMA((4,)),
        ],
        cost_estimate=SMALL_COST,
        compiler_params=pltpu.CompilerParams(vmem_limit_bytes=VMEM, dimension_semantics=("arbitrary",)),
        name="attn_grads",
    )(*operands)


MESH = pl.DeviceIdType.MESH
AHEAD = 3
OTHER = 2


def reduce_kernel(count, seqs, sizes, trades, *refs):
    number = len(sizes)
    if trades:
        give_ref, take_ref = refs[number], refs[2 * number + 1]
        refs = refs[:number] + refs[number + 1 : 2 * number + 1] + refs[2 * number + 2 :]
    sources = refs[:number]
    outs = refs[number : 2 * number]
    bits = count.bit_length() - 1
    turns = seqs.bit_length() - 1
    levels = bits + turns
    held = refs[2 * number : 2 * number + levels]
    send_sem, recv_sem, give_sem, take_sem = refs[2 * number + levels :]
    me = lax.axis_index("shard")
    place = lax.axis_index("seq")

    def across(index, bit):
        return index + (1 - 2 * ((index // 2**bit) % 2)) * 2**bit

    partners = [{"shard": across(me, b)} for b in range(bits)] + [{"seq": across(place, t)} for t in range(turns)]
    others = [{"shard": lax.rem(me + k, count)} for k in range(1, count)]
    greeted = others + partners[bits:] if trades else partners
    barrier = pltpu.get_barrier_semaphore()
    for partner in greeted:
        pl.semaphore_signal(barrier, inc=1, device_id=partner, device_id_type=MESH)
    pl.semaphore_wait(barrier, len(greeted))

    pieces = []
    offset = 0
    for source, out, (rows, cut) in zip(sources, outs, sizes):
        for start in range(0, rows, cut):
            pieces.append((source, out, start, offset + start, cut))
        offset += rows
    orders = [list(range(bits)), list(range(bits))]
    if bits > 2:
        orders[1] = [0] + list(range(2, bits)) + [1]
    flights = {}

    def moves(piece, level):
        order = orders[1 if piece % 5 == OTHER else 0]
        if level >= bits:
            return [(0, 0)], partners[level]
        bit = order[level]
        left = sorted(order[level:])
        low = 2 ** left.index(bit)
        side = (me // 2**bit) % 2
        pairs = []
        for j in range(2 ** (bits - level - 1)):
            base = (j // low) * 2 * low + j % low
            pairs.append((base + side * low, base + (1 - side) * low))
        return pairs, partners[bit]

    def data(piece, level, index):
        source, _, start, spot, cut = pieces[piece]
        if level == 0:
            return source.at[index, pl.ds(start, cut)]
        return held[level - 1].at[index, pl.ds(spot, cut)]

    def launch(piece, level):
        pairs, partner = moves(piece, level)
        _, _, _, spot, cut = pieces[piece]
        copies = []
        for j, (_, sent) in enumerate(pairs):
            copies.append(
                pltpu.make_async_remote_copy(
                    src_ref=data(piece, level, sent),
                    dst_ref=held[level].at[j, pl.ds(spot, cut)],
                    send_sem=send_sem.at[piece, level, j],
                    recv_sem=recv_sem.at[piece, level, j],
                    device_id=partner,
                    device_id_type=MESH,
                )
            )
        for copy in copies:
            copy.start()
        flights[piece, level] = copies

    def absorb(piece, level):
        pairs, _ = moves(piece, level)
        _, out, start, spot, cut = pieces[piece]
        for j, (kept, _) in enumerate(pairs):
            flights[piece, level][j].wait()
            mine, other = data(piece, level, kept)[...], held[level][j, pl.ds(spot, cut)]
            if level == levels - 1:
                out[pl.ds(start, cut)] = mine.astype(jnp.float32) + other.astype(jnp.float32)
            else:
                held[level][j, pl.ds(spot, cut)] = mine + other

    swaps = []
    if trades:
        for k in range(1, count):
            target = lax.rem(me + k, count)
            swaps.append(
                pltpu.make_async_remote_copy(
                    src_ref=give_ref.at[target],
                    dst_ref=take_ref.at[me],
                    send_sem=give_sem.at[k],
                    recv_sem=take_sem.at[k],
                    device_id={"shard": target},
                    device_id_type=MESH,
                )
            )
        own = pltpu.make_async_copy(give_ref.at[me], take_ref.at[me], give_sem.at[0])
        own.start()
        for swap in swaps:
            swap.start()
    delay = [0, 1] + [1 + AHEAD * level for level in range(1, levels)]
    for wave in range(len(pieces) + delay[-1]):
        for level in range(levels, -1, -1):
            piece = wave - delay[level]
            if 0 <= piece < len(pieces):
                if level > 0:
                    absorb(piece, level - 1)
                if level < levels:
                    launch(piece, level)
    if trades:
        own.wait()
        for swap in swaps:
            swap.wait()


def reduce_chunks(mesh_sizes, cuts, chunks, give):
    count, seqs = mesh_sizes
    bits, turns = count.bit_length() - 1, seqs.bit_length() - 1
    lanes = chunks[0].shape[2]
    sizes = [(c.shape[1], cut) for c, cut in zip(chunks, cuts)]
    total = sum(rows for rows, _ in sizes)
    number = sum(rows // cut for rows, cut in sizes)
    slots = [2 ** (bits - 1 - level) for level in range(bits)] + [1] * turns
    spec = pl.BlockSpec(memory_space=pltpu.VMEM)
    return pl.pallas_call(
        functools.partial(reduce_kernel, count, seqs, sizes, True),
        in_specs=[spec] * (len(chunks) + 1),
        out_specs=[spec] * (len(chunks) + 1),
        out_shape=[jax.ShapeDtypeStruct(c.shape[1:], jnp.float32) for c in chunks]
        + [jax.ShapeDtypeStruct(give.shape, give.dtype)],
        scratch_shapes=[pltpu.VMEM((n, total, lanes), jnp.bfloat16) for n in slots]
        + [pltpu.SemaphoreType.DMA((number, bits + turns, count // 2))] * 2
        + [pltpu.SemaphoreType.DMA((count,))] * 2,
        cost_estimate=SMALL_COST,
        compiler_params=pltpu.CompilerParams(collective_id=0, has_side_effects=True, vmem_limit_bytes=VMEM),
        name="reduce_chunks",
    )(*chunks, give)


def swap_moves(count, step):
    return [(i, (i - step) % count) for i in range(count)]


def gather_ring(block):
    count = lax.axis_size("seq")
    return [block] + [lax.ppermute(block, "seq", swap_moves(count, step)) for step in range(1, count)]


def return_ring(blocks):
    count = lax.axis_size("seq")
    return [lax.ppermute(block, "seq", swap_moves(count, -step)) for step, block in enumerate(blocks) if step > 0]


def seq_sum(values):
    if lax.axis_size("seq") > 2:
        return lax.psum(values, "seq").astype(jnp.float32)
    other = lax.ppermute(values, "seq", [(0, 1), (1, 0)])
    return values.astype(jnp.float32) + other.astype(jnp.float32)


def lowered(values):
    return values.astype(jnp.bfloat16)


def bdot(left_side, right_side):
    return jnp.dot(left_side, right_side, preferred_element_type=jnp.float32)


def turned_dot(left_side, right_side):
    return lax.dot_general(left_side, right_side, NT, preferred_element_type=jnp.float32)


def rows_dot(left_side, right_side):
    return lax.dot_general(left_side, right_side, (((0,), (0,)), ((), ())), preferred_element_type=jnp.float32)


def fdot(left_side, right_side):
    return jnp.dot(left_side, right_side, precision=lax.Precision.HIGHEST, preferred_element_type=jnp.float32)


def column_sum(values):
    return jnp.sum(values.astype(jnp.float32), 0, keepdims=True)


def norm_forward(values, gain_row, bias_row):
    centred = values - jnp.mean(values, -1, keepdims=True)
    spread = jnp.mean(centred * centred, -1, keepdims=True)
    scale = lax.rsqrt(spread + norm_epsilon)
    level = centred * scale
    return level * gain_row + bias_row, (level, scale, gain_row)


def norm_vectors(grad, kept):
    level = kept[0]
    return jnp.sum(grad * level, 0, keepdims=True), jnp.sum(grad, 0, keepdims=True)


def norm_backward(grad, kept):
    level, scale, gain_row = kept
    inside = grad * gain_row
    centred = inside - jnp.mean(inside, -1, keepdims=True) - level * jnp.mean(inside * level, -1, keepdims=True)
    return (scale * centred,) + norm_vectors(grad, kept)


def unit_rows(values):
    return values * lax.rsqrt(jnp.sum(values * values, -1, keepdims=True) + unit_epsilon)


def vector_pieces(vector):
    widths = [CIN, CIN, D, D, D, D, D] + [D, D, D, D, D, FF, D, D, D] * LAYERS + [PROJ, PROJ]
    pieces = []
    offset = 0
    for width in widths:
        pieces.append(vector[offset : offset + width])
        offset = offset + width
    return pieces


def with_halo(block, width):
    count = lax.axis_size("seq")
    forward = [(i, i + 1) for i in range(count - 1)]
    backward = [(i + 1, i) for i in range(count - 1)]
    low = lax.ppermute(block[:, block.shape[1] - width :], "seq", forward)
    high = lax.ppermute(block[:, :width], "seq", backward)
    return jnp.concatenate([low, block, high], axis=1)


def layer_forward(hidden, hidden_low, weights, pieces, clip_count, waiting):
    attn_w, expand_w, shrink_w = weights
    q_bias, v_bias, o_bias, gain_one, bias_one, expand_bias, shrink_bias, gain_two, bias_two = pieces
    entries = gather_ring(hidden_low)
    query = lowered(bdot(entries[0], attn_w[:, :D]) + q_bias)
    keys = [lowered(bdot(entry, attn_w[:, D : 2 * D])) for entry in entries]
    values = [lowered(bdot(entry, attn_w[:, 2 * D : 3 * D]) + v_bias) for entry in entries]
    mixed, stat = attend(query, keys, values, clip_count)
    if waiting is not None:
        mixed, waiting = fence(mixed, waiting)
    branch = bdot(mixed, attn_w[:, 3 * D :]) + o_bias
    middle, middle_kept = norm_forward(hidden + branch, gain_one, bias_one)
    middle_low = lowered(middle)
    inner = bdot(middle_low, expand_w) + expand_bias
    activated, slope = gelu_parts(inner)
    active_low = lowered(activated)
    slope_low = lowered(slope)
    outer = bdot(active_low, shrink_w) + shrink_bias
    result, final_kept = norm_forward(middle + outer, gain_two, bias_two)
    cache = (entries, query, keys, values, mixed, stat, middle_kept, middle_low, slope_low, active_low, final_kept)
    return result, lowered(result), cache, waiting


def feed_backward(grad_out, cache, expand_w, shrink_w):
    middle_low, slope_low, active_low, final_kept = cache[7:]
    grad_sum, grad_gain, grad_bias = norm_backward(grad_out, final_kept)
    grad_outer = lowered(grad_sum)
    grad_shrink = lowered(rows_dot(active_low, grad_outer))
    grad_inner = lowered(slope_low.astype(jnp.float32) * turned_dot(grad_outer, shrink_w))
    grad_expand = lowered(rows_dot(middle_low, grad_inner))
    grad_middle = grad_sum + turned_dot(grad_inner, expand_w)
    vectors = [column_sum(grad_inner), column_sum(grad_outer), grad_gain, grad_bias]
    return grad_middle, grad_expand, grad_shrink, vectors


def attend_backward(grad_middle, cache, attn_w, clip_count, *waiting):
    entries, query, keys, values, mixed, stat, middle_kept = cache[:7]
    grad_sum, grad_gain, grad_bias = norm_backward(grad_middle, middle_kept)
    grad_branch = lowered(grad_sum)
    grad_mixed = lowered(turned_dot(grad_branch, attn_w[:, 3 * D :]))
    results = attend_back(query, grad_mixed, stat, keys, values, clip_count)
    results, grad_branch, *waiting = fence(results, grad_branch, *waiting)
    grad_query, grad_keys, grad_values = results[0], results[1::2], results[2::2]
    back = [
        turned_dot(dk, attn_w[:, D : 2 * D]) + turned_dot(dv, attn_w[:, 2 * D : 3 * D])
        for dk, dv in zip(grad_keys, grad_values)
    ]
    arrived = return_ring([lowered(block) for block in back])
    grad_hidden = grad_sum + turned_dot(grad_query, attn_w[:, :D]) + back[0]
    for block in arrived:
        grad_hidden = grad_hidden + block.astype(jnp.float32)
    grads = [
        lowered(rows_dot(entries[0], grad_query)),
        lowered(sum(rows_dot(entry, dk) for entry, dk in zip(entries, grad_keys))),
        lowered(sum(rows_dot(entry, dv) for entry, dv in zip(entries, grad_values))),
        lowered(rows_dot(mixed, grad_branch)),
    ]
    vectors = [
        column_sum(grad_query),
        sum(column_sum(dv) for dv in grad_values),
        column_sum(grad_branch),
        grad_gain,
        grad_bias,
    ]
    return grad_hidden, grads, vectors, waiting


def fused_forward(hidden, hidden_low, weights, pieces, clip_count, waiting):
    attn_whole, feed_whole, first = weights
    place = 0
    none = jnp.zeros_like(pieces[0])
    entries = [hidden_low]
    packs = [project(hidden_low, attn_whole, place, [pieces[0], none, pieces[1]])]
    for entry in gather_ring(hidden_low)[1:]:
        entries.append(entry)
        packs.append(project(entry, attn_whole, place + 1, [none, pieces[1]]))
    query = (packs[0], 0)
    keys = [(pack, 1 if j == 0 else 0) for j, pack in enumerate(packs)]
    values = [(pack, 2 if j == 0 else 1) for j, pack in enumerate(packs)]
    mixed, stat = attend(query, keys, values, clip_count)
    if waiting is not None:
        mixed, waiting = fence(mixed, waiting)
    low, level1, scale1, active, slope, result, result_low, level2, scale2 = feed_forward(
        hidden, mixed, attn_whole, feed_whole, first, place, pieces[2:]
    )
    cache = (entries, query, keys, values, mixed, stat, (level1, scale1, low, slope, active, level2, scale2))
    return result, result_low, cache, waiting


def fused_backward(grads, cache, weights, pieces, clip_count, chunks, room, waiting):
    attn_whole, feed_whole, first = weights
    entries, query, keys, values, mixed, stat, kept = cache
    shards = lax.axis_size("shard")
    grad_sum, branch, grad_mixed, sums, grad_expand_bias, feed_chunks = feed_back(
        grads, kept, attn_whole, feed_whole, first, 0, pieces[3], pieces[7], chunks
    )
    if waiting is not None:
        grad_mixed, held = fence(grad_mixed, waiting[1])
        waiting = waiting[0](held)
    results = attend_back(query, grad_mixed, stat, keys, values, clip_count)
    if waiting is not None:
        results, waiting = fence(results, waiting)
    backs = entry_back(grad_sum, results[0], results[1:], attn_whole, 0)
    results, backs, branch = fence(results, backs, branch)
    arrived = return_ring(backs)
    attn_chunks, more = attn_grads(entries, results[0], mixed, branch, results[1:], shards, room)
    arrived, more = fence(arrived, more)
    vectors = [more[0:1], more[1:2], sums[0:1], sums[1:2], sums[2:3], grad_expand_bias, sums[3:4], sums[4:5], sums[5:6]]
    return [backs[0]] + arrived, feed_chunks, attn_chunks, vectors, waiting


def plain_backward(grads, cache, weights, pieces, clip_count, chunks, room, waiting):
    attn_w, expand_w, shrink_w = weights
    shards = lax.axis_size("shard")
    grad = grads[0]
    for part in grads[1:]:
        grad = grad + part.astype(jnp.float32)
    grad_middle, grad_expand, grad_shrink, feed_vectors = feed_backward(grad, cache, expand_w, shrink_w)
    rest = [] if waiting is None else [waiting[0](waiting[1])]
    grad_hidden, attn_list, attn_vectors, rest = attend_backward(grad_middle, cache, attn_w, clip_count, *rest)
    blocks = [] if chunks is None else [chunks]
    blocks += [grad_expand[:, j * D : (j + 1) * D].reshape(shards, -1, D) for j in range(FF // D)]
    blocks.append(grad_shrink.reshape(shards, -1, D))
    attn_chunks = jnp.concatenate([item.reshape(shards, -1, D) for item in attn_list], 1)
    vectors = attn_vectors + feed_vectors
    return [grad_hidden], jnp.concatenate(blocks, 1), attn_chunks, vectors, rest[0] if rest else None


def adam_update(weight, grad, first, second, rate, decay):
    first = beta_one * first + (1 - beta_one) * grad
    second = beta_two * second + (1 - beta_two) * grad * grad
    share_fraction = (
        first / (1 - beta_one**STEP) / (jnp.sqrt(second / (1 - beta_two**STEP)) + adam_epsilon)
    )
    return (weight - rate * (share_fraction + decay * weight), first, second)


def matrix_rule(weight, grad, first, second):
    return adam_update(weight, grad, first, second, rate_matrix, decay_rate)


def gather_rows(block):
    whole = lax.all_gather(block, "shard", axis=0, tiled=True)
    return whole.reshape((-1,) + block.shape)


def pass_kernel(*refs):
    pass


def fence(*values):
    flat, tree = jax.tree.flatten(values)
    spec = pl.BlockSpec(memory_space=pl.ANY)
    flat = pl.pallas_call(
        pass_kernel,
        in_specs=[spec] * len(flat),
        out_specs=[spec] * len(flat),
        out_shape=[jax.ShapeDtypeStruct(v.shape, v.dtype) for v in flat],
        input_output_aliases={i: i for i in range(len(flat))},
        cost_estimate=SMALL_COST,
        name="fence",
    )(*flat)
    return jax.tree.unflatten(tree, flat)


def scatter_chunks(chunks):
    return lax.psum_scatter(chunks, "shard", scatter_dimension=0, tiled=False)


def trade(chunks):
    return lax.all_to_all(chunks, "shard", split_axis=0, concat_axis=0, tiled=True)


def on_device(
    features,
    time_mask,
    negatives,
    target_codes,
    feature_weight,
    feature_first,
    feature_second,
    conv_weight,
    conv_first,
    conv_second,
    attention_weight,
    attention_first,
    attention_second,
    left_basis_t,
    right_orthogonal_basis,
    expand_weight,
    expand_first,
    expand_second,
    shrink_weight,
    shrink_first,
    shrink_second,
    final_weight,
    final_first,
    final_second,
    target_weight,
    target_first,
    target_second,
    codebook_weight,
    codebook_first,
    codebook_second,
    vector_params,
    vector_first,
    vector_second,
):
    clip_count, frame_count = (features.shape[0], features.shape[1])
    row_count = clip_count * frame_count
    seq_count = lax.axis_size("seq")
    shards = lax.axis_size("shard")
    clip_frames = frame_count * seq_count
    taps = conv_weight.shape[0]
    small_items = [feature_weight, final_weight, target_weight, codebook_weight]

    def split_small(packed):
        blocks = []
        start = 0
        for item in small_items:
            depth, width = item.shape
            count = -(-width // taps)
            pieces = [packed[..., start + j * depth : start + (j + 1) * depth, :] for j in range(count)]
            blocks.append(jnp.concatenate(pieces, -1)[..., :width])
            start += count * depth
        size = vector_params.shape[0]
        count = -(-size // taps)
        vector = packed[..., start : start + count, :].reshape(packed.shape[:-2] + (-1,))[..., :size]
        return blocks, vector, packed[..., start + count, :2]

    parts = shards // (4 * LAYERS)
    rows = D // shards

    def own_attn(layer):
        return jnp.concatenate([lowered(attention_weight[4 * layer + i]) for i in range(4)])

    def own_feed(layer):
        expand_own = lowered(expand_weight[layer])
        return jnp.concatenate(
            [expand_own[:, j * D : (j + 1) * D] for j in range(FF // D)] + [lowered(shrink_weight[layer])]
        )

    first_all = gather_rows(pack_weights(conv_weight, small_items, vector_params, SMALL_ROWS))
    conv_w = first_all
    blocks, vector_low, _ = split_small(first_all[:, D:])
    feat_w, final_w, target_w, code_w = [block.reshape(-1, block.shape[-1]) for block in blocks]

    def spread_halves(block):
        number = block.shape[1]
        columns = D // parts
        cut = block.reshape(4 * LAYERS, number, rows, parts, columns).transpose(0, 3, 1, 2, 4)
        return trade(cut.reshape(shards, number, rows, columns))

    def join_halves(got):
        number = got.shape[1]
        got = got.transpose(1, 0, 2, 3).reshape(number, D, D // parts)
        if parts != 2:
            groups = [[i * parts + j for j in range(parts)] for i in range(shards // parts)]
            return lax.all_gather(got, "shard", axis=2, tiled=True, axis_index_groups=groups)
        other = lax.ppermute(got, "shard", [(i, i ^ 1) for i in range(shards)])
        second = lax.axis_index("shard") % 2 == 1
        return jnp.concatenate([jnp.where(second, other, got), jnp.where(second, got, other)], 2)

    def plain_weights(attn_whole, feed_whole):
        blocks = [attn_whole[:, j * rows : (j + 1) * rows].reshape(D, D) for j in range(4)]
        columns = [feed_whole[:, j * rows : (j + 1) * rows].reshape(D, D) for j in range(FF // D)]
        shrink = feed_whole[:, FF // D * rows :].reshape(FF, D)
        return jnp.concatenate(blocks, 1), jnp.concatenate(columns, 1), shrink

    first_frame = lax.axis_index("seq") * frame_count
    ring_draws = (negatives - first_frame + clip_frames) % clip_frames
    counts = count_draws(ring_draws.transpose(0, 2, 1), clip_frames)
    held = jnp.stack([lowered(left_basis_t), lowered(attention_first), lowered(attention_second)], 1)
    counts, own_0 = fence(counts, jnp.concatenate([own_attn(0), own_feed(0)]))
    whole_0 = gather_rows(own_0)
    fused = rows % 16 == 0
    weights = [(whole_0, whole_0, 4) if fused else plain_weights(whole_0[:, : 4 * rows], whole_0[:, 4 * rows :])]

    pieces = vector_pieces(vector_low.reshape(-1).astype(jnp.float32))
    mask_on = (time_mask > 0).reshape(row_count, 1)
    feats = features.reshape(row_count, CIN).astype(jnp.float32)
    normed, norm_kept = norm_forward(feats, pieces[0], pieces[1])
    normed_low = lowered(normed)
    projected = bdot(normed_low, feat_w) + pieces[2]
    masked = jnp.where(mask_on, pieces[3][None, :], projected)
    padded = with_halo(lowered(masked).reshape(clip_count, frame_count, D), KW // 2)
    strip_rows = frame_count * clip_count // 16 // PACK
    strips = to_strips(padded, frame_count)
    conv_out = from_strips(conv_forward(strips, conv_w, 0, strip_rows, shards), clip_count) + pieces[4]
    conv_active, conv_slope = gelu_parts(conv_out)
    hidden, front_kept = norm_forward(masked + conv_active, pieces[5], pieces[6])

    hidden_low = lowered(hidden)
    codes = jnp.concatenate(gather_ring(target_codes), 1).reshape(clip_count * clip_frames, QGROUPS)
    width = PROJ // QGROUPS
    code_f = code_w.astype(jnp.float32)
    target_f = target_w.astype(jnp.float32)
    table = jnp.concatenate(
        [fdot(code_f[g * width : (g + 1) * width].T, target_f[g * width : (g + 1) * width]) for g in range(QGROUPS)]
    )
    choice = jnp.concatenate(
        [(codes[:, g : g + 1] == jnp.arange(CODES)[None, :]).astype(jnp.float32) for g in range(QGROUPS)], 1
    )
    raw_targets = fdot(choice, table) + pieces[-1]
    target_kept = lax.rsqrt(jnp.sum(raw_targets * raw_targets, -1, keepdims=True) + unit_epsilon)
    targets = raw_targets * target_kept
    forward = fused_forward if fused else layer_forward
    hidden, hidden_low, own_1 = fence(hidden, hidden_low, own_attn(1))
    attn_whole_1 = gather_rows(own_1)
    hidden, hidden_low, cache, own_1 = forward(hidden, hidden_low, weights[0], pieces[7:16], clip_count, own_feed(1))
    feed_whole_1 = gather_rows(own_1)
    caches = [cache]
    weights.append((attn_whole_1, feed_whole_1, 0) if fused else plain_weights(attn_whole_1, feed_whole_1))
    hidden, top_low, cache, (targets, target_kept) = forward(
        hidden, hidden_low, weights[1], pieces[16:25], clip_count, (targets, target_kept)
    )
    caches.append(cache)
    context, context_pull = jax.vjp(unit_rows, bdot(top_low, final_w) + pieces[-2])
    context_low = lowered(context).reshape(clip_count, frame_count, PROJ)

    counts = counts.astype(jnp.float32)
    targets_low = lowered(targets).reshape(clip_count, clip_frames, PROJ)
    similar = jnp.einsum("clp,cfp->clf", targets_low, context_low, preferred_element_type=jnp.float32)
    logits = similar / contrastive_sharpness
    place = jnp.arange(clip_frames)[:, None] == jnp.arange(frame_count)[None, :]
    own = place.astype(jnp.float32)[None]
    weight = counts + own
    largest = jnp.max(jnp.where(weight > 0, logits, -jnp.inf), 1, keepdims=True)
    power = weight * jnp.exp(jnp.where(weight > 0, logits - largest, 0.0))
    running_totals = jnp.sum(power, 1, keepdims=True)
    mask_as_floats = time_mask.astype(jnp.float32)
    own_logit = jnp.sum(own * logits, 1)
    row_loss = largest[:, 0] + jnp.log(running_totals[:, 0]) - own_logit
    loss_sum = jnp.sum(mask_as_floats * row_loss)
    mask_count = jnp.sum(mask_as_floats)
    derivative_multiplier = 1.0 / (clip_count * shards * clip_frames)
    grad_similar = lowered(
        mask_as_floats[:, None, :]
        * (power / running_totals - own)
        * (derivative_multiplier / contrastive_sharpness)
    )
    grad_context = jnp.einsum("clf,clp->cfp", grad_similar, targets_low, preferred_element_type=jnp.float32)
    grad_targets = jnp.einsum("clf,cfp->clp", grad_similar, context_low, preferred_element_type=jnp.float32)
    grad_targets = grad_targets.reshape(-1, PROJ)
    grad_raw = target_kept * (grad_targets - targets * jnp.sum(grad_targets * targets, -1, keepdims=True))
    grad_table = fdot(choice.T, grad_raw)
    tables = [grad_table[g * CODES : (g + 1) * CODES] for g in range(QGROUPS)]
    grad_target_w = jnp.concatenate([fdot(code_f[g * width : (g + 1) * width], tables[g]) for g in range(QGROUPS)])
    grad_codebook = jnp.concatenate(
        [fdot(target_f[g * width : (g + 1) * width], tables[g].T) for g in range(QGROUPS)]
    )
    grad_target_bias = column_sum(grad_raw)
    (grad_context_raw,) = context_pull(grad_context.reshape(row_count, PROJ))
    grad_context_low = lowered(grad_context_raw)
    grad_final_w = rows_dot(top_low, grad_context_low)
    grad_final_bias = column_sum(grad_context_low)
    grad_hidden = turned_dot(grad_context_low, final_w)

    columns = D // parts
    def rotated_adam(first, second, grad):
        first = beta_rotated * first + (1 - beta_rotated) * grad
        second = beta_rotated * second + (1 - beta_rotated) * grad * grad
        share = first / (1 - beta_rotated**STEP) / (jnp.sqrt(second / (1 - beta_rotated**STEP)) + adam_epsilon)
        return share, first, second

    def rotate(whole_grad):
        left_low, first_low, second_low = traded[0], traded[1], traded[2]
        group = lax.axis_index("shard") // parts
        right_low = lowered(lax.dynamic_index_in_dim(right_orthogonal_basis, group, 0, keepdims=False))
        rotated = bdot(lowered(bdot(left_low, whole_grad)), right_low)
        direction = rotated_adam(first_low.astype(jnp.float32), second_low.astype(jnp.float32), rotated)[0]
        half_back = lowered(turned_dot(lowered(direction), right_low))
        part_start = (lax.axis_index("shard") % parts) * columns
        rotated_part = lax.dynamic_slice_in_dim(lowered(rotated), part_start, columns, 1)
        update_part = lowered(rows_dot(left_low, lax.dynamic_slice_in_dim(half_back, part_start, columns, 1)))
        sent = jnp.stack([rotated_part.reshape(shards, rows, columns), update_part.reshape(shards, rows, columns)], 1)
        return sent

    backward = fused_backward if fused else plain_backward
    grads, chunks, attn_chunks, vectors_1, _ = backward(
        [grad_hidden], caches[1], weights[1], pieces[16:25], clip_count, None, 4 * rows + 8 * rows * fused, None
    )
    (chunks,) = fence(chunks)
    sum_feed_1 = scatter_chunks(chunks)
    grads, chunks, attn_chunks, vectors_0, traded = backward(
        grads, caches[0], weights[0], pieces[7:16], clip_count, attn_chunks, 4 * rows, (spread_halves, held)
    )
    (chunks,) = fence(chunks)
    sum_feed_0 = scatter_chunks(chunks)
    (attn_chunks,) = fence(attn_chunks)
    sum_attn = scatter_chunks(attn_chunks)
    grad_hidden = grads[0]
    for part in grads[1:]:
        grad_hidden = grad_hidden + part.astype(jnp.float32)
    grad_sum, grad_gain_enc, grad_bias_enc = norm_backward(grad_hidden, front_kept)
    grad_conv_low = lowered(grad_sum * conv_slope)
    grad_strips = to_strips(with_halo(grad_conv_low.reshape(clip_count, frame_count, D), KW // 2), frame_count)
    conv_chunks = conv_weight_grad(strips, grad_strips, strip_rows, shards)
    grad_strips, conv_chunks, sum_feed_1 = fence(grad_strips, conv_chunks, sum_feed_1)
    grad_back = conv_input_grad(grad_strips, conv_w, 0, strip_rows, shards)
    traded = join_halves(traded)
    sum_feed_1 = seq_sum(sum_feed_1)
    grad_back, sum_feed_1, sum_feed_0, traded = fence(grad_back, sum_feed_1, sum_feed_0, traded)
    grad_masked = grad_sum + from_strips(grad_back, clip_count)
    grad_embedding = jnp.sum(jnp.where(mask_on, grad_masked, 0.0), 0, keepdims=True)
    grad_projected = lowered(jnp.where(mask_on, 0.0, grad_masked))
    grad_feat_w = rows_dot(normed_low, grad_projected)
    grad_gain_feat, grad_bias_feat = norm_vectors(turned_dot(grad_projected, feat_w), norm_kept)
    vector_grads = [
        grad_gain_feat,
        grad_bias_feat,
        column_sum(grad_projected),
        grad_embedding,
        column_sum(grad_conv_low),
        grad_gain_enc,
        grad_bias_enc,
    ]
    vector_grads += vectors_0 + vectors_1
    vector_grads += [grad_final_bias, grad_target_bias]
    extra = jnp.pad(jnp.stack([loss_sum, mask_count])[None], ((0, 0), (0, 126)))
    small_grads = [grad_feat_w, grad_final_w, grad_target_w, grad_codebook]
    small_chunks = pack_grads(small_grads, vector_grads, extra, shards, SMALL_ROWS, taps)
    sum_feed_0 = seq_sum(sum_feed_0)
    small_chunks, sum_attn, sum_feed_0 = fence(small_chunks, sum_attn, sum_feed_0)
    attn_rows = jnp.concatenate([seq_sum(sum_attn), sum_feed_0[: 4 * rows]]).reshape(4 * LAYERS, 1, rows, D)
    whole_grad = join_halves(spread_halves(lowered(attn_rows)))[0]
    sent = rotate(whole_grad)
    small_sum, sum_conv, rotation = reduce_chunks(
        (shards, seq_count), (SMALL_ROWS, 96), [small_chunks, conv_chunks], sent
    )
    arrived = rotation.reshape(4 * LAYERS, parts, 2, rows, columns).transpose(2, 0, 3, 1, 4)
    arrived = arrived.reshape(2, 4 * LAYERS, rows, D).astype(jnp.float32)
    _, rot_first, rot_second = rotated_adam(attention_first, attention_second, arrived[0])
    new_attention = attention_weight - rate_rotated * arrived[1]
    feed_sums = [sum_feed_0[4 * rows :], sum_feed_1]
    (sum_feat, sum_final, sum_target, sum_code), sum_vector, sum_loss = split_small(small_sum)
    sum_expand = jnp.stack(
        [s[: -shrink_weight.shape[1]].reshape(FF // D, -1, D).transpose(1, 0, 2).reshape(-1, FF) for s in feed_sums]
    )
    sum_shrink = jnp.stack([s[-shrink_weight.shape[1] :] for s in feed_sums])
    feature_new = adam_update(feature_weight, sum_feat, feature_first, feature_second, rate_matrix, decay_rate)
    conv_new = turned_adam(matrix_rule, conv_weight, sum_conv, conv_first, conv_second)
    expand_new = adam_update(expand_weight, sum_expand, expand_first, expand_second, rate_matrix, decay_rate)
    shrink_new = adam_update(shrink_weight, sum_shrink, shrink_first, shrink_second, rate_matrix, decay_rate)
    final_new = adam_update(final_weight, sum_final, final_first, final_second, rate_matrix, decay_rate)
    target_new = adam_update(target_weight, sum_target, target_first, target_second, rate_target, decay_rate)
    codebook_new = adam_update(codebook_weight, sum_code, codebook_first, codebook_second, rate_codebook, decay_rate)
    vector_new = adam_update(vector_params, sum_vector, vector_first, vector_second, rate_vector, 0.0)
    return (
        (sum_loss,)
        + feature_new
        + conv_new
        + (new_attention, rot_first, rot_second)
        + expand_new
        + shrink_new
        + final_new
        + target_new
        + codebook_new
        + vector_new
    )


def solution(mesh):
    return jax.shard_map(
        on_device,
        mesh=mesh,
        in_specs=(
            P("shard", "seq", None),
            P("shard", "seq"),
            P("shard", "seq", None),
            P("shard", "seq", None),
            P("shard", None),
            P("shard", None),
            P("shard", None),
            P("shard", None),
            P("shard", None),
            P("shard", None),
            P(None, "shard", None),
            P(None, "shard", None),
            P(None, "shard", None),
            P(None, "shard", None),
            P(),
            P(None, "shard", None),
            P(None, "shard", None),
            P(None, "shard", None),
            P(None, "shard", None),
            P(None, "shard", None),
            P(None, "shard", None),
            P("shard", None),
            P("shard", None),
            P("shard", None),
            P("shard", None),
            P("shard", None),
            P("shard", None),
            P("shard", None),
            P("shard", None),
            P("shard", None),
            P("shard"),
            P("shard"),
            P("shard"),
        ),
        out_specs=(
            P(),
            P("shard", None),
            P("shard", None),
            P("shard", None),
            P("shard", None),
            P("shard", None),
            P("shard", None),
            P(None, "shard", None),
            P(None, "shard", None),
            P(None, "shard", None),
            P(None, "shard", None),
            P(None, "shard", None),
            P(None, "shard", None),
            P(None, "shard", None),
            P(None, "shard", None),
            P(None, "shard", None),
            P("shard", None),
            P("shard", None),
            P("shard", None),
            P("shard", None),
            P("shard", None),
            P("shard", None),
            P("shard", None),
            P("shard", None),
            P("shard", None),
            P("shard"),
            P("shard"),
            P("shard"),
        ),
        check_vma=False,
    )
```

```python
import functools

import jax
import jax.numpy as jnp
from jax import lax
from jax.experimental import pallas as pl
from jax.experimental.pallas import tpu as pltpu
from jax.sharding import PartitionSpec as P

D = 768
HEADS = 12
HDIM = 64
FF = 3072
CIN = 512
PROJ = 256
CODES = 320
QGROUPS = 2
LAYERS = 2
STEP = 10
SMALL_ROWS = 160


beta_one = 0.9
beta_two = 0.95
beta_rotated = 0.5
adam_epsilon = 1e-08
decay_rate = 0.01
rate_matrix = 0.02
rate_target = 0.08
rate_codebook = 0.6
rate_vector = 0.3
rate_rotated = 0.08
contrastive_sharpness = 0.1
norm_epsilon = 1e-05
unit_epsilon = 1e-06

KW = 128
GROUPS = 16
GC = D // GROUPS
LANE = 64
PACK = 4
PADW = GROUPS * LANE
HALF = KW // PACK
STEPS = HALF + 1
VMEM = 56 * 1024 * 1024
SMALL_COST = pl.CostEstimate(flops=1024, bytes_accessed=1024, transcendentals=0)
CONV_COST = pl.CostEstimate(flops=35 * 10**9, bytes_accessed=10**7, transcendentals=0)
NT = (((1,), (1,)), ((), ()))
NN = (((1,), (0,)), ((), ()))


def mm(a, b, dims=NN):
    return lax.dot_general(a, b, dims, preferred_element_type=jnp.float32)


def spread_matrix(rows, out_cols, block, wide):
    i = lax.broadcasted_iota(jnp.int32, (rows, out_cols), 0)
    j = lax.broadcasted_iota(jnp.int32, (rows, out_cols), 1)
    return ((i // block) * wide + i % block == j).astype(jnp.bfloat16)


def pack_pair(x_ref, even_ref, odd_ref, rows):
    low = lax.broadcasted_iota(jnp.int32, (rows * 16, 128), 1) < LANE
    x = x_ref[...].reshape(rows, PACK, 16, 128)
    for half in range(2):
        first = x[:, 2 * half].reshape(rows * 16, 128).astype(jnp.float32)
        second = x[:, 2 * half + 1].reshape(rows * 16, 128).astype(jnp.float32)
        even_ref[:, half * 128:half * 128 + 128] = jnp.where(low, first, pltpu.roll(second, LANE, 1)).astype(jnp.bfloat16)
        odd_ref[:, half * 128:half * 128 + 128] = jnp.where(low, pltpu.roll(first, LANE, 1), second).astype(jnp.bfloat16)


def unpack_pair(even, odd, out_ref, rows):
    low = lax.broadcasted_iota(jnp.int32, (rows * 16, 128), 1) < LANE
    parts = []
    for half in range(2):
        e = even[:, half * 128:half * 128 + 128]
        o = odd[:, half * 128:half * 128 + 128]
        parts.append(jnp.where(low, e, pltpu.roll(o, LANE, 1)).reshape(rows, 1, 16, 128))
        parts.append(jnp.where(low, pltpu.roll(e, LANE, 1), o).reshape(rows, 1, 16, 128))
    out_ref[...] = jnp.concatenate(parts, axis=1).reshape(PACK * rows, 16, 128)


def widen_taps(w_ref, wide_ref, shards):
    per = KW // shards
    sel = spread_matrix(per * GC, per * LANE, GC, LANE)
    block = mm(w_ref[...].reshape(shards * 2 * GC, per * GC), sel).astype(jnp.bfloat16)
    for group in range(2):
        wide_ref[group, GC:, :] = jnp.zeros((LANE - GC, STEPS * 256), jnp.bfloat16)
        wide_ref[group, 0:GC, KW * LANE:] = jnp.zeros((GC, STEPS * 256 - KW * LANE), jnp.bfloat16)
        for s in range(shards):
            start = (2 * s + group) * GC
            wide_ref[group, 0:GC, s * per * LANE:(s + 1) * per * LANE] = block[start:start + GC]


def build_taps(wide_ref, taps_ref, group):
    wide = wide_ref[group]
    shifted = pltpu.roll(wide.astype(jnp.float32), LANE, 1).astype(jnp.bfloat16)
    total = STEPS * 256
    taps_ref[0:64, :] = wide
    taps_ref[64:128, :] = shifted
    taps_ref[128:192, 0:128] = jnp.zeros((64, 128), jnp.bfloat16)
    taps_ref[128:192, 128:total] = wide[:, 0:total - 128]
    taps_ref[192:256, 0:128] = jnp.zeros((64, 128), jnp.bfloat16)
    taps_ref[192:256, 128:total] = shifted[:, 0:total - 128]


def conv_forward_kernel(rows, shards, x_ref, w_ref, y_ref, even_ref, odd_ref, taps_ref, wide_ref):
    m = rows * 16
    pack_pair(x_ref, even_ref, odd_ref, rows + HALF)
    widen_taps(w_ref, wide_ref, shards)
    results = []
    for group, packed in enumerate((even_ref, odd_ref)):
        build_taps(wide_ref, taps_ref, group)
        left = jnp.concatenate([packed[q * 16:q * 16 + m, :] for q in range(STEPS)], axis=1)
        results.append(mm(left, taps_ref[...], NT))
    unpack_pair(results[0], results[1], y_ref, rows)


def conv_forward(x, w, first, rows, shards):
    frames = PACK * (rows + HALF)
    return pl.pallas_call(
        functools.partial(conv_forward_kernel, rows, shards),
        grid=(GROUPS // 2,),
        in_specs=[
            pl.BlockSpec((frames, 16, 128), lambda g: (0, 0, g)),
            pl.BlockSpec((shards, 2 * GC, w.shape[2]), lambda g: (0, first + g, 0)),
        ],
        out_specs=pl.BlockSpec((PACK * rows, 16, 128), lambda g: (0, 0, g)),
        out_shape=jax.ShapeDtypeStruct((PACK * rows, 16, PADW), jnp.float32),
        scratch_shapes=[pltpu.VMEM(((rows + HALF) * 16, 256), jnp.bfloat16)] * 2 + [
            pltpu.VMEM((256, STEPS * 256), jnp.bfloat16),
            pltpu.VMEM((2, LANE, STEPS * 256), jnp.bfloat16),
        ],
        cost_estimate=SMALL_COST,
        compiler_params=pltpu.CompilerParams(vmem_limit_bytes=VMEM, dimension_semantics=("arbitrary",)),
        name="conv_forward",
    )(x, w)


def conv_input_kernel(rows, shards, d_ref, w_ref, dx_ref, even_ref, odd_ref, taps_ref, wide_ref):
    m = rows * 16
    pack_pair(d_ref, even_ref, odd_ref, rows + HALF)
    widen_taps(w_ref, wide_ref, shards)
    results = []
    for group, packed in enumerate((even_ref, odd_ref)):
        build_taps(wide_ref, taps_ref, group)
        acc = jnp.zeros((m, 256), jnp.float32)
        for q in range(STEPS):
            left = packed[(HALF - q) * 16:(HALF - q) * 16 + m, :]
            acc = acc + mm(left, taps_ref[:, q * 256:q * 256 + 256])
        results.append(acc)
    unpack_pair(results[0], results[1], dx_ref, rows)


def conv_input_grad(d, w, first, rows, shards):
    frames = PACK * (rows + HALF)
    return pl.pallas_call(
        functools.partial(conv_input_kernel, rows, shards),
        grid=(GROUPS // 2,),
        in_specs=[
            pl.BlockSpec((frames, 16, 128), lambda g: (0, 0, g)),
            pl.BlockSpec((shards, 2 * GC, w.shape[2]), lambda g: (0, first + g, 0)),
        ],
        out_specs=pl.BlockSpec((PACK * rows, 16, 128), lambda g: (0, 0, g)),
        out_shape=jax.ShapeDtypeStruct((PACK * rows, 16, PADW), jnp.float32),
        scratch_shapes=[pltpu.VMEM(((rows + HALF) * 16, 256), jnp.bfloat16)] * 2 + [
            pltpu.VMEM((256, STEPS * 256), jnp.bfloat16),
            pltpu.VMEM((2, LANE, STEPS * 256), jnp.bfloat16),
        ],
        cost_estimate=CONV_COST,
        compiler_params=pltpu.CompilerParams(vmem_limit_bytes=VMEM, dimension_semantics=("arbitrary",)),
        name="conv_input_grad",
    )(d, w)


def conv_weight_kernel(rows, shards, x_ref, d_ref, dw_ref, xe_ref, xo_ref, de_ref, do_ref, prod_ref, grad_ref):
    m = rows * 16
    per = KW // shards
    width = KW * LANE
    pack_pair(x_ref, xe_ref, xo_ref, rows + HALF)
    pack_pair(d_ref, de_ref, do_ref, rows)
    for group, (x_packed, d_packed) in enumerate(((xe_ref, de_ref), (xo_ref, do_ref))):
        d_turned = d_packed[...].astype(jnp.float32).T.astype(jnp.bfloat16)
        for q in range(STEPS):
            prod_ref[:, q * 256:q * 256 + 256] = mm(d_turned, x_packed[q * 16:q * 16 + m, :])
        straight = prod_ref[0:GC, 0:width] + prod_ref[128:128 + GC, 128:128 + width]
        turned_part = prod_ref[64:64 + GC, :] + pltpu.roll(prod_ref[192:192 + GC, :], STEPS * 256 - 128, 1)
        grad = straight + pltpu.roll(turned_part, STEPS * 256 - 64, 1)[:, 0:width]
        grad = grad.astype(jnp.bfloat16)
        for s in range(shards):
            start = (2 * s + group) * GC
            grad_ref[start:start + GC, :] = grad[:, s * per * LANE:(s + 1) * per * LANE]
    sel = spread_matrix(per * GC, per * LANE, GC, LANE)
    dw_ref[...] = mm(grad_ref[...], sel, NT).astype(jnp.bfloat16).reshape(shards, 2 * GC, per * GC)


def conv_weight_grad(x, d, rows, shards):
    per = KW // shards
    first = HALF * PACK // 2
    d = d[first:first + PACK * rows]
    return pl.pallas_call(
        functools.partial(conv_weight_kernel, rows, shards),
        grid=(GROUPS // 2,),
        in_specs=[
            pl.BlockSpec((PACK * (rows + HALF), 16, 128), lambda g: (0, 0, g)),
            pl.BlockSpec((PACK * rows, 16, 128), lambda g: (0, 0, g)),
        ],
        out_specs=pl.BlockSpec((shards, 2 * GC, per * GC), lambda g: (0, g, 0)),
        out_shape=jax.ShapeDtypeStruct((shards, D, per * GC), jnp.bfloat16),
        scratch_shapes=[
            pltpu.VMEM(((rows + HALF) * 16, 256), jnp.bfloat16),
            pltpu.VMEM(((rows + HALF) * 16, 256), jnp.bfloat16),
            pltpu.VMEM((rows * 16, 256), jnp.bfloat16),
            pltpu.VMEM((rows * 16, 256), jnp.bfloat16),
            pltpu.VMEM((256, STEPS * 256), jnp.float32),
            pltpu.VMEM((shards * 2 * GC, per * LANE), jnp.bfloat16),
        ],
        cost_estimate=CONV_COST,
        compiler_params=pltpu.CompilerParams(vmem_limit_bytes=VMEM, dimension_semantics=("arbitrary",)),
        name="conv_weight_grad",
    )(x, d)


def turned_adam_kernel(rule, grad_ref, weight_ref, first_ref, second_ref, new_ref, new_first_ref, new_second_ref):
    new, first, second = rule(weight_ref[...], grad_ref[...].T, first_ref[...], second_ref[...])
    new_ref[...] = new
    new_first_ref[...] = first
    new_second_ref[...] = second


def turned_adam(rule, weight, grad, first, second):
    return tuple(
        pl.pallas_call(
            functools.partial(turned_adam_kernel, rule),
            out_shape=[jax.ShapeDtypeStruct(weight.shape, jnp.float32)] * 3,
            cost_estimate=SMALL_COST,
            compiler_params=pltpu.CompilerParams(vmem_limit_bytes=VMEM),
            name="turned_adam",
        )(grad, weight, first, second)
    )


def put_pieces(out_ref, start, block, taps):
    depth, width = block.shape[-2:]
    for at in range(0, width, taps):
        size = min(taps, width - at)
        out_ref[..., start:start + depth, 0:size] = block[..., at:at + size]
        start += depth
    return start


def pack_weights_kernel(conv_ref, *refs):
    vector_ref, out_ref, held = refs[-3:]
    taps = conv_ref.shape[0]
    out_ref[0:D, :] = conv_ref[...].T.astype(jnp.bfloat16)
    held[...] = jnp.zeros_like(held)
    start = 0
    for ref in refs[:-3]:
        start = put_pieces(held, start, ref[...], taps)
    size = vector_ref.shape[1]
    for at in range(0, size, taps):
        width = min(taps, size - at)
        held[start:start + 1, 0:width] = vector_ref[:, at:at + width]
        start += 1
    out_ref[D:, :] = held[...].astype(jnp.bfloat16)


def pack_weights(conv, blocks, vector, rows):
    taps = conv.shape[0]
    return pl.pallas_call(
        pack_weights_kernel,
        out_shape=jax.ShapeDtypeStruct((D + rows, taps), jnp.bfloat16),
        scratch_shapes=[pltpu.VMEM((rows, taps), jnp.float32)],
        cost_estimate=SMALL_COST,
        compiler_params=pltpu.CompilerParams(vmem_limit_bytes=VMEM),
        name="pack_weights",
    )(conv, *blocks, vector.reshape(1, -1))


def pack_grads_kernel(blocks, *refs):
    extra_ref, out_ref, held, flat = refs[-4:]
    shards, _, taps = out_ref.shape
    held[...] = jnp.zeros_like(held)
    start = 0
    for ref in refs[:blocks]:
        start = put_pieces(held, start, ref[...], taps)
    place = 0
    for ref in refs[blocks:-4]:
        flat[:, place:place + ref.shape[1]] = ref[...]
        place += ref.shape[1]
    size = place // shards
    for s in range(shards):
        for row, at in enumerate(range(0, size, taps)):
            width = min(taps, size - at)
            held[s, start + row:start + row + 1, 0:width] = flat[:, s * size + at:s * size + at + width]
    start += -(-size // taps)
    held[:, start:start + 1, 0:128] = jnp.broadcast_to(extra_ref[...][None], (shards, 1, 128))
    out_ref[...] = held[...].astype(jnp.bfloat16)


def pack_grads(blocks, vectors, extra, shards, rows, taps):
    blocks = [block.reshape(shards, -1, block.shape[-1]) for block in blocks]
    vectors = [v.reshape(1, -1) for v in vectors]
    total = sum(v.shape[1] for v in vectors)
    return pl.pallas_call(
        functools.partial(pack_grads_kernel, len(blocks)),
        out_shape=jax.ShapeDtypeStruct((shards, rows, taps), jnp.bfloat16),
        scratch_shapes=[pltpu.VMEM((shards, rows, taps), jnp.float32), pltpu.VMEM((1, total), jnp.float32)],
        cost_estimate=SMALL_COST,
        compiler_params=pltpu.CompilerParams(vmem_limit_bytes=VMEM),
        name="pack_grads",
    )(*blocks, *vectors, extra)


def to_strips(padded, frame_count):
    clips = padded.shape[0]
    strips = 16 // clips
    length = frame_count // strips
    sel = spread_matrix(D, PADW, GC, LANE)
    wide = mm(padded.reshape(-1, D), sel).astype(jnp.bfloat16).reshape(clips, -1, PADW)
    parts = jnp.stack([wide[:, s * length:s * length + length + KW] for s in range(strips)], 1)
    return parts.reshape(16, length + KW, PADW).transpose(1, 0, 2)


def from_strips(y, clips):
    rows = y.transpose(1, 0, 2).reshape(-1, PADW)
    high = lax.reduce_precision(rows, 8, 7)
    rest = (rows - high).astype(jnp.bfloat16)
    high = high.astype(jnp.bfloat16)
    sel = spread_matrix(D, PADW, GC, LANE)
    return mm(high, sel, NT) + mm(rest, sel, NT)


SCALE = HDIM ** (-0.5)


def turned(block):
    return block.astype(jnp.float32).T.astype(jnp.bfloat16)


def attend_kernel(blocks, q_ref, *refs):
    keys = [refs[2 * j] for j in range(blocks)]
    values = [refs[2 * j + 1] for j in range(blocks)]
    mixed_ref, stat_ref = refs[2 * blocks:]
    frames = q_ref.shape[0]
    low = lax.broadcasted_iota(jnp.int32, (frames, 128), 1) < HDIM
    scaled = q_ref[...] * jnp.bfloat16(SCALE)
    none = jnp.zeros_like(scaled)
    turned_keys = [turned(k[...]) for k in keys]
    parts = []
    stats = []
    for head in range(2):
        query = jnp.where(low, scaled, none) if head == 0 else jnp.where(low, none, scaled)
        scores = [mm(query, k) for k in turned_keys]
        largest = functools.reduce(jnp.maximum, [jnp.max(s, 1, keepdims=True) for s in scores])
        powers = [jnp.exp(s - largest) for s in scores]
        total = functools.reduce(jnp.add, [jnp.sum(p, 1, keepdims=True) for p in powers])
        out = functools.reduce(jnp.add, [mm(p.astype(jnp.bfloat16), v[...]) for p, v in zip(powers, values)])
        parts.append(out * (1.0 / total))
        stats.append(jnp.broadcast_to(largest + jnp.log(total), (frames, 128)))
    mixed_ref[...] = jnp.where(low, parts[0], parts[1]).astype(jnp.bfloat16)
    rows = jnp.where(low, stats[0], stats[1]).T
    stat_ref[0, 0, 0:1, :] = rows[0:1, :]
    stat_ref[0, 0, 1:2, :] = rows[HDIM:HDIM + 1, :]


def head_spec(item, frames):
    if isinstance(item, tuple):
        return pl.BlockSpec((None, frames, 128), lambda c, h: (item[1], c, h))
    return pl.BlockSpec((frames, 128), lambda c, h: (c, h))


def head_array(item):
    return item[0] if isinstance(item, tuple) else item


def attend(query, keys, values, clips):
    blocks = len(keys)
    rows = head_array(query).shape[-2]
    frames = rows // clips
    spec = pl.BlockSpec((frames, 128), lambda c, h: (c, h))
    operands = [query]
    for k, v in zip(keys, values):
        operands += [k, v]
    return pl.pallas_call(
        functools.partial(attend_kernel, blocks),
        grid=(clips, HEADS // 2),
        in_specs=[head_spec(item, frames) for item in operands],
        out_specs=[spec, pl.BlockSpec((1, 1, 2, frames), lambda c, h: (c, h, 0, 0))],
        out_shape=[
            jax.ShapeDtypeStruct((rows, D), jnp.bfloat16),
            jax.ShapeDtypeStruct((clips, HEADS // 2, 2, frames), jnp.float32),
        ],
        cost_estimate=SMALL_COST,
        compiler_params=pltpu.CompilerParams(vmem_limit_bytes=VMEM, dimension_semantics=("arbitrary", "arbitrary")),
        name="attend",
    )(*[head_array(item) for item in operands])


def attend_back_kernel(blocks, q_ref, d_ref, stat_ref, *refs):
    keys = [refs[2 * j] for j in range(blocks)]
    values = [refs[2 * j + 1] for j in range(blocks)]
    dq_ref = refs[2 * blocks]
    dk = [refs[2 * blocks + 1 + 2 * j] for j in range(blocks)]
    dv = [refs[2 * blocks + 2 + 2 * j] for j in range(blocks)]
    frames = q_ref.shape[0]
    low = lax.broadcasted_iota(jnp.int32, (frames, 128), 1) < HDIM
    scaled = q_ref[...] * jnp.bfloat16(SCALE)
    grad = d_ref[...]
    none = jnp.zeros_like(scaled)
    q_turned = turned(scaled)
    d_turned = turned(grad)
    gap = jnp.zeros((HDIM, frames), jnp.bfloat16)
    k_turned = [turned(k[...]) for k in keys]
    dq_rows = []
    dk_sum = [None] * blocks
    dv_sum = [None] * blocks
    for head in range(2):
        pick = slice(head * HDIM, head * HDIM + HDIM)
        if head == 0:
            query, grad_head = jnp.where(low, scaled, none), jnp.where(low, grad, none)
            q_side = jnp.concatenate([q_turned[pick], gap], 0)
            d_side = jnp.concatenate([d_turned[pick], gap], 0)
        else:
            query, grad_head = jnp.where(low, none, scaled), jnp.where(low, none, grad)
            q_side = jnp.concatenate([gap, q_turned[pick]], 0)
            d_side = jnp.concatenate([gap, d_turned[pick]], 0)
        stat = stat_ref[0, 0, head:head + 1, :]
        probs = [jnp.exp(mm(k[...], q_side) - stat) for k in keys]
        weighted = [p * mm(v[...], d_side) for p, v in zip(probs, values)]
        delta = functools.reduce(jnp.add, [jnp.sum(w, 0, keepdims=True) for w in weighted])
        dq = None
        for j in range(blocks):
            ds = (weighted[j] - probs[j] * delta).astype(jnp.bfloat16)
            grad_v = mm(probs[j].astype(jnp.bfloat16), grad_head)
            grad_k = mm(ds, query)
            part = mm(k_turned[j][pick], ds)
            dq = part if dq is None else dq + part
            dv_sum[j] = grad_v if dv_sum[j] is None else dv_sum[j] + grad_v
            dk_sum[j] = grad_k if dk_sum[j] is None else dk_sum[j] + grad_k
        dq_rows.append(dq)
    dq_ref[...] = (jnp.concatenate(dq_rows, 0) * SCALE).T.astype(jnp.bfloat16)
    for j in range(blocks):
        dk[j][...] = dk_sum[j].astype(jnp.bfloat16)
        dv[j][...] = dv_sum[j].astype(jnp.bfloat16)


def attend_back(query, grad, stat, keys, values, clips):
    blocks = len(keys)
    rows = grad.shape[0]
    frames = rows // clips
    spec = pl.BlockSpec((frames, 128), lambda c, h: (c, h))
    operands = []
    for k, v in zip(keys, values):
        operands += [k, v]
    shape = jax.ShapeDtypeStruct((rows, D), jnp.bfloat16)
    return pl.pallas_call(
        functools.partial(attend_back_kernel, blocks),
        grid=(clips, HEADS // 2),
        in_specs=[head_spec(query, frames), spec, pl.BlockSpec((1, 1, 2, frames), lambda c, h: (c, h, 0, 0))]
        + [head_spec(item, frames) for item in operands],
        out_specs=[spec] * (1 + 2 * blocks),
        out_shape=[shape] * (1 + 2 * blocks),
        cost_estimate=SMALL_COST,
        compiler_params=pltpu.CompilerParams(vmem_limit_bytes=VMEM, dimension_semantics=("arbitrary", "arbitrary")),
        name="attend_back",
    )(head_array(query), grad, stat, *[head_array(item) for item in operands])


def count_kernel(draws, n_ref, out_ref):
    length, frames = out_ref.shape[1:]
    place = lax.broadcasted_iota(jnp.int32, (length // 8, 8, frames), 0) * 8 + lax.broadcasted_iota(
        jnp.int32, (length // 8, 8, frames), 1)
    total = jnp.zeros((length // 8, 8, frames), jnp.float32)
    for n in range(draws):
        row = n_ref[0, n:n + 1, :]
        total = total + jnp.where(place == row[None], 1.0, 0.0)
    out_ref[0] = total.reshape(length, frames).astype(jnp.bfloat16)


def count_draws(negatives, length):
    clips, draws, frames = negatives.shape
    tile = 128 if frames % 128 == 0 else frames
    return pl.pallas_call(
        functools.partial(count_kernel, draws),
        grid=(clips, frames // tile),
        in_specs=[pl.BlockSpec((1, draws, tile), lambda c, f: (c, 0, f))],
        out_specs=pl.BlockSpec((1, length, tile), lambda c, f: (c, 0, f)),
        out_shape=jax.ShapeDtypeStruct((clips, length, frames), jnp.bfloat16),
        cost_estimate=SMALL_COST,
        compiler_params=pltpu.CompilerParams(vmem_limit_bytes=VMEM, dimension_semantics=("arbitrary", "arbitrary")),
        name="count_draws",
    )(negatives)


def square(ref):
    return ref[...].reshape(D, D)


def project_kernel(x_ref, w_ref, b_ref, out_ref):
    out_ref[0] = (mm(x_ref[...], square(w_ref)) + b_ref[0]).astype(jnp.bfloat16)


def project(entry, whole, first, biases):
    count = len(biases)
    rows = entry.shape[0]
    shards, _, _ = whole.shape
    depth = D // shards
    return pl.pallas_call(
        project_kernel,
        grid=(count,),
        in_specs=[
            pl.BlockSpec((rows, D), lambda i: (0, 0)),
            pl.BlockSpec((shards, depth, D), lambda i: (0, first + i, 0)),
            pl.BlockSpec((1, 1, D), lambda i: (i, 0, 0)),
        ],
        out_specs=pl.BlockSpec((1, rows, D), lambda i: (i, 0, 0)),
        out_shape=jax.ShapeDtypeStruct((count, rows, D), jnp.bfloat16),
        cost_estimate=SMALL_COST,
        compiler_params=pltpu.CompilerParams(vmem_limit_bytes=VMEM, dimension_semantics=("arbitrary",)),
        name="project",
    )(entry, whole, jnp.stack(biases).reshape(count, 1, D))


def norm_rows(values, gain_row, bias_row):
    centred = values - jnp.mean(values, -1, keepdims=True)
    scale = lax.rsqrt(jnp.mean(centred * centred, -1, keepdims=True) + norm_epsilon)
    level = centred * scale
    return level * gain_row + bias_row, level, scale


def norm_rows_back(grad, level, scale, gain_row):
    inside = grad * gain_row
    centred = inside - jnp.mean(inside, -1, keepdims=True) - level * jnp.mean(inside * level, -1, keepdims=True)
    return scale * centred


def gelu_parts(values):
    half = 0.5 * (1.0 + lax.erf(values * 0.5**0.5))
    density = jnp.exp(-0.5 * values * values) * (2.0 * jnp.pi) ** -0.5
    return values * half, half + values * density


def feed_kernel(
    hidden_ref, mixed_ref, wo_ref, e_ref, s_ref, ob_ref, g1_ref, b1_ref, eb_ref, sb_ref, g2_ref, b2_ref,
    low_ref, level1_ref, scale1_ref, active_ref, slope_ref, result_ref, result_low_ref, level2_ref, scale2_ref,
    middle_ref, total_ref,
):
    step = pl.program_id(0)

    @pl.when(step == 0)
    def _():
        branch = mm(mixed_ref[...], square(wo_ref)) + ob_ref[...]
        middle, level, scale = norm_rows(hidden_ref[...] + branch, g1_ref[...], b1_ref[...])
        middle_ref[...] = middle
        low_ref[...] = middle.astype(jnp.bfloat16)
        level1_ref[...] = level
        scale1_ref[...] = scale
        total_ref[...] = jnp.zeros_like(total_ref)

    inner = mm(low_ref[...], square(e_ref)) + eb_ref[...]
    active, slope = gelu_parts(inner)
    active = active.astype(jnp.bfloat16)
    active_ref[...] = active
    slope_ref[...] = slope.astype(jnp.bfloat16)
    total_ref[...] += mm(active, square(s_ref))

    @pl.when(step == pl.num_programs(0) - 1)
    def _():
        result, level, scale = norm_rows(middle_ref[...] + (total_ref[...] + sb_ref[...]), g2_ref[...], b2_ref[...])
        result_ref[...] = result
        result_low_ref[...] = result.astype(jnp.bfloat16)
        level2_ref[...] = level
        scale2_ref[...] = scale


def feed_forward(hidden, mixed, attn_whole, feed_whole, first, place, vectors):
    rows = hidden.shape[0]
    shards = attn_whole.shape[0]
    depth = D // shards
    parts = FF // D
    row = pl.BlockSpec((1, D), lambda j: (0, 0))
    flat = pl.BlockSpec((rows, D), lambda j: (0, 0))
    column = pl.BlockSpec((rows, 1), lambda j: (0, 0))
    tile = pl.BlockSpec((rows, D), lambda j: (0, j))
    o_bias, gain_one, bias_one, expand_bias, shrink_bias, gain_two, bias_two = [v.reshape(1, -1) for v in vectors]

    def shape(width, dtype):
        return jax.ShapeDtypeStruct((rows, width), dtype)

    return pl.pallas_call(
        feed_kernel,
        grid=(parts,),
        in_specs=[
            flat,
            flat,
            pl.BlockSpec((shards, depth, D), lambda j: (0, place + 3, 0)),
            pl.BlockSpec((shards, depth, D), lambda j: (0, first + j, 0)),
            pl.BlockSpec((shards // parts, parts * depth, D), lambda j: (j, first // parts + 1, 0)),
            row, row, row,
            pl.BlockSpec((1, D), lambda j: (0, j)),
            row, row, row,
        ],
        out_specs=[flat, flat, column, tile, tile, flat, flat, flat, column],
        out_shape=[
            shape(D, jnp.bfloat16), shape(D, jnp.float32), shape(1, jnp.float32),
            shape(FF, jnp.bfloat16), shape(FF, jnp.bfloat16),
            shape(D, jnp.float32), shape(D, jnp.bfloat16), shape(D, jnp.float32), shape(1, jnp.float32),
        ],
        scratch_shapes=[pltpu.VMEM((rows, D), jnp.float32)] * 2,
        cost_estimate=SMALL_COST,
        compiler_params=pltpu.CompilerParams(vmem_limit_bytes=VMEM, dimension_semantics=("arbitrary",)),
        name="feed_forward",
    )(hidden, mixed, attn_whole, feed_whole, feed_whole, o_bias, gain_one, bias_one, expand_bias, shrink_bias, gain_two, bias_two)


def row_sum(values):
    return jnp.sum(values, 0, keepdims=True)


def feed_back_kernel(arrivals, base, *refs):
    if base:
        refs = refs[1:]
    grad_ref = refs[0]
    extra = refs[1 : 1 + arrivals]
    (
        level2_ref, scale2_ref, g2_ref, slope_ref, active_ref, low_ref, e_ref, s_ref, level1_ref, scale1_ref, g1_ref, wo_ref,
        sum_ref, branch_ref, mixed_ref, vec_ref, eb_ref, chunk_ref,
        outer_ref, turned_ref, total_ref, e_slot, s_slot, e_sem, s_sem,
    ) = refs[1 + arrivals :]
    step = pl.program_id(0)
    last = pl.num_programs(0) - 1
    slot = lax.rem(step, 2)
    shards, depth = e_slot.shape[1:3]
    group = s_slot.shape[1]

    @pl.when(step == 0)
    def _():
        grad = grad_ref[...]
        for ref in extra:
            grad = grad + ref[...].astype(jnp.float32)
        level = level2_ref[...]
        total = norm_rows_back(grad, level, scale2_ref[...], g2_ref[...])
        outer = total.astype(jnp.bfloat16)
        outer_ref[...] = outer
        total_ref[...] = total
        vec_ref[3:4, :] = row_sum(outer.astype(jnp.float32))
        vec_ref[4:5, :] = row_sum(grad * level)
        vec_ref[5:6, :] = row_sum(grad)
        turned_ref[...] = turned(low_ref[...])

    def copies(at, index):
        e_copy = pltpu.make_async_copy(
            e_slot.at[at], chunk_ref.at[:, pl.ds(base + index * depth, depth), :], e_sem.at[at]
        )
        s_copy = pltpu.make_async_copy(
            s_slot.at[at],
            chunk_ref.at[pl.ds(index * group, group), pl.ds(base + (last + 1) * depth, (last + 1) * depth), :],
            s_sem.at[at],
        )
        return e_copy, s_copy

    @pl.when(step >= 2)
    def _():
        for copy in copies(slot, step - 2):
            copy.wait()

    outer = outer_ref[...]
    inner = (mm(outer, square(s_ref), NT) * slope_ref[...].astype(jnp.float32)).astype(jnp.bfloat16)
    eb_ref[...] = row_sum(inner.astype(jnp.float32))
    total_ref[...] += mm(inner, square(e_ref), NT)
    e_slot[slot] = mm(turned_ref[...], inner).astype(jnp.bfloat16).reshape(shards, depth, D)
    s_slot[slot] = mm(turned(active_ref[...]), outer).astype(jnp.bfloat16).reshape(group, (last + 1) * depth, D)
    for copy in copies(slot, step):
        copy.start()

    @pl.when(step == last)
    def _():
        grad = total_ref[...]
        level = level1_ref[...]
        total = norm_rows_back(grad, level, scale1_ref[...], g1_ref[...])
        branch = total.astype(jnp.bfloat16)
        sum_ref[...] = total
        branch_ref[...] = branch
        vec_ref[0:1, :] = row_sum(branch.astype(jnp.float32))
        vec_ref[1:2, :] = row_sum(grad * level)
        vec_ref[2:3, :] = row_sum(grad)
        vec_ref[6:8, :] = jnp.zeros((2, D), jnp.float32)
        mixed_ref[...] = mm(branch, square(wo_ref), NT).astype(jnp.bfloat16)
        for index in (last - 1, last):
            for copy in copies(lax.rem(index, 2), index):
                copy.wait()


def feed_back(grads, cache, attn_whole, feed_whole, first, place, gain_one, gain_two, chunks):
    level1, scale1, low, slope, active, level2, scale2 = cache
    rows = low.shape[0]
    shards = attn_whole.shape[0]
    depth = D // shards
    parts = FF // D
    flat = pl.BlockSpec((rows, D), lambda j: (0, 0))
    row = pl.BlockSpec((1, D), lambda j: (0, 0))
    column = pl.BlockSpec((rows, 1), lambda j: (0, 0))
    tile = pl.BlockSpec((rows, D), lambda j: (0, j))
    return pl.pallas_call(
        functools.partial(feed_back_kernel, len(grads) - 1, 0 if chunks is None else 4 * depth),
        grid=(parts,),
        in_specs=[pl.BlockSpec(memory_space=pl.ANY)] * (chunks is not None)
        + [flat] * len(grads)
        + [
            flat, column, row, tile, tile, flat,
            pl.BlockSpec((shards, depth, D), lambda j: (0, first + j, 0)),
            pl.BlockSpec((shards // parts, parts * depth, D), lambda j: (j, first // parts + 1, 0)),
            flat, column, row,
            pl.BlockSpec((shards, depth, D), lambda j: (0, place + 3, 0)),
        ],
        out_specs=[
            flat, flat, flat,
            pl.BlockSpec((8, D), lambda j: (0, 0)),
            pl.BlockSpec((1, D), lambda j: (0, j)),
            pl.BlockSpec(memory_space=pl.ANY),
        ],
        out_shape=[
            jax.ShapeDtypeStruct((rows, D), jnp.float32),
            jax.ShapeDtypeStruct((rows, D), jnp.bfloat16),
            jax.ShapeDtypeStruct((rows, D), jnp.bfloat16),
            jax.ShapeDtypeStruct((8, D), jnp.float32),
            jax.ShapeDtypeStruct((1, FF), jnp.float32),
            jax.ShapeDtypeStruct((shards, (4 * (chunks is not None) + 2 * parts) * depth, D), jnp.bfloat16),
        ],
        input_output_aliases={} if chunks is None else {0: 5},
        scratch_shapes=[
            pltpu.VMEM((rows, D), jnp.bfloat16),
            pltpu.VMEM((D, rows), jnp.bfloat16),
            pltpu.VMEM((rows, D), jnp.float32),
            pltpu.VMEM((2, shards, depth, D), jnp.bfloat16),
            pltpu.VMEM((2, shards // parts, parts * depth, D), jnp.bfloat16),
            pltpu.SemaphoreType.DMA((2,)),
            pltpu.SemaphoreType.DMA((2,)),
        ],
        cost_estimate=SMALL_COST,
        compiler_params=pltpu.CompilerParams(vmem_limit_bytes=VMEM, dimension_semantics=("arbitrary",)),
        name="feed_back",
    )(
        *([] if chunks is None else [chunks]), *grads, level2, scale2, gain_two.reshape(1, D), slope, active, low, feed_whole, feed_whole,
        level1, scale1, gain_one.reshape(1, D), attn_whole,
    )


def entry_back_kernel(blocks, sum_ref, dq_ref, *refs):
    keys, values = refs[0 : 2 * blocks : 2], refs[1 : 2 * blocks : 2]
    wq_ref, wk_ref, wv_ref = refs[2 * blocks : 2 * blocks + 3]
    outs = refs[2 * blocks + 3 :]
    key_w, value_w = square(wk_ref), square(wv_ref)
    for j in range(blocks):
        back = mm(keys[j][...], key_w, NT) + mm(values[j][...], value_w, NT)
        if j == 0:
            outs[0][...] = sum_ref[...] + mm(dq_ref[...], square(wq_ref), NT) + back
        else:
            outs[j][...] = back.astype(jnp.bfloat16)


def entry_back(grad_sum, dq, pairs, attn_whole, place):
    rows = dq.shape[0]
    shards = attn_whole.shape[0]
    flat = pl.BlockSpec((rows, D), lambda i: (0, 0))
    weights = [pl.BlockSpec((shards, D // shards, D), lambda i, m=m: (0, place + m, 0)) for m in range(3)]
    return pl.pallas_call(
        functools.partial(entry_back_kernel, len(pairs) // 2),
        grid=(1,),
        in_specs=[flat] * (2 + len(pairs)) + weights,
        out_specs=[flat] * (len(pairs) // 2),
        out_shape=[
            jax.ShapeDtypeStruct((rows, D), jnp.float32 if j == 0 else jnp.bfloat16) for j in range(len(pairs) // 2)
        ],
        cost_estimate=SMALL_COST,
        compiler_params=pltpu.CompilerParams(vmem_limit_bytes=VMEM, dimension_semantics=("arbitrary",)),
        name="entry_back",
    )(grad_sum, dq, *pairs, attn_whole, attn_whole, attn_whole)


def attn_grads_kernel(blocks, *refs):
    entries = refs[:blocks]
    dq_ref, mixed_ref, branch_ref = refs[blocks : blocks + 3]
    pairs = refs[blocks + 3 : 3 * blocks + 3]
    out_ref, vec_ref, slots, sem = refs[3 * blocks + 3 :]
    shards, depth = slots.shape[1:3]
    entry_turned = [turned(e[...]) for e in entries]

    def put(i, value):
        slots[i] = value.astype(jnp.bfloat16).reshape(shards, depth, D)
        pltpu.make_async_copy(slots.at[i], out_ref.at[:, pl.ds(i * depth, depth), :], sem.at[i]).start()

    put(0, mm(entry_turned[0], dq_ref[...]))
    put(1, functools.reduce(jnp.add, [mm(e, k[...]) for e, k in zip(entry_turned, pairs[0::2])]))
    put(2, functools.reduce(jnp.add, [mm(e, v[...]) for e, v in zip(entry_turned, pairs[1::2])]))
    put(3, mm(turned(mixed_ref[...]), branch_ref[...]))
    vec_ref[0:1, :] = row_sum(dq_ref[...].astype(jnp.float32))
    vec_ref[1:2, :] = functools.reduce(jnp.add, [row_sum(v[...].astype(jnp.float32)) for v in pairs[1::2]])
    vec_ref[2:8, :] = jnp.zeros((6, D), jnp.float32)
    for i in range(4):
        pltpu.make_async_copy(slots.at[i], out_ref.at[:, pl.ds(i * depth, depth), :], sem.at[i]).wait()


def attn_grads(entries, dq, mixed, branch, pairs, shards, room):
    blocks = len(entries)
    rows = dq.shape[0]
    flat = pl.BlockSpec((rows, D), lambda i: (0, 0))
    operands = list(entries) + [dq, mixed, branch] + list(pairs)
    return pl.pallas_call(
        functools.partial(attn_grads_kernel, blocks),
        grid=(1,),
        in_specs=[flat] * len(operands),
        out_specs=[pl.BlockSpec(memory_space=pl.ANY), pl.BlockSpec((8, D), lambda i: (0, 0))],
        out_shape=[
            jax.ShapeDtypeStruct((shards, room, D), jnp.bfloat16),
            jax.ShapeDtypeStruct((8, D), jnp.float32),
        ],
        scratch_shapes=[
            pltpu.VMEM((4, shards, D // shards, D), jnp.bfloat16),
            pltpu.SemaphoreType.DMA((4,)),
        ],
        cost_estimate=SMALL_COST,
        compiler_params=pltpu.CompilerParams(vmem_limit_bytes=VMEM, dimension_semantics=("arbitrary",)),
        name="attn_grads",
    )(*operands)


MESH = pl.DeviceIdType.MESH
AHEAD = 3
OTHER = 2
GATHER_AT = 5


def reduce_kernel(count, seqs, sizes, parts, rule, *refs):
    number = len(sizes)
    extra = 5 if parts else 1
    give_ref, basis = refs[number], refs[number + 1 : number + extra]
    take_ref = refs[2 * number + extra]
    refs = refs[:number] + refs[number + extra : 2 * number + extra] + refs[2 * number + extra + 1 :]
    sources = refs[:number]
    outs = refs[number : 2 * number]
    bits = count.bit_length() - 1
    turns = seqs.bit_length() - 1
    levels = bits + turns
    held = refs[2 * number : 2 * number + levels]
    send_sem, recv_sem, give_sem, take_sem = refs[2 * number + levels : 2 * number + levels + 4]
    rest = refs[2 * number + levels + 4 :]
    me = lax.axis_index("shard")
    place = lax.axis_index("seq")

    def across(index, bit):
        return index + (1 - 2 * ((index // 2**bit) % 2)) * 2**bit

    partners = [{"shard": across(me, b)} for b in range(bits)] + [{"seq": across(place, t)} for t in range(turns)]
    others = [{"shard": lax.rem(me + k, count)} for k in range(1, count)]
    greeted = others + partners[bits:]
    barrier = pltpu.get_barrier_semaphore()
    for partner in greeted:
        pl.semaphore_signal(barrier, inc=1, device_id=partner, device_id_type=MESH)
    pl.semaphore_wait(barrier, len(greeted))

    pieces = []
    offset = 0
    for source, out, (rows, cut) in zip(sources, outs, sizes):
        for start in range(0, rows, cut):
            pieces.append((source, out, start, offset + start, cut))
        offset += rows
    orders = [list(range(bits)), list(range(bits))]
    if bits > 2:
        orders[1] = [0] + list(range(2, bits)) + [1]
    flights = {}

    def moves(piece, level):
        order = orders[1 if piece % 5 == OTHER else 0]
        if level >= bits:
            return [(0, 0)], partners[level]
        bit = order[level]
        left = sorted(order[level:])
        low = 2 ** left.index(bit)
        side = (me // 2**bit) % 2
        pairs = []
        for j in range(2 ** (bits - level - 1)):
            base = (j // low) * 2 * low + j % low
            pairs.append((base + side * low, base + (1 - side) * low))
        return pairs, partners[bit]

    def data(piece, level, index):
        source, _, start, spot, cut = pieces[piece]
        if level == 0:
            return source.at[index, pl.ds(start, cut)]
        return held[level - 1].at[index, pl.ds(spot, cut)]

    def launch(piece, level):
        pairs, partner = moves(piece, level)
        _, _, _, spot, cut = pieces[piece]
        copies = []
        for j, (_, sent) in enumerate(pairs):
            copies.append(
                pltpu.make_async_remote_copy(
                    src_ref=data(piece, level, sent),
                    dst_ref=held[level].at[j, pl.ds(spot, cut)],
                    send_sem=send_sem.at[piece, level, j],
                    recv_sem=recv_sem.at[piece, level, j],
                    device_id=partner,
                    device_id_type=MESH,
                )
            )
        for copy in copies:
            copy.start()
        flights[piece, level] = copies

    def absorb(piece, level):
        pairs, _ = moves(piece, level)
        _, out, start, spot, cut = pieces[piece]
        for j, (kept, _) in enumerate(pairs):
            flights[piece, level][j].wait()
            mine, other = data(piece, level, kept)[...], held[level][j, pl.ds(spot, cut)]
            if level == levels - 1:
                out[pl.ds(start, cut)] = mine.astype(jnp.float32) + other.astype(jnp.float32)
            else:
                held[level][j, pl.ds(spot, cut)] = mine + other

    def trade_all(source, target_ref, send, recv):
        copies = [pltpu.make_async_copy(source.at[me], target_ref.at[me], send.at[0])]
        for k in range(1, count):
            target = lax.rem(me + k, count)
            copies.append(
                pltpu.make_async_remote_copy(
                    src_ref=source.at[target],
                    dst_ref=target_ref.at[me],
                    send_sem=send.at[k],
                    recv_sem=recv.at[k],
                    device_id={"shard": target},
                    device_id_type=MESH,
                )
            )
        for copy in copies:
            copy.start()
        return copies

    def wait_all(copies):
        for copy in copies:
            copy.wait()

    if parts:
        left_ref, first_ref, second_ref, right_ref = basis
        held_rows, whole, turned_rows, near_send, near_recv, back_send, back_recv = rest
        part = lax.rem(me, parts)
        columns = give_ref.shape[2]

        def gather_near():
            wait_all(away[0])
            whole[part] = held_rows[...].reshape(D, columns)
            copies = []
            for j in range(1, parts):
                copies.append(
                    pltpu.make_async_remote_copy(
                        src_ref=whole.at[part],
                        dst_ref=whole.at[part],
                        send_sem=near_send.at[j],
                        recv_sem=near_recv.at[j],
                        device_id={"shard": me - part + lax.rem(part + j, parts)},
                        device_id_type=MESH,
                    )
                )
                copies[-1].start()
            away.append(copies)

        def own_columns(values):
            kept = values[:, 0:columns]
            for j in range(1, parts):
                kept = jnp.where(part == j, values[:, j * columns : (j + 1) * columns], kept)
            return kept.astype(jnp.bfloat16)

        def turn():
            wait_all(away[1])
            grad = jnp.concatenate([whole[j] for j in range(parts)], 1)
            left, right = left_ref[...], right_ref[...]
            rotated = mm(mm(left, grad).astype(jnp.bfloat16), right)
            share = rule(first_ref[...].astype(jnp.float32), second_ref[...].astype(jnp.float32), rotated)[0]
            back = own_columns(mm(share.astype(jnp.bfloat16), right, NT))
            turned_rows[:, 0] = own_columns(rotated).reshape(count, -1, columns)
            turned_rows[:, 1] = mm(turned(left), back).astype(jnp.bfloat16).reshape(count, -1, columns)
            away.append(trade_all(turned_rows, take_ref, back_send, back_recv))

        away = [trade_all(give_ref, held_rows, give_sem, take_sem)]
        between = {GATHER_AT: gather_near, GATHER_AT + 2: turn}
    else:
        away = [trade_all(give_ref, take_ref, give_sem, take_sem)]
        between = {}
    delay = [0, 1] + [1 + AHEAD * level for level in range(1, levels)]
    for wave in range(len(pieces) + delay[-1]):
        if wave in between:
            between[wave]()
        for level in range(levels, -1, -1):
            piece = wave - delay[level]
            if 0 <= piece < len(pieces):
                if level > 0:
                    absorb(piece, level - 1)
                if level < levels:
                    launch(piece, level)
    wait_all(away[-1])


def reduce_chunks(mesh_sizes, cuts, chunks, give, parts, rule, basis):
    count, seqs = mesh_sizes
    bits, turns = count.bit_length() - 1, seqs.bit_length() - 1
    lanes = chunks[0].shape[2]
    sizes = [(c.shape[1], cut) for c, cut in zip(chunks, cuts)]
    total = sum(rows for rows, _ in sizes)
    number = sum(rows // cut for rows, cut in sizes)
    slots = [2 ** (bits - 1 - level) for level in range(bits)] + [1] * turns
    spec = pl.BlockSpec(memory_space=pltpu.VMEM)
    scratch = [pltpu.VMEM((n, total, lanes), jnp.bfloat16) for n in slots]
    scratch += [pltpu.SemaphoreType.DMA((number, bits + turns, count // 2))] * 2
    scratch += [pltpu.SemaphoreType.DMA((count,))] * 2
    taken = give.shape
    if parts:
        _, depth, columns = give.shape
        taken = (count, 2, depth, columns)
        scratch += [
            pltpu.VMEM(give.shape, jnp.bfloat16),
            pltpu.VMEM((parts, D, columns), jnp.bfloat16),
            pltpu.VMEM(taken, jnp.bfloat16),
        ]
        scratch += [pltpu.SemaphoreType.DMA((parts,))] * 2 + [pltpu.SemaphoreType.DMA((count,))] * 2
    return pl.pallas_call(
        functools.partial(reduce_kernel, count, seqs, sizes, parts, rule),
        in_specs=[spec] * (len(chunks) + 1 + len(basis)),
        out_specs=[spec] * (len(chunks) + 1),
        out_shape=[jax.ShapeDtypeStruct(c.shape[1:], jnp.float32) for c in chunks]
        + [jax.ShapeDtypeStruct(taken, give.dtype)],
        scratch_shapes=scratch,
        cost_estimate=SMALL_COST,
        compiler_params=pltpu.CompilerParams(collective_id=0, has_side_effects=True, vmem_limit_bytes=VMEM),
        name="reduce_chunks",
    )(*chunks, give, *basis)


def finish_kernel(rules, parts, shapes, *refs):
    number = len(shapes)
    small_ref, conv_sum_ref, take_ref = refs[:3]
    ins = [refs[3 + 3 * i : 6 + 3 * i] for i in range(number + 3)]
    outs = [refs[3 * number + 12 + 3 * i : 3 * number + 15 + 3 * i] for i in range(number + 3)]
    conv_rule, turned_rule, vector_rule, small_rules = rules

    def put(at, values):
        for ref, value in zip(outs[at], values):
            ref[...] = value

    put(0, conv_rule(ins[0][0][...], conv_sum_ref[...].T, ins[0][1][...], ins[0][2][...]))
    for m in range(ins[1][0].shape[0]):
        rotated = jnp.concatenate([take_ref[m * parts + j, 0] for j in range(parts)], 1).astype(jnp.float32)
        update = jnp.concatenate([take_ref[m * parts + j, 1] for j in range(parts)], 1).astype(jnp.float32)
        weight, first, second = turned_rule(ins[1][0][m], update, ins[1][1][m], ins[1][2][m], rotated)
        outs[1][0][m] = weight
        outs[1][1][m] = first
        outs[1][2][m] = second
    taps = small_ref.shape[1]
    start = 0
    for i, (depth, width) in enumerate(shapes):
        count = -(-width // taps)
        grad = jnp.concatenate([small_ref[start + j * depth : start + (j + 1) * depth, :] for j in range(count)], 1)
        start += count * depth
        put(3 + i, small_rules[i](ins[3 + i][0][...], grad[:, :width], ins[3 + i][1][...], ins[3 + i][2][...]))
    size = ins[2][0].shape[1]
    count = -(-size // taps)
    grad = jnp.concatenate([small_ref[start + j : start + j + 1, :] for j in range(count)], 1)[:, :size]
    put(2, vector_rule(ins[2][0][...], grad, ins[2][1][...], ins[2][2][...]))


def finish(rules, parts, small_sum, conv_sum, take, conv, attention, vector, small):
    vector = tuple(v.reshape(1, -1) for v in vector)
    operands = list(conv) + list(attention) + list(vector) + [item for triple in small for item in triple]
    shapes = [triple[0].shape for triple in small]
    results = pl.pallas_call(
        functools.partial(finish_kernel, rules, parts, shapes),
        out_shape=[jax.ShapeDtypeStruct(item.shape, jnp.float32) for item in operands],
        cost_estimate=SMALL_COST,
        compiler_params=pltpu.CompilerParams(vmem_limit_bytes=VMEM),
        name="finish",
    )(small_sum, conv_sum, take, *operands)
    triples = [tuple(results[3 * i : 3 * i + 3]) for i in range(len(results) // 3)]
    triples[2] = tuple(v.reshape(-1) for v in triples[2])
    return triples


def swap_moves(count, step):
    return [(i, (i - step) % count) for i in range(count)]


def gather_ring(block):
    count = lax.axis_size("seq")
    return [block] + [lax.ppermute(block, "seq", swap_moves(count, step)) for step in range(1, count)]


def return_ring(blocks):
    count = lax.axis_size("seq")
    return [lax.ppermute(block, "seq", swap_moves(count, -step)) for step, block in enumerate(blocks) if step > 0]


def seq_sum(values):
    if lax.axis_size("seq") > 2:
        return lax.psum(values, "seq").astype(jnp.float32)
    other = lax.ppermute(values, "seq", [(0, 1), (1, 0)])
    return values.astype(jnp.float32) + other.astype(jnp.float32)


def lowered(values):
    return values.astype(jnp.bfloat16)


def bdot(left_side, right_side):
    return jnp.dot(left_side, right_side, preferred_element_type=jnp.float32)


def turned_dot(left_side, right_side):
    return lax.dot_general(left_side, right_side, NT, preferred_element_type=jnp.float32)


def rows_dot(left_side, right_side):
    return lax.dot_general(left_side, right_side, (((0,), (0,)), ((), ())), preferred_element_type=jnp.float32)


def fdot(left_side, right_side):
    return jnp.dot(left_side, right_side, precision=lax.Precision.HIGHEST, preferred_element_type=jnp.float32)


def column_sum(values):
    return jnp.sum(values.astype(jnp.float32), 0, keepdims=True)


def norm_forward(values, gain_row, bias_row):
    centred = values - jnp.mean(values, -1, keepdims=True)
    spread = jnp.mean(centred * centred, -1, keepdims=True)
    scale = lax.rsqrt(spread + norm_epsilon)
    level = centred * scale
    return level * gain_row + bias_row, (level, scale, gain_row)


def norm_vectors(grad, kept):
    level = kept[0]
    return jnp.sum(grad * level, 0, keepdims=True), jnp.sum(grad, 0, keepdims=True)


def norm_backward(grad, kept):
    level, scale, gain_row = kept
    inside = grad * gain_row
    centred = inside - jnp.mean(inside, -1, keepdims=True) - level * jnp.mean(inside * level, -1, keepdims=True)
    return (scale * centred,) + norm_vectors(grad, kept)


def unit_rows(values):
    return values * lax.rsqrt(jnp.sum(values * values, -1, keepdims=True) + unit_epsilon)


def vector_pieces(vector):
    widths = [CIN, CIN, D, D, D, D, D] + [D, D, D, D, D, FF, D, D, D] * LAYERS + [PROJ, PROJ]
    pieces = []
    offset = 0
    for width in widths:
        pieces.append(vector[offset : offset + width])
        offset = offset + width
    return pieces


def with_halo(block, width):
    count = lax.axis_size("seq")
    forward = [(i, i + 1) for i in range(count - 1)]
    backward = [(i + 1, i) for i in range(count - 1)]
    low = lax.ppermute(block[:, block.shape[1] - width :], "seq", forward)
    high = lax.ppermute(block[:, :width], "seq", backward)
    return jnp.concatenate([low, block, high], axis=1)


def layer_forward(hidden, hidden_low, weights, pieces, clip_count, waiting):
    attn_w, expand_w, shrink_w = weights
    q_bias, v_bias, o_bias, gain_one, bias_one, expand_bias, shrink_bias, gain_two, bias_two = pieces
    entries = gather_ring(hidden_low)
    query = lowered(bdot(entries[0], attn_w[:, :D]) + q_bias)
    keys = [lowered(bdot(entry, attn_w[:, D : 2 * D])) for entry in entries]
    values = [lowered(bdot(entry, attn_w[:, 2 * D : 3 * D]) + v_bias) for entry in entries]
    mixed, stat = attend(query, keys, values, clip_count)
    if waiting is not None:
        mixed, waiting = fence(mixed, waiting)
    branch = bdot(mixed, attn_w[:, 3 * D :]) + o_bias
    middle, middle_kept = norm_forward(hidden + branch, gain_one, bias_one)
    middle_low = lowered(middle)
    inner = bdot(middle_low, expand_w) + expand_bias
    activated, slope = gelu_parts(inner)
    active_low = lowered(activated)
    slope_low = lowered(slope)
    outer = bdot(active_low, shrink_w) + shrink_bias
    result, final_kept = norm_forward(middle + outer, gain_two, bias_two)
    cache = (entries, query, keys, values, mixed, stat, middle_kept, middle_low, slope_low, active_low, final_kept)
    return result, lowered(result), cache, waiting


def feed_backward(grad_out, cache, expand_w, shrink_w):
    middle_low, slope_low, active_low, final_kept = cache[7:]
    grad_sum, grad_gain, grad_bias = norm_backward(grad_out, final_kept)
    grad_outer = lowered(grad_sum)
    grad_shrink = lowered(rows_dot(active_low, grad_outer))
    grad_inner = lowered(slope_low.astype(jnp.float32) * turned_dot(grad_outer, shrink_w))
    grad_expand = lowered(rows_dot(middle_low, grad_inner))
    grad_middle = grad_sum + turned_dot(grad_inner, expand_w)
    vectors = [column_sum(grad_inner), column_sum(grad_outer), grad_gain, grad_bias]
    return grad_middle, grad_expand, grad_shrink, vectors


def attend_backward(grad_middle, cache, attn_w, clip_count, *waiting):
    entries, query, keys, values, mixed, stat, middle_kept = cache[:7]
    grad_sum, grad_gain, grad_bias = norm_backward(grad_middle, middle_kept)
    grad_branch = lowered(grad_sum)
    grad_mixed = lowered(turned_dot(grad_branch, attn_w[:, 3 * D :]))
    results = attend_back(query, grad_mixed, stat, keys, values, clip_count)
    results, grad_branch, *waiting = fence(results, grad_branch, *waiting)
    grad_query, grad_keys, grad_values = results[0], results[1::2], results[2::2]
    back = [
        turned_dot(dk, attn_w[:, D : 2 * D]) + turned_dot(dv, attn_w[:, 2 * D : 3 * D])
        for dk, dv in zip(grad_keys, grad_values)
    ]
    arrived = return_ring([lowered(block) for block in back])
    grad_hidden = grad_sum + turned_dot(grad_query, attn_w[:, :D]) + back[0]
    for block in arrived:
        grad_hidden = grad_hidden + block.astype(jnp.float32)
    grads = [
        lowered(rows_dot(entries[0], grad_query)),
        lowered(sum(rows_dot(entry, dk) for entry, dk in zip(entries, grad_keys))),
        lowered(sum(rows_dot(entry, dv) for entry, dv in zip(entries, grad_values))),
        lowered(rows_dot(mixed, grad_branch)),
    ]
    vectors = [
        column_sum(grad_query),
        sum(column_sum(dv) for dv in grad_values),
        column_sum(grad_branch),
        grad_gain,
        grad_bias,
    ]
    return grad_hidden, grads, vectors, waiting


def fused_forward(hidden, hidden_low, weights, pieces, clip_count, waiting):
    attn_whole, feed_whole, first = weights
    place = 0
    none = jnp.zeros_like(pieces[0])
    entries = [hidden_low]
    packs = [project(hidden_low, attn_whole, place, [pieces[0], none, pieces[1]])]
    for entry in gather_ring(hidden_low)[1:]:
        entries.append(entry)
        packs.append(project(entry, attn_whole, place + 1, [none, pieces[1]]))
    query = (packs[0], 0)
    keys = [(pack, 1 if j == 0 else 0) for j, pack in enumerate(packs)]
    values = [(pack, 2 if j == 0 else 1) for j, pack in enumerate(packs)]
    mixed, stat = attend(query, keys, values, clip_count)
    if waiting is not None:
        mixed, waiting = fence(mixed, waiting)
    low, level1, scale1, active, slope, result, result_low, level2, scale2 = feed_forward(
        hidden, mixed, attn_whole, feed_whole, first, place, pieces[2:]
    )
    cache = (entries, query, keys, values, mixed, stat, (level1, scale1, low, slope, active, level2, scale2))
    return result, result_low, cache, waiting


def fused_backward(grads, cache, weights, pieces, clip_count, chunks, room, waiting):
    attn_whole, feed_whole, first = weights
    entries, query, keys, values, mixed, stat, kept = cache
    shards = lax.axis_size("shard")
    grad_sum, branch, grad_mixed, sums, grad_expand_bias, feed_chunks = feed_back(
        grads, kept, attn_whole, feed_whole, first, 0, pieces[3], pieces[7], chunks
    )
    if waiting is not None:
        grad_mixed, held = fence(grad_mixed, waiting[1])
        waiting = waiting[0](held)
    results = attend_back(query, grad_mixed, stat, keys, values, clip_count)
    if waiting is not None:
        results, waiting = fence(results, waiting)
    backs = entry_back(grad_sum, results[0], results[1:], attn_whole, 0)
    results, backs, branch = fence(results, backs, branch)
    arrived = return_ring(backs)
    attn_chunks, more = attn_grads(entries, results[0], mixed, branch, results[1:], shards, room)
    arrived, more = fence(arrived, more)
    vectors = [more[0:1], more[1:2], sums[0:1], sums[1:2], sums[2:3], grad_expand_bias, sums[3:4], sums[4:5], sums[5:6]]
    return [backs[0]] + arrived, feed_chunks, attn_chunks, vectors, waiting


def plain_backward(grads, cache, weights, pieces, clip_count, chunks, room, waiting):
    attn_w, expand_w, shrink_w = weights
    shards = lax.axis_size("shard")
    grad = grads[0]
    for part in grads[1:]:
        grad = grad + part.astype(jnp.float32)
    grad_middle, grad_expand, grad_shrink, feed_vectors = feed_backward(grad, cache, expand_w, shrink_w)
    rest = [] if waiting is None else [waiting[0](waiting[1])]
    grad_hidden, attn_list, attn_vectors, rest = attend_backward(grad_middle, cache, attn_w, clip_count, *rest)
    blocks = [] if chunks is None else [chunks]
    blocks += [grad_expand[:, j * D : (j + 1) * D].reshape(shards, -1, D) for j in range(FF // D)]
    blocks.append(grad_shrink.reshape(shards, -1, D))
    attn_chunks = jnp.concatenate([item.reshape(shards, -1, D) for item in attn_list], 1)
    vectors = attn_vectors + feed_vectors
    return [grad_hidden], jnp.concatenate(blocks, 1), attn_chunks, vectors, rest[0] if rest else None


def adam_update(weight, grad, first, second, rate, decay):
    first = beta_one * first + (1 - beta_one) * grad
    second = beta_two * second + (1 - beta_two) * grad * grad
    share_fraction = (
        first / (1 - beta_one**STEP) / (jnp.sqrt(second / (1 - beta_two**STEP)) + adam_epsilon)
    )
    return (weight - rate * (share_fraction + decay * weight), first, second)


def matrix_rule(weight, grad, first, second):
    return adam_update(weight, grad, first, second, rate_matrix, decay_rate)


def target_rule(weight, grad, first, second):
    return adam_update(weight, grad, first, second, rate_target, decay_rate)


def codebook_rule(weight, grad, first, second):
    return adam_update(weight, grad, first, second, rate_codebook, decay_rate)


def vector_rule(weight, grad, first, second):
    return adam_update(weight, grad, first, second, rate_vector, 0.0)


def rotated_adam(first, second, grad):
    first = beta_rotated * first + (1 - beta_rotated) * grad
    second = beta_rotated * second + (1 - beta_rotated) * grad * grad
    share = first / (1 - beta_rotated**STEP) / (jnp.sqrt(second / (1 - beta_rotated**STEP)) + adam_epsilon)
    return share, first, second


def attention_rule(weight, update, first, second, rotated):
    _, first, second = rotated_adam(first, second, rotated)
    return weight - rate_rotated * update, first, second


def gather_rows(block):
    whole = lax.all_gather(block, "shard", axis=0, tiled=True)
    return whole.reshape((-1,) + block.shape)


def pass_kernel(*refs):
    pass


def fence(*values):
    flat, tree = jax.tree.flatten(values)
    spec = pl.BlockSpec(memory_space=pl.ANY)
    flat = pl.pallas_call(
        pass_kernel,
        in_specs=[spec] * len(flat),
        out_specs=[spec] * len(flat),
        out_shape=[jax.ShapeDtypeStruct(v.shape, v.dtype) for v in flat],
        input_output_aliases={i: i for i in range(len(flat))},
        cost_estimate=SMALL_COST,
        name="fence",
    )(*flat)
    return jax.tree.unflatten(tree, flat)


def scatter_chunks(chunks):
    return lax.psum_scatter(chunks, "shard", scatter_dimension=0, tiled=False)


def trade(chunks):
    return lax.all_to_all(chunks, "shard", split_axis=0, concat_axis=0, tiled=True)


def on_device(
    features,
    time_mask,
    negatives,
    target_codes,
    feature_weight,
    feature_first,
    feature_second,
    conv_weight,
    conv_first,
    conv_second,
    attention_weight,
    attention_first,
    attention_second,
    left_basis_t,
    right_orthogonal_basis,
    expand_weight,
    expand_first,
    expand_second,
    shrink_weight,
    shrink_first,
    shrink_second,
    final_weight,
    final_first,
    final_second,
    target_weight,
    target_first,
    target_second,
    codebook_weight,
    codebook_first,
    codebook_second,
    vector_params,
    vector_first,
    vector_second,
):
    clip_count, frame_count = (features.shape[0], features.shape[1])
    row_count = clip_count * frame_count
    seq_count = lax.axis_size("seq")
    shards = lax.axis_size("shard")
    clip_frames = frame_count * seq_count
    taps = conv_weight.shape[0]
    small_items = [feature_weight, final_weight, target_weight, codebook_weight]

    def split_small(packed):
        blocks = []
        start = 0
        for item in small_items:
            depth, width = item.shape
            count = -(-width // taps)
            pieces = [packed[..., start + j * depth : start + (j + 1) * depth, :] for j in range(count)]
            blocks.append(jnp.concatenate(pieces, -1)[..., :width])
            start += count * depth
        size = vector_params.shape[0]
        count = -(-size // taps)
        vector = packed[..., start : start + count, :].reshape(packed.shape[:-2] + (-1,))[..., :size]
        return blocks, vector, packed[..., start + count, :2]

    parts = shards // (4 * LAYERS)
    rows = D // shards

    def own_attn(layer):
        return jnp.concatenate([lowered(attention_weight[4 * layer + i]) for i in range(4)])

    def own_feed(layer):
        expand_own = lowered(expand_weight[layer])
        return jnp.concatenate(
            [expand_own[:, j * D : (j + 1) * D] for j in range(FF // D)] + [lowered(shrink_weight[layer])]
        )

    first_all = gather_rows(pack_weights(conv_weight, small_items, vector_params, SMALL_ROWS))
    conv_w = first_all
    blocks, vector_low, _ = split_small(first_all[:, D:])
    feat_w, final_w, target_w, code_w = [block.reshape(-1, block.shape[-1]) for block in blocks]

    def cut_halves(block):
        number = block.shape[1]
        cut = block.reshape(4 * LAYERS, number, rows, parts, D // parts).transpose(0, 3, 1, 2, 4)
        return cut.reshape(shards, number, rows, D // parts)

    def spread_halves(block):
        return trade(cut_halves(block))

    def join_halves(got):
        number = got.shape[1]
        got = got.transpose(1, 0, 2, 3).reshape(number, D, D // parts)
        if parts != 2:
            groups = [[i * parts + j for j in range(parts)] for i in range(shards // parts)]
            return lax.all_gather(got, "shard", axis=2, tiled=True, axis_index_groups=groups)
        other = lax.ppermute(got, "shard", [(i, i ^ 1) for i in range(shards)])
        second = lax.axis_index("shard") % 2 == 1
        return jnp.concatenate([jnp.where(second, other, got), jnp.where(second, got, other)], 2)

    def plain_weights(attn_whole, feed_whole):
        blocks = [attn_whole[:, j * rows : (j + 1) * rows].reshape(D, D) for j in range(4)]
        columns = [feed_whole[:, j * rows : (j + 1) * rows].reshape(D, D) for j in range(FF // D)]
        shrink = feed_whole[:, FF // D * rows :].reshape(FF, D)
        return jnp.concatenate(blocks, 1), jnp.concatenate(columns, 1), shrink

    first_frame = lax.axis_index("seq") * frame_count
    ring_draws = (negatives - first_frame + clip_frames) % clip_frames
    counts = count_draws(ring_draws.transpose(0, 2, 1), clip_frames)
    held = jnp.stack([lowered(left_basis_t), lowered(attention_first), lowered(attention_second)], 1)
    counts, own_0 = fence(counts, jnp.concatenate([own_attn(0), own_feed(0)]))
    whole_0 = gather_rows(own_0)
    fused = rows % 16 == 0
    weights = [(whole_0, whole_0, 4) if fused else plain_weights(whole_0[:, : 4 * rows], whole_0[:, 4 * rows :])]

    pieces = vector_pieces(vector_low.reshape(-1).astype(jnp.float32))
    mask_on = (time_mask > 0).reshape(row_count, 1)
    feats = features.reshape(row_count, CIN).astype(jnp.float32)
    normed, norm_kept = norm_forward(feats, pieces[0], pieces[1])
    normed_low = lowered(normed)
    projected = bdot(normed_low, feat_w) + pieces[2]
    masked = jnp.where(mask_on, pieces[3][None, :], projected)
    padded = with_halo(lowered(masked).reshape(clip_count, frame_count, D), KW // 2)
    strip_rows = frame_count * clip_count // 16 // PACK
    strips = to_strips(padded, frame_count)
    conv_out = from_strips(conv_forward(strips, conv_w, 0, strip_rows, shards), clip_count) + pieces[4]
    conv_active, conv_slope = gelu_parts(conv_out)
    hidden, front_kept = norm_forward(masked + conv_active, pieces[5], pieces[6])

    hidden_low = lowered(hidden)
    codes = jnp.concatenate(gather_ring(target_codes), 1).reshape(clip_count * clip_frames, QGROUPS)
    width = PROJ // QGROUPS
    code_f = code_w.astype(jnp.float32)
    target_f = target_w.astype(jnp.float32)
    table = jnp.concatenate(
        [fdot(code_f[g * width : (g + 1) * width].T, target_f[g * width : (g + 1) * width]) for g in range(QGROUPS)]
    )
    choice = jnp.concatenate(
        [(codes[:, g : g + 1] == jnp.arange(CODES)[None, :]).astype(jnp.float32) for g in range(QGROUPS)], 1
    )
    raw_targets = fdot(choice, table) + pieces[-1]
    target_kept = lax.rsqrt(jnp.sum(raw_targets * raw_targets, -1, keepdims=True) + unit_epsilon)
    targets = raw_targets * target_kept
    forward = fused_forward if fused else layer_forward
    hidden, hidden_low, own_1 = fence(hidden, hidden_low, own_attn(1))
    attn_whole_1 = gather_rows(own_1)
    hidden, hidden_low, cache, own_1 = forward(hidden, hidden_low, weights[0], pieces[7:16], clip_count, own_feed(1))
    feed_whole_1 = gather_rows(own_1)
    caches = [cache]
    weights.append((attn_whole_1, feed_whole_1, 0) if fused else plain_weights(attn_whole_1, feed_whole_1))
    hidden, top_low, cache, (targets, target_kept) = forward(
        hidden, hidden_low, weights[1], pieces[16:25], clip_count, (targets, target_kept)
    )
    caches.append(cache)
    context, context_pull = jax.vjp(unit_rows, bdot(top_low, final_w) + pieces[-2])
    context_low = lowered(context).reshape(clip_count, frame_count, PROJ)

    counts = counts.astype(jnp.float32)
    targets_low = lowered(targets).reshape(clip_count, clip_frames, PROJ)
    similar = jnp.einsum("clp,cfp->clf", targets_low, context_low, preferred_element_type=jnp.float32)
    logits = similar / contrastive_sharpness
    place = jnp.arange(clip_frames)[:, None] == jnp.arange(frame_count)[None, :]
    own = place.astype(jnp.float32)[None]
    weight = counts + own
    largest = jnp.max(jnp.where(weight > 0, logits, -jnp.inf), 1, keepdims=True)
    power = weight * jnp.exp(jnp.where(weight > 0, logits - largest, 0.0))
    running_totals = jnp.sum(power, 1, keepdims=True)
    mask_as_floats = time_mask.astype(jnp.float32)
    own_logit = jnp.sum(own * logits, 1)
    row_loss = largest[:, 0] + jnp.log(running_totals[:, 0]) - own_logit
    loss_sum = jnp.sum(mask_as_floats * row_loss)
    mask_count = jnp.sum(mask_as_floats)
    derivative_multiplier = 1.0 / (clip_count * shards * clip_frames)
    grad_similar = lowered(
        mask_as_floats[:, None, :]
        * (power / running_totals - own)
        * (derivative_multiplier / contrastive_sharpness)
    )
    grad_context = jnp.einsum("clf,clp->cfp", grad_similar, targets_low, preferred_element_type=jnp.float32)
    grad_targets = jnp.einsum("clf,cfp->clp", grad_similar, context_low, preferred_element_type=jnp.float32)
    grad_targets = grad_targets.reshape(-1, PROJ)
    grad_raw = target_kept * (grad_targets - targets * jnp.sum(grad_targets * targets, -1, keepdims=True))
    grad_table = fdot(choice.T, grad_raw)
    tables = [grad_table[g * CODES : (g + 1) * CODES] for g in range(QGROUPS)]
    grad_target_w = jnp.concatenate([fdot(code_f[g * width : (g + 1) * width], tables[g]) for g in range(QGROUPS)])
    grad_codebook = jnp.concatenate(
        [fdot(target_f[g * width : (g + 1) * width], tables[g].T) for g in range(QGROUPS)]
    )
    grad_target_bias = column_sum(grad_raw)
    (grad_context_raw,) = context_pull(grad_context.reshape(row_count, PROJ))
    grad_context_low = lowered(grad_context_raw)
    grad_final_w = rows_dot(top_low, grad_context_low)
    grad_final_bias = column_sum(grad_context_low)
    grad_hidden = turned_dot(grad_context_low, final_w)

    columns = D // parts
    group = lax.axis_index("shard") // parts
    right_low = lowered(lax.dynamic_index_in_dim(right_orthogonal_basis, group, 0, keepdims=False))

    def rotate(whole_grad):
        left_low, first_low, second_low = traded[0], traded[1], traded[2]
        rotated = bdot(lowered(bdot(left_low, whole_grad)), right_low)
        direction = rotated_adam(first_low.astype(jnp.float32), second_low.astype(jnp.float32), rotated)[0]
        half_back = lowered(turned_dot(lowered(direction), right_low))
        part_start = (lax.axis_index("shard") % parts) * columns
        rotated_part = lax.dynamic_slice_in_dim(lowered(rotated), part_start, columns, 1)
        update_part = lowered(rows_dot(left_low, lax.dynamic_slice_in_dim(half_back, part_start, columns, 1)))
        sent = jnp.stack([rotated_part.reshape(shards, rows, columns), update_part.reshape(shards, rows, columns)], 1)
        return sent

    backward = fused_backward if fused else plain_backward
    grads, chunks, attn_chunks, vectors_1, _ = backward(
        [grad_hidden], caches[1], weights[1], pieces[16:25], clip_count, None, 4 * rows + 8 * rows * fused, None
    )
    (chunks,) = fence(chunks)
    sum_feed_1 = scatter_chunks(chunks)
    grads, chunks, attn_chunks, vectors_0, traded = backward(
        grads, caches[0], weights[0], pieces[7:16], clip_count, attn_chunks, 4 * rows, (spread_halves, held)
    )
    (chunks,) = fence(chunks)
    sum_feed_0 = scatter_chunks(chunks)
    (attn_chunks,) = fence(attn_chunks)
    sum_attn = scatter_chunks(attn_chunks)
    grad_hidden = grads[0]
    for part in grads[1:]:
        grad_hidden = grad_hidden + part.astype(jnp.float32)
    grad_sum, grad_gain_enc, grad_bias_enc = norm_backward(grad_hidden, front_kept)
    grad_conv_low = lowered(grad_sum * conv_slope)
    grad_strips = to_strips(with_halo(grad_conv_low.reshape(clip_count, frame_count, D), KW // 2), frame_count)
    conv_chunks = conv_weight_grad(strips, grad_strips, strip_rows, shards)
    grad_strips, conv_chunks, sum_feed_1 = fence(grad_strips, conv_chunks, sum_feed_1)
    grad_back = conv_input_grad(grad_strips, conv_w, 0, strip_rows, shards)
    traded = join_halves(traded)
    sum_feed_1 = seq_sum(sum_feed_1)
    grad_back, sum_feed_1, sum_feed_0, traded = fence(grad_back, sum_feed_1, sum_feed_0, traded)
    grad_masked = grad_sum + from_strips(grad_back, clip_count)
    grad_embedding = jnp.sum(jnp.where(mask_on, grad_masked, 0.0), 0, keepdims=True)
    grad_projected = lowered(jnp.where(mask_on, 0.0, grad_masked))
    grad_feat_w = rows_dot(normed_low, grad_projected)
    grad_gain_feat, grad_bias_feat = norm_vectors(turned_dot(grad_projected, feat_w), norm_kept)
    vector_grads = [
        grad_gain_feat,
        grad_bias_feat,
        column_sum(grad_projected),
        grad_embedding,
        column_sum(grad_conv_low),
        grad_gain_enc,
        grad_bias_enc,
    ]
    vector_grads += vectors_0 + vectors_1
    vector_grads += [grad_final_bias, grad_target_bias]
    extra = jnp.pad(jnp.stack([loss_sum, mask_count])[None], ((0, 0), (0, 126)))
    small_grads = [grad_feat_w, grad_final_w, grad_target_w, grad_codebook]
    small_chunks = pack_grads(small_grads, vector_grads, extra, shards, SMALL_ROWS, taps)
    sum_feed_0 = seq_sum(sum_feed_0)
    small_chunks, sum_attn, sum_feed_0 = fence(small_chunks, sum_attn, sum_feed_0)
    attn_rows = jnp.concatenate([seq_sum(sum_attn), sum_feed_0[: 4 * rows]]).reshape(4 * LAYERS, 1, rows, D)
    mesh_sizes, cuts, last_chunks = (shards, seq_count), (SMALL_ROWS, 128), [small_chunks, conv_chunks]
    if fused:
        give = cut_halves(lowered(attn_rows)).reshape(shards, rows, columns)
        basis = [traded[0], traded[1], traded[2], right_low]
        small_sum, sum_conv, rotation = reduce_chunks(mesh_sizes, cuts, last_chunks, give, parts, rotated_adam, basis)
    else:
        sent = rotate(join_halves(spread_halves(lowered(attn_rows)))[0])
        small_sum, sum_conv, rotation = reduce_chunks(mesh_sizes, cuts, last_chunks, sent, 0, None, [])
    feed_sums = [sum_feed_0[4 * rows :], sum_feed_1]
    small_sums, sum_vector, sum_loss = split_small(small_sum)
    sum_expand = jnp.stack(
        [s[: -shrink_weight.shape[1]].reshape(FF // D, -1, D).transpose(1, 0, 2).reshape(-1, FF) for s in feed_sums]
    )
    sum_shrink = jnp.stack([s[-shrink_weight.shape[1] :] for s in feed_sums])
    expand_new = adam_update(expand_weight, sum_expand, expand_first, expand_second, rate_matrix, decay_rate)
    shrink_new = adam_update(shrink_weight, sum_shrink, shrink_first, shrink_second, rate_matrix, decay_rate)
    conv_all = (conv_weight, conv_first, conv_second)
    attention_all = (attention_weight, attention_first, attention_second)
    vector_all = (vector_params, vector_first, vector_second)
    small_all = [
        (feature_weight, feature_first, feature_second),
        (final_weight, final_first, final_second),
        (target_weight, target_first, target_second),
        (codebook_weight, codebook_first, codebook_second),
    ]
    small_rules = [matrix_rule, matrix_rule, target_rule, codebook_rule]
    if fused:
        rules = (matrix_rule, attention_rule, vector_rule, small_rules)
        results = finish(rules, parts, small_sum, sum_conv, rotation, conv_all, attention_all, vector_all, small_all)
        conv_new, attention_new, vector_new, feature_new, final_new, target_new, codebook_new = results
    else:
        arrived = rotation.reshape(4 * LAYERS, parts, 2, rows, columns).transpose(2, 0, 3, 1, 4)
        arrived = arrived.reshape(2, 4 * LAYERS, rows, D).astype(jnp.float32)
        attention_new = attention_rule(attention_weight, arrived[1], attention_first, attention_second, arrived[0])
        conv_new = turned_adam(matrix_rule, conv_weight, sum_conv, conv_first, conv_second)
        vector_new = vector_rule(vector_params, sum_vector, vector_first, vector_second)
        feature_new, final_new, target_new, codebook_new = [
            rule(triple[0], grad, triple[1], triple[2]) for rule, grad, triple in zip(small_rules, small_sums, small_all)
        ]
    return (
        (sum_loss,)
        + feature_new
        + conv_new
        + attention_new
        + expand_new
        + shrink_new
        + final_new
        + target_new
        + codebook_new
        + vector_new
    )


def solution(mesh):
    return jax.shard_map(
        on_device,
        mesh=mesh,
        in_specs=(
            P("shard", "seq", None),
            P("shard", "seq"),
            P("shard", "seq", None),
            P("shard", "seq", None),
            P("shard", None),
            P("shard", None),
            P("shard", None),
            P("shard", None),
            P("shard", None),
            P("shard", None),
            P(None, "shard", None),
            P(None, "shard", None),
            P(None, "shard", None),
            P(None, "shard", None),
            P(),
            P(None, "shard", None),
            P(None, "shard", None),
            P(None, "shard", None),
            P(None, "shard", None),
            P(None, "shard", None),
            P(None, "shard", None),
            P("shard", None),
            P("shard", None),
            P("shard", None),
            P("shard", None),
            P("shard", None),
            P("shard", None),
            P("shard", None),
            P("shard", None),
            P("shard", None),
            P("shard"),
            P("shard"),
            P("shard"),
        ),
        out_specs=(
            P(),
            P("shard", None),
            P("shard", None),
            P("shard", None),
            P("shard", None),
            P("shard", None),
            P("shard", None),
            P(None, "shard", None),
            P(None, "shard", None),
            P(None, "shard", None),
            P(None, "shard", None),
            P(None, "shard", None),
            P(None, "shard", None),
            P(None, "shard", None),
            P(None, "shard", None),
            P(None, "shard", None),
            P("shard", None),
            P("shard", None),
            P("shard", None),
            P("shard", None),
            P("shard", None),
            P("shard", None),
            P("shard", None),
            P("shard", None),
            P("shard", None),
            P("shard"),
            P("shard"),
            P("shard"),
        ),
        check_vma=False,
    )
```

```python
import functools

import jax
import jax.numpy as jnp
from jax import lax
from jax.experimental import pallas as pl
from jax.experimental.pallas import tpu as pltpu
from jax.sharding import PartitionSpec as P

D = 768
HEADS = 12
HDIM = 64
FF = 3072
CIN = 512
PROJ = 256
CODES = 320
QGROUPS = 2
LAYERS = 2
STEP = 10
SMALL_ROWS = 160


beta_one = 0.9
beta_two = 0.95
beta_rotated = 0.5
adam_epsilon = 1e-08
decay_rate = 0.01
rate_matrix = 0.02
rate_target = 0.08
rate_codebook = 0.6
rate_vector = 0.3
rate_rotated = 0.08
contrastive_sharpness = 0.1
norm_epsilon = 1e-05
unit_epsilon = 1e-06

KW = 128
GROUPS = 16
GC = D // GROUPS
LANE = 64
PACK = 4
PADW = GROUPS * LANE
HALF = KW // PACK
STEPS = HALF + 1
VMEM = 56 * 1024 * 1024
SMALL_COST = pl.CostEstimate(flops=1024, bytes_accessed=1024, transcendentals=0)
CONV_COST = pl.CostEstimate(flops=35 * 10**9, bytes_accessed=10**7, transcendentals=0)
NT = (((1,), (1,)), ((), ()))
NN = (((1,), (0,)), ((), ()))


def mm(a, b, dims=NN):
    return lax.dot_general(a, b, dims, preferred_element_type=jnp.float32)


def spread_matrix(rows, out_cols, block, wide):
    i = lax.broadcasted_iota(jnp.int32, (rows, out_cols), 0)
    j = lax.broadcasted_iota(jnp.int32, (rows, out_cols), 1)
    return ((i // block) * wide + i % block == j).astype(jnp.bfloat16)


def pack_pair(x_ref, even_ref, odd_ref, rows):
    low = lax.broadcasted_iota(jnp.int32, (rows * 16, 128), 1) < LANE
    x = x_ref[...].reshape(rows, PACK, 16, 128)
    for half in range(2):
        first = x[:, 2 * half].reshape(rows * 16, 128).astype(jnp.float32)
        second = x[:, 2 * half + 1].reshape(rows * 16, 128).astype(jnp.float32)
        even_ref[:, half * 128:half * 128 + 128] = jnp.where(low, first, pltpu.roll(second, LANE, 1)).astype(jnp.bfloat16)
        odd_ref[:, half * 128:half * 128 + 128] = jnp.where(low, pltpu.roll(first, LANE, 1), second).astype(jnp.bfloat16)


def unpack_pair(even, odd, out_ref, rows):
    low = lax.broadcasted_iota(jnp.int32, (rows * 16, 128), 1) < LANE
    parts = []
    for half in range(2):
        e = even[:, half * 128:half * 128 + 128]
        o = odd[:, half * 128:half * 128 + 128]
        parts.append(jnp.where(low, e, pltpu.roll(o, LANE, 1)).reshape(rows, 1, 16, 128))
        parts.append(jnp.where(low, pltpu.roll(e, LANE, 1), o).reshape(rows, 1, 16, 128))
    out_ref[...] = jnp.concatenate(parts, axis=1).reshape(PACK * rows, 16, 128)


def widen_taps(w_ref, wide_ref, shards):
    per = KW // shards
    sel = spread_matrix(per * GC, per * LANE, GC, LANE)
    block = mm(w_ref[...].reshape(shards * 2 * GC, per * GC), sel).astype(jnp.bfloat16)
    for group in range(2):
        wide_ref[group, GC:, :] = jnp.zeros((LANE - GC, STEPS * 256), jnp.bfloat16)
        wide_ref[group, 0:GC, KW * LANE:] = jnp.zeros((GC, STEPS * 256 - KW * LANE), jnp.bfloat16)
        for s in range(shards):
            start = (2 * s + group) * GC
            wide_ref[group, 0:GC, s * per * LANE:(s + 1) * per * LANE] = block[start:start + GC]


def build_taps(wide_ref, taps_ref, group):
    wide = wide_ref[group]
    shifted = pltpu.roll(wide.astype(jnp.float32), LANE, 1).astype(jnp.bfloat16)
    total = STEPS * 256
    taps_ref[0:64, :] = wide
    taps_ref[64:128, :] = shifted
    taps_ref[128:192, 0:128] = jnp.zeros((64, 128), jnp.bfloat16)
    taps_ref[128:192, 128:total] = wide[:, 0:total - 128]
    taps_ref[192:256, 0:128] = jnp.zeros((64, 128), jnp.bfloat16)
    taps_ref[192:256, 128:total] = shifted[:, 0:total - 128]


def conv_forward_kernel(rows, shards, x_ref, w_ref, y_ref, even_ref, odd_ref, taps_ref, wide_ref):
    m = rows * 16
    pack_pair(x_ref, even_ref, odd_ref, rows + HALF)
    widen_taps(w_ref, wide_ref, shards)
    results = []
    for group, packed in enumerate((even_ref, odd_ref)):
        build_taps(wide_ref, taps_ref, group)
        left = jnp.concatenate([packed[q * 16:q * 16 + m, :] for q in range(STEPS)], axis=1)
        results.append(mm(left, taps_ref[...], NT))
    unpack_pair(results[0], results[1], y_ref, rows)


def conv_forward(x, w, first, rows, shards):
    frames = PACK * (rows + HALF)
    return pl.pallas_call(
        functools.partial(conv_forward_kernel, rows, shards),
        grid=(GROUPS // 2,),
        in_specs=[
            pl.BlockSpec((frames, 16, 128), lambda g: (0, 0, g)),
            pl.BlockSpec((shards, 2 * GC, w.shape[2]), lambda g: (0, first + g, 0)),
        ],
        out_specs=pl.BlockSpec((PACK * rows, 16, 128), lambda g: (0, 0, g)),
        out_shape=jax.ShapeDtypeStruct((PACK * rows, 16, PADW), jnp.float32),
        scratch_shapes=[pltpu.VMEM(((rows + HALF) * 16, 256), jnp.bfloat16)] * 2 + [
            pltpu.VMEM((256, STEPS * 256), jnp.bfloat16),
            pltpu.VMEM((2, LANE, STEPS * 256), jnp.bfloat16),
        ],
        cost_estimate=SMALL_COST,
        compiler_params=pltpu.CompilerParams(vmem_limit_bytes=VMEM, dimension_semantics=("arbitrary",)),
        name="conv_forward",
    )(x, w)


def conv_input_kernel(rows, shards, d_ref, w_ref, dx_ref, even_ref, odd_ref, taps_ref, wide_ref):
    m = rows * 16
    pack_pair(d_ref, even_ref, odd_ref, rows + HALF)
    widen_taps(w_ref, wide_ref, shards)
    results = []
    for group, packed in enumerate((even_ref, odd_ref)):
        build_taps(wide_ref, taps_ref, group)
        acc = jnp.zeros((m, 256), jnp.float32)
        for q in range(STEPS):
            left = packed[(HALF - q) * 16:(HALF - q) * 16 + m, :]
            acc = acc + mm(left, taps_ref[:, q * 256:q * 256 + 256])
        results.append(acc)
    unpack_pair(results[0], results[1], dx_ref, rows)


def conv_input_grad(d, w, first, rows, shards):
    frames = PACK * (rows + HALF)
    return pl.pallas_call(
        functools.partial(conv_input_kernel, rows, shards),
        grid=(GROUPS // 2,),
        in_specs=[
            pl.BlockSpec((frames, 16, 128), lambda g: (0, 0, g)),
            pl.BlockSpec((shards, 2 * GC, w.shape[2]), lambda g: (0, first + g, 0)),
        ],
        out_specs=pl.BlockSpec((PACK * rows, 16, 128), lambda g: (0, 0, g)),
        out_shape=jax.ShapeDtypeStruct((PACK * rows, 16, PADW), jnp.float32),
        scratch_shapes=[pltpu.VMEM(((rows + HALF) * 16, 256), jnp.bfloat16)] * 2 + [
            pltpu.VMEM((256, STEPS * 256), jnp.bfloat16),
            pltpu.VMEM((2, LANE, STEPS * 256), jnp.bfloat16),
        ],
        cost_estimate=CONV_COST,
        compiler_params=pltpu.CompilerParams(vmem_limit_bytes=VMEM, dimension_semantics=("arbitrary",)),
        name="conv_input_grad",
    )(d, w)


def conv_weight_kernel(rows, shards, x_ref, d_ref, dw_ref, xe_ref, xo_ref, de_ref, do_ref, prod_ref, grad_ref):
    m = rows * 16
    per = KW // shards
    width = KW * LANE
    pack_pair(x_ref, xe_ref, xo_ref, rows + HALF)
    pack_pair(d_ref, de_ref, do_ref, rows)
    for group, (x_packed, d_packed) in enumerate(((xe_ref, de_ref), (xo_ref, do_ref))):
        d_turned = d_packed[...].astype(jnp.float32).T.astype(jnp.bfloat16)
        for q in range(STEPS):
            prod_ref[:, q * 256:q * 256 + 256] = mm(d_turned, x_packed[q * 16:q * 16 + m, :])
        straight = prod_ref[0:GC, 0:width] + prod_ref[128:128 + GC, 128:128 + width]
        turned_part = prod_ref[64:64 + GC, :] + pltpu.roll(prod_ref[192:192 + GC, :], STEPS * 256 - 128, 1)
        grad = straight + pltpu.roll(turned_part, STEPS * 256 - 64, 1)[:, 0:width]
        grad = grad.astype(jnp.bfloat16)
        for s in range(shards):
            start = (2 * s + group) * GC
            grad_ref[start:start + GC, :] = grad[:, s * per * LANE:(s + 1) * per * LANE]
    sel = spread_matrix(per * GC, per * LANE, GC, LANE)
    dw_ref[...] = mm(grad_ref[...], sel, NT).astype(jnp.bfloat16).reshape(shards, 2 * GC, per * GC)


def conv_weight_grad(x, d, rows, shards):
    per = KW // shards
    first = HALF * PACK // 2
    d = d[first:first + PACK * rows]
    return pl.pallas_call(
        functools.partial(conv_weight_kernel, rows, shards),
        grid=(GROUPS // 2,),
        in_specs=[
            pl.BlockSpec((PACK * (rows + HALF), 16, 128), lambda g: (0, 0, g)),
            pl.BlockSpec((PACK * rows, 16, 128), lambda g: (0, 0, g)),
        ],
        out_specs=pl.BlockSpec((shards, 2 * GC, per * GC), lambda g: (0, g, 0)),
        out_shape=jax.ShapeDtypeStruct((shards, D, per * GC), jnp.bfloat16),
        scratch_shapes=[
            pltpu.VMEM(((rows + HALF) * 16, 256), jnp.bfloat16),
            pltpu.VMEM(((rows + HALF) * 16, 256), jnp.bfloat16),
            pltpu.VMEM((rows * 16, 256), jnp.bfloat16),
            pltpu.VMEM((rows * 16, 256), jnp.bfloat16),
            pltpu.VMEM((256, STEPS * 256), jnp.float32),
            pltpu.VMEM((shards * 2 * GC, per * LANE), jnp.bfloat16),
        ],
        cost_estimate=CONV_COST,
        compiler_params=pltpu.CompilerParams(vmem_limit_bytes=VMEM, dimension_semantics=("arbitrary",)),
        name="conv_weight_grad",
    )(x, d)


def turned_adam_kernel(rule, grad_ref, weight_ref, first_ref, second_ref, new_ref, new_first_ref, new_second_ref):
    new, first, second = rule(weight_ref[...], grad_ref[...].T, first_ref[...], second_ref[...])
    new_ref[...] = new
    new_first_ref[...] = first
    new_second_ref[...] = second


def turned_adam(rule, weight, grad, first, second):
    return tuple(
        pl.pallas_call(
            functools.partial(turned_adam_kernel, rule),
            out_shape=[jax.ShapeDtypeStruct(weight.shape, jnp.float32)] * 3,
            cost_estimate=SMALL_COST,
            compiler_params=pltpu.CompilerParams(vmem_limit_bytes=VMEM),
            name="turned_adam",
        )(grad, weight, first, second)
    )


def put_pieces(out_ref, start, block, taps):
    depth, width = block.shape[-2:]
    for at in range(0, width, taps):
        size = min(taps, width - at)
        out_ref[..., start:start + depth, 0:size] = block[..., at:at + size]
        start += depth
    return start


def pack_weights_kernel(conv_ref, *refs):
    vector_ref, out_ref, held = refs[-3:]
    taps = conv_ref.shape[0]
    out_ref[0:D, :] = conv_ref[...].T.astype(jnp.bfloat16)
    held[...] = jnp.zeros_like(held)
    start = 0
    for ref in refs[:-3]:
        start = put_pieces(held, start, ref[...], taps)
    size = vector_ref.shape[1]
    for at in range(0, size, taps):
        width = min(taps, size - at)
        held[start:start + 1, 0:width] = vector_ref[:, at:at + width]
        start += 1
    out_ref[D:, :] = held[...].astype(jnp.bfloat16)


def pack_weights(conv, blocks, vector, rows):
    taps = conv.shape[0]
    return pl.pallas_call(
        pack_weights_kernel,
        out_shape=jax.ShapeDtypeStruct((D + rows, taps), jnp.bfloat16),
        scratch_shapes=[pltpu.VMEM((rows, taps), jnp.float32)],
        cost_estimate=SMALL_COST,
        compiler_params=pltpu.CompilerParams(vmem_limit_bytes=VMEM),
        name="pack_weights",
    )(conv, *blocks, vector.reshape(1, -1))


def pack_grads_kernel(blocks, *refs):
    extra_ref, out_ref, held, flat = refs[-4:]
    shards, _, taps = out_ref.shape
    held[...] = jnp.zeros_like(held)
    start = 0
    for ref in refs[:blocks]:
        start = put_pieces(held, start, ref[...], taps)
    place = 0
    for ref in refs[blocks:-4]:
        flat[:, place:place + ref.shape[1]] = ref[...]
        place += ref.shape[1]
    size = place // shards
    for s in range(shards):
        for row, at in enumerate(range(0, size, taps)):
            width = min(taps, size - at)
            held[s, start + row:start + row + 1, 0:width] = flat[:, s * size + at:s * size + at + width]
    start += -(-size // taps)
    held[:, start:start + 1, 0:128] = jnp.broadcast_to(extra_ref[...][None], (shards, 1, 128))
    out_ref[...] = held[...].astype(jnp.bfloat16)


def pack_grads(blocks, vectors, extra, shards, rows, taps):
    blocks = [block.reshape(shards, -1, block.shape[-1]) for block in blocks]
    vectors = [v.reshape(1, -1) for v in vectors]
    total = sum(v.shape[1] for v in vectors)
    return pl.pallas_call(
        functools.partial(pack_grads_kernel, len(blocks)),
        out_shape=jax.ShapeDtypeStruct((shards, rows, taps), jnp.bfloat16),
        scratch_shapes=[pltpu.VMEM((shards, rows, taps), jnp.float32), pltpu.VMEM((1, total), jnp.float32)],
        cost_estimate=SMALL_COST,
        compiler_params=pltpu.CompilerParams(vmem_limit_bytes=VMEM),
        name="pack_grads",
    )(*blocks, *vectors, extra)


def to_strips(padded, frame_count):
    clips = padded.shape[0]
    strips = 16 // clips
    length = frame_count // strips
    sel = spread_matrix(D, PADW, GC, LANE)
    wide = mm(padded.reshape(-1, D), sel).astype(jnp.bfloat16).reshape(clips, -1, PADW)
    parts = jnp.stack([wide[:, s * length:s * length + length + KW] for s in range(strips)], 1)
    return parts.reshape(16, length + KW, PADW).transpose(1, 0, 2)


def from_strips(y, clips):
    rows = y.transpose(1, 0, 2).reshape(-1, PADW)
    high = lax.reduce_precision(rows, 8, 7)
    rest = (rows - high).astype(jnp.bfloat16)
    high = high.astype(jnp.bfloat16)
    sel = spread_matrix(D, PADW, GC, LANE)
    return mm(high, sel, NT) + mm(rest, sel, NT)


SCALE = HDIM ** (-0.5)


def turned(block):
    return block.astype(jnp.float32).T.astype(jnp.bfloat16)


def attend_kernel(blocks, q_ref, *refs):
    keys = [refs[2 * j] for j in range(blocks)]
    values = [refs[2 * j + 1] for j in range(blocks)]
    mixed_ref, stat_ref = refs[2 * blocks:]
    frames = q_ref.shape[0]
    low = lax.broadcasted_iota(jnp.int32, (frames, 128), 1) < HDIM
    scaled = q_ref[...] * jnp.bfloat16(SCALE)
    none = jnp.zeros_like(scaled)
    turned_keys = [turned(k[...]) for k in keys]
    parts = []
    stats = []
    for head in range(2):
        query = jnp.where(low, scaled, none) if head == 0 else jnp.where(low, none, scaled)
        scores = [mm(query, k) for k in turned_keys]
        largest = functools.reduce(jnp.maximum, [jnp.max(s, 1, keepdims=True) for s in scores])
        powers = [jnp.exp(s - largest) for s in scores]
        total = functools.reduce(jnp.add, [jnp.sum(p, 1, keepdims=True) for p in powers])
        out = functools.reduce(jnp.add, [mm(p.astype(jnp.bfloat16), v[...]) for p, v in zip(powers, values)])
        parts.append(out * (1.0 / total))
        stats.append(jnp.broadcast_to(largest + jnp.log(total), (frames, 128)))
    mixed_ref[...] = jnp.where(low, parts[0], parts[1]).astype(jnp.bfloat16)
    rows = jnp.where(low, stats[0], stats[1]).T
    stat_ref[0, 0, 0:1, :] = rows[0:1, :]
    stat_ref[0, 0, 1:2, :] = rows[HDIM:HDIM + 1, :]


def head_spec(item, frames):
    if isinstance(item, tuple):
        return pl.BlockSpec((None, frames, 128), lambda c, h: (item[1], c, h))
    return pl.BlockSpec((frames, 128), lambda c, h: (c, h))


def head_array(item):
    return item[0] if isinstance(item, tuple) else item


def attend(query, keys, values, clips):
    blocks = len(keys)
    rows = head_array(query).shape[-2]
    frames = rows // clips
    spec = pl.BlockSpec((frames, 128), lambda c, h: (c, h))
    operands = [query]
    for k, v in zip(keys, values):
        operands += [k, v]
    return pl.pallas_call(
        functools.partial(attend_kernel, blocks),
        grid=(clips, HEADS // 2),
        in_specs=[head_spec(item, frames) for item in operands],
        out_specs=[spec, pl.BlockSpec((1, 1, 2, frames), lambda c, h: (c, h, 0, 0))],
        out_shape=[
            jax.ShapeDtypeStruct((rows, D), jnp.bfloat16),
            jax.ShapeDtypeStruct((clips, HEADS // 2, 2, frames), jnp.float32),
        ],
        cost_estimate=SMALL_COST,
        compiler_params=pltpu.CompilerParams(vmem_limit_bytes=VMEM, dimension_semantics=("arbitrary", "arbitrary")),
        name="attend",
    )(*[head_array(item) for item in operands])


def attend_back_kernel(blocks, q_ref, d_ref, stat_ref, *refs):
    keys = [refs[2 * j] for j in range(blocks)]
    values = [refs[2 * j + 1] for j in range(blocks)]
    dq_ref = refs[2 * blocks]
    dk = [refs[2 * blocks + 1 + 2 * j] for j in range(blocks)]
    dv = [refs[2 * blocks + 2 + 2 * j] for j in range(blocks)]
    frames = q_ref.shape[0]
    low = lax.broadcasted_iota(jnp.int32, (frames, 128), 1) < HDIM
    scaled = q_ref[...] * jnp.bfloat16(SCALE)
    grad = d_ref[...]
    none = jnp.zeros_like(scaled)
    q_turned = turned(scaled)
    d_turned = turned(grad)
    gap = jnp.zeros((HDIM, frames), jnp.bfloat16)
    k_turned = [turned(k[...]) for k in keys]
    dq_rows = []
    dk_sum = [None] * blocks
    dv_sum = [None] * blocks
    for head in range(2):
        pick = slice(head * HDIM, head * HDIM + HDIM)
        if head == 0:
            query, grad_head = jnp.where(low, scaled, none), jnp.where(low, grad, none)
            q_side = jnp.concatenate([q_turned[pick], gap], 0)
            d_side = jnp.concatenate([d_turned[pick], gap], 0)
        else:
            query, grad_head = jnp.where(low, none, scaled), jnp.where(low, none, grad)
            q_side = jnp.concatenate([gap, q_turned[pick]], 0)
            d_side = jnp.concatenate([gap, d_turned[pick]], 0)
        stat = stat_ref[0, 0, head:head + 1, :]
        probs = [jnp.exp(mm(k[...], q_side) - stat) for k in keys]
        weighted = [p * mm(v[...], d_side) for p, v in zip(probs, values)]
        delta = functools.reduce(jnp.add, [jnp.sum(w, 0, keepdims=True) for w in weighted])
        dq = None
        for j in range(blocks):
            ds = (weighted[j] - probs[j] * delta).astype(jnp.bfloat16)
            grad_v = mm(probs[j].astype(jnp.bfloat16), grad_head)
            grad_k = mm(ds, query)
            part = mm(k_turned[j][pick], ds)
            dq = part if dq is None else dq + part
            dv_sum[j] = grad_v if dv_sum[j] is None else dv_sum[j] + grad_v
            dk_sum[j] = grad_k if dk_sum[j] is None else dk_sum[j] + grad_k
        dq_rows.append(dq)
    dq_ref[...] = (jnp.concatenate(dq_rows, 0) * SCALE).T.astype(jnp.bfloat16)
    for j in range(blocks):
        dk[j][...] = dk_sum[j].astype(jnp.bfloat16)
        dv[j][...] = dv_sum[j].astype(jnp.bfloat16)


def attend_back(query, grad, stat, keys, values, clips):
    blocks = len(keys)
    rows = grad.shape[0]
    frames = rows // clips
    spec = pl.BlockSpec((frames, 128), lambda c, h: (c, h))
    operands = []
    for k, v in zip(keys, values):
        operands += [k, v]
    shape = jax.ShapeDtypeStruct((rows, D), jnp.bfloat16)
    return pl.pallas_call(
        functools.partial(attend_back_kernel, blocks),
        grid=(clips, HEADS // 2),
        in_specs=[head_spec(query, frames), spec, pl.BlockSpec((1, 1, 2, frames), lambda c, h: (c, h, 0, 0))]
        + [head_spec(item, frames) for item in operands],
        out_specs=[spec] * (1 + 2 * blocks),
        out_shape=[shape] * (1 + 2 * blocks),
        cost_estimate=SMALL_COST,
        compiler_params=pltpu.CompilerParams(vmem_limit_bytes=VMEM, dimension_semantics=("arbitrary", "arbitrary")),
        name="attend_back",
    )(head_array(query), grad, stat, *[head_array(item) for item in operands])


def count_kernel(draws, n_ref, out_ref):
    length, frames = out_ref.shape[1:]
    place = lax.broadcasted_iota(jnp.int32, (length // 8, 8, frames), 0) * 8 + lax.broadcasted_iota(
        jnp.int32, (length // 8, 8, frames), 1)
    total = jnp.zeros((length // 8, 8, frames), jnp.float32)
    for n in range(draws):
        row = n_ref[0, n:n + 1, :]
        total = total + jnp.where(place == row[None], 1.0, 0.0)
    out_ref[0] = total.reshape(length, frames).astype(jnp.bfloat16)


def count_draws(negatives, length):
    clips, draws, frames = negatives.shape
    tile = 128 if frames % 128 == 0 else frames
    return pl.pallas_call(
        functools.partial(count_kernel, draws),
        grid=(clips, frames // tile),
        in_specs=[pl.BlockSpec((1, draws, tile), lambda c, f: (c, 0, f))],
        out_specs=pl.BlockSpec((1, length, tile), lambda c, f: (c, 0, f)),
        out_shape=jax.ShapeDtypeStruct((clips, length, frames), jnp.bfloat16),
        cost_estimate=SMALL_COST,
        compiler_params=pltpu.CompilerParams(vmem_limit_bytes=VMEM, dimension_semantics=("arbitrary", "arbitrary")),
        name="count_draws",
    )(negatives)


def square(ref):
    return ref[...].reshape(D, D)


def project_kernel(x_ref, w_ref, b_ref, out_ref):
    out_ref[0] = (mm(x_ref[...], square(w_ref)) + b_ref[0]).astype(jnp.bfloat16)


def project(entry, whole, first, biases):
    count = len(biases)
    rows = entry.shape[0]
    shards, _, _ = whole.shape
    depth = D // shards
    return pl.pallas_call(
        project_kernel,
        grid=(count,),
        in_specs=[
            pl.BlockSpec((rows, D), lambda i: (0, 0)),
            pl.BlockSpec((shards, depth, D), lambda i: (0, first + i, 0)),
            pl.BlockSpec((1, 1, D), lambda i: (i, 0, 0)),
        ],
        out_specs=pl.BlockSpec((1, rows, D), lambda i: (i, 0, 0)),
        out_shape=jax.ShapeDtypeStruct((count, rows, D), jnp.bfloat16),
        cost_estimate=SMALL_COST,
        compiler_params=pltpu.CompilerParams(vmem_limit_bytes=VMEM, dimension_semantics=("arbitrary",)),
        name="project",
    )(entry, whole, jnp.stack(biases).reshape(count, 1, D))


def norm_rows(values, gain_row, bias_row):
    centred = values - jnp.mean(values, -1, keepdims=True)
    scale = lax.rsqrt(jnp.mean(centred * centred, -1, keepdims=True) + norm_epsilon)
    level = centred * scale
    return level * gain_row + bias_row, level, scale


def norm_rows_back(grad, level, scale, gain_row):
    inside = grad * gain_row
    centred = inside - jnp.mean(inside, -1, keepdims=True) - level * jnp.mean(inside * level, -1, keepdims=True)
    return scale * centred


def gelu_parts(values):
    half = 0.5 * (1.0 + lax.erf(values * 0.5**0.5))
    density = jnp.exp(-0.5 * values * values) * (2.0 * jnp.pi) ** -0.5
    return values * half, half + values * density


def feed_kernel(
    hidden_ref, mixed_ref, wo_ref, e_ref, s_ref, ob_ref, g1_ref, b1_ref, eb_ref, sb_ref, g2_ref, b2_ref,
    low_ref, level1_ref, scale1_ref, active_ref, slope_ref, result_ref, result_low_ref, level2_ref, scale2_ref,
    middle_ref, total_ref,
):
    step = pl.program_id(0)

    @pl.when(step == 0)
    def _():
        branch = mm(mixed_ref[...], square(wo_ref)) + ob_ref[...]
        middle, level, scale = norm_rows(hidden_ref[...] + branch, g1_ref[...], b1_ref[...])
        middle_ref[...] = middle
        low_ref[...] = middle.astype(jnp.bfloat16)
        level1_ref[...] = level
        scale1_ref[...] = scale
        total_ref[...] = jnp.zeros_like(total_ref)

    inner = mm(low_ref[...], square(e_ref)) + eb_ref[...]
    active, slope = gelu_parts(inner)
    active = active.astype(jnp.bfloat16)
    active_ref[...] = active
    slope_ref[...] = slope.astype(jnp.bfloat16)
    total_ref[...] += mm(active, square(s_ref))

    @pl.when(step == pl.num_programs(0) - 1)
    def _():
        result, level, scale = norm_rows(middle_ref[...] + (total_ref[...] + sb_ref[...]), g2_ref[...], b2_ref[...])
        result_ref[...] = result
        result_low_ref[...] = result.astype(jnp.bfloat16)
        level2_ref[...] = level
        scale2_ref[...] = scale


def feed_forward(hidden, mixed, attn_whole, feed_whole, first, place, vectors):
    rows = hidden.shape[0]
    shards = attn_whole.shape[0]
    depth = D // shards
    parts = FF // D
    row = pl.BlockSpec((1, D), lambda j: (0, 0))
    flat = pl.BlockSpec((rows, D), lambda j: (0, 0))
    column = pl.BlockSpec((rows, 1), lambda j: (0, 0))
    tile = pl.BlockSpec((rows, D), lambda j: (0, j))
    o_bias, gain_one, bias_one, expand_bias, shrink_bias, gain_two, bias_two = [v.reshape(1, -1) for v in vectors]

    def shape(width, dtype):
        return jax.ShapeDtypeStruct((rows, width), dtype)

    return pl.pallas_call(
        feed_kernel,
        grid=(parts,),
        in_specs=[
            flat,
            flat,
            pl.BlockSpec((shards, depth, D), lambda j: (0, place + 3, 0)),
            pl.BlockSpec((shards, depth, D), lambda j: (0, first + j, 0)),
            pl.BlockSpec((shards // parts, parts * depth, D), lambda j: (j, first // parts + 1, 0)),
            row, row, row,
            pl.BlockSpec((1, D), lambda j: (0, j)),
            row, row, row,
        ],
        out_specs=[flat, flat, column, tile, tile, flat, flat, flat, column],
        out_shape=[
            shape(D, jnp.bfloat16), shape(D, jnp.float32), shape(1, jnp.float32),
            shape(FF, jnp.bfloat16), shape(FF, jnp.bfloat16),
            shape(D, jnp.float32), shape(D, jnp.bfloat16), shape(D, jnp.float32), shape(1, jnp.float32),
        ],
        scratch_shapes=[pltpu.VMEM((rows, D), jnp.float32)] * 2,
        cost_estimate=SMALL_COST,
        compiler_params=pltpu.CompilerParams(vmem_limit_bytes=VMEM, dimension_semantics=("arbitrary",)),
        name="feed_forward",
    )(hidden, mixed, attn_whole, feed_whole, feed_whole, o_bias, gain_one, bias_one, expand_bias, shrink_bias, gain_two, bias_two)


def row_sum(values):
    return jnp.sum(values, 0, keepdims=True)


def feed_back_kernel(arrivals, base, *refs):
    if base:
        refs = refs[1:]
    grad_ref = refs[0]
    extra = refs[1 : 1 + arrivals]
    (
        level2_ref, scale2_ref, g2_ref, slope_ref, active_ref, low_ref, e_ref, s_ref, level1_ref, scale1_ref, g1_ref, wo_ref,
        sum_ref, branch_ref, mixed_ref, vec_ref, eb_ref, chunk_ref,
        outer_ref, turned_ref, total_ref, e_slot, s_slot, e_sem, s_sem,
    ) = refs[1 + arrivals :]
    step = pl.program_id(0)
    last = pl.num_programs(0) - 1
    slot = lax.rem(step, 2)
    shards, depth = e_slot.shape[1:3]
    group = s_slot.shape[1]

    @pl.when(step == 0)
    def _():
        grad = grad_ref[...]
        for ref in extra:
            grad = grad + ref[...].astype(jnp.float32)
        level = level2_ref[...]
        total = norm_rows_back(grad, level, scale2_ref[...], g2_ref[...])
        outer = total.astype(jnp.bfloat16)
        outer_ref[...] = outer
        total_ref[...] = total
        vec_ref[3:4, :] = row_sum(outer.astype(jnp.float32))
        vec_ref[4:5, :] = row_sum(grad * level)
        vec_ref[5:6, :] = row_sum(grad)
        turned_ref[...] = turned(low_ref[...])

    def copies(at, index):
        e_copy = pltpu.make_async_copy(
            e_slot.at[at], chunk_ref.at[:, pl.ds(base + index * depth, depth), :], e_sem.at[at]
        )
        s_copy = pltpu.make_async_copy(
            s_slot.at[at],
            chunk_ref.at[pl.ds(index * group, group), pl.ds(base + (last + 1) * depth, (last + 1) * depth), :],
            s_sem.at[at],
        )
        return e_copy, s_copy

    @pl.when(step >= 2)
    def _():
        for copy in copies(slot, step - 2):
            copy.wait()

    outer = outer_ref[...]
    inner = (mm(outer, square(s_ref), NT) * slope_ref[...].astype(jnp.float32)).astype(jnp.bfloat16)
    eb_ref[...] = row_sum(inner.astype(jnp.float32))
    total_ref[...] += mm(inner, square(e_ref), NT)
    e_slot[slot] = mm(turned_ref[...], inner).astype(jnp.bfloat16).reshape(shards, depth, D)
    s_slot[slot] = mm(turned(active_ref[...]), outer).astype(jnp.bfloat16).reshape(group, (last + 1) * depth, D)
    for copy in copies(slot, step):
        copy.start()

    @pl.when(step == last)
    def _():
        grad = total_ref[...]
        level = level1_ref[...]
        total = norm_rows_back(grad, level, scale1_ref[...], g1_ref[...])
        branch = total.astype(jnp.bfloat16)
        sum_ref[...] = total
        branch_ref[...] = branch
        vec_ref[0:1, :] = row_sum(branch.astype(jnp.float32))
        vec_ref[1:2, :] = row_sum(grad * level)
        vec_ref[2:3, :] = row_sum(grad)
        vec_ref[6:8, :] = jnp.zeros((2, D), jnp.float32)
        mixed_ref[...] = mm(branch, square(wo_ref), NT).astype(jnp.bfloat16)
        for index in (last - 1, last):
            for copy in copies(lax.rem(index, 2), index):
                copy.wait()


def feed_back(grads, cache, attn_whole, feed_whole, first, place, gain_one, gain_two, chunks):
    level1, scale1, low, slope, active, level2, scale2 = cache
    rows = low.shape[0]
    shards = attn_whole.shape[0]
    depth = D // shards
    parts = FF // D
    flat = pl.BlockSpec((rows, D), lambda j: (0, 0))
    row = pl.BlockSpec((1, D), lambda j: (0, 0))
    column = pl.BlockSpec((rows, 1), lambda j: (0, 0))
    tile = pl.BlockSpec((rows, D), lambda j: (0, j))
    return pl.pallas_call(
        functools.partial(feed_back_kernel, len(grads) - 1, 0 if chunks is None else 4 * depth),
        grid=(parts,),
        in_specs=[pl.BlockSpec(memory_space=pl.ANY)] * (chunks is not None)
        + [flat] * len(grads)
        + [
            flat, column, row, tile, tile, flat,
            pl.BlockSpec((shards, depth, D), lambda j: (0, first + j, 0)),
            pl.BlockSpec((shards // parts, parts * depth, D), lambda j: (j, first // parts + 1, 0)),
            flat, column, row,
            pl.BlockSpec((shards, depth, D), lambda j: (0, place + 3, 0)),
        ],
        out_specs=[
            flat, flat, flat,
            pl.BlockSpec((8, D), lambda j: (0, 0)),
            pl.BlockSpec((1, D), lambda j: (0, j)),
            pl.BlockSpec(memory_space=pl.ANY),
        ],
        out_shape=[
            jax.ShapeDtypeStruct((rows, D), jnp.float32),
            jax.ShapeDtypeStruct((rows, D), jnp.bfloat16),
            jax.ShapeDtypeStruct((rows, D), jnp.bfloat16),
            jax.ShapeDtypeStruct((8, D), jnp.float32),
            jax.ShapeDtypeStruct((1, FF), jnp.float32),
            jax.ShapeDtypeStruct((shards, (4 * (chunks is not None) + 2 * parts) * depth, D), jnp.bfloat16),
        ],
        input_output_aliases={} if chunks is None else {0: 5},
        scratch_shapes=[
            pltpu.VMEM((rows, D), jnp.bfloat16),
            pltpu.VMEM((D, rows), jnp.bfloat16),
            pltpu.VMEM((rows, D), jnp.float32),
            pltpu.VMEM((2, shards, depth, D), jnp.bfloat16),
            pltpu.VMEM((2, shards // parts, parts * depth, D), jnp.bfloat16),
            pltpu.SemaphoreType.DMA((2,)),
            pltpu.SemaphoreType.DMA((2,)),
        ],
        cost_estimate=SMALL_COST,
        compiler_params=pltpu.CompilerParams(vmem_limit_bytes=VMEM, dimension_semantics=("arbitrary",)),
        name="feed_back",
    )(
        *([] if chunks is None else [chunks]), *grads, level2, scale2, gain_two.reshape(1, D), slope, active, low, feed_whole, feed_whole,
        level1, scale1, gain_one.reshape(1, D), attn_whole,
    )


def entry_back_kernel(blocks, sum_ref, dq_ref, *refs):
    keys, values = refs[0 : 2 * blocks : 2], refs[1 : 2 * blocks : 2]
    wq_ref, wk_ref, wv_ref = refs[2 * blocks : 2 * blocks + 3]
    outs = refs[2 * blocks + 3 :]
    key_w, value_w = square(wk_ref), square(wv_ref)
    for j in range(blocks):
        back = mm(keys[j][...], key_w, NT) + mm(values[j][...], value_w, NT)
        if j == 0:
            outs[0][...] = sum_ref[...] + mm(dq_ref[...], square(wq_ref), NT) + back
        else:
            outs[j][...] = back.astype(jnp.bfloat16)


def entry_back(grad_sum, dq, pairs, attn_whole, place):
    rows = dq.shape[0]
    shards = attn_whole.shape[0]
    flat = pl.BlockSpec((rows, D), lambda i: (0, 0))
    weights = [pl.BlockSpec((shards, D // shards, D), lambda i, m=m: (0, place + m, 0)) for m in range(3)]
    return pl.pallas_call(
        functools.partial(entry_back_kernel, len(pairs) // 2),
        grid=(1,),
        in_specs=[flat] * (2 + len(pairs)) + weights,
        out_specs=[flat] * (len(pairs) // 2),
        out_shape=[
            jax.ShapeDtypeStruct((rows, D), jnp.float32 if j == 0 else jnp.bfloat16) for j in range(len(pairs) // 2)
        ],
        cost_estimate=SMALL_COST,
        compiler_params=pltpu.CompilerParams(vmem_limit_bytes=VMEM, dimension_semantics=("arbitrary",)),
        name="entry_back",
    )(grad_sum, dq, *pairs, attn_whole, attn_whole, attn_whole)


def attn_grads_kernel(blocks, *refs):
    entries = refs[:blocks]
    dq_ref, mixed_ref, branch_ref = refs[blocks : blocks + 3]
    pairs = refs[blocks + 3 : 3 * blocks + 3]
    out_ref, vec_ref, slots, sem = refs[3 * blocks + 3 :]
    shards, depth = slots.shape[1:3]
    entry_turned = [turned(e[...]) for e in entries]

    def put(i, value):
        slots[i] = value.astype(jnp.bfloat16).reshape(shards, depth, D)
        pltpu.make_async_copy(slots.at[i], out_ref.at[:, pl.ds(i * depth, depth), :], sem.at[i]).start()

    put(0, mm(entry_turned[0], dq_ref[...]))
    put(1, functools.reduce(jnp.add, [mm(e, k[...]) for e, k in zip(entry_turned, pairs[0::2])]))
    put(2, functools.reduce(jnp.add, [mm(e, v[...]) for e, v in zip(entry_turned, pairs[1::2])]))
    put(3, mm(turned(mixed_ref[...]), branch_ref[...]))
    vec_ref[0:1, :] = row_sum(dq_ref[...].astype(jnp.float32))
    vec_ref[1:2, :] = functools.reduce(jnp.add, [row_sum(v[...].astype(jnp.float32)) for v in pairs[1::2]])
    vec_ref[2:8, :] = jnp.zeros((6, D), jnp.float32)
    for i in range(4):
        pltpu.make_async_copy(slots.at[i], out_ref.at[:, pl.ds(i * depth, depth), :], sem.at[i]).wait()


def attn_grads(entries, dq, mixed, branch, pairs, shards, room):
    blocks = len(entries)
    rows = dq.shape[0]
    flat = pl.BlockSpec((rows, D), lambda i: (0, 0))
    operands = list(entries) + [dq, mixed, branch] + list(pairs)
    return pl.pallas_call(
        functools.partial(attn_grads_kernel, blocks),
        grid=(1,),
        in_specs=[flat] * len(operands),
        out_specs=[pl.BlockSpec(memory_space=pl.ANY), pl.BlockSpec((8, D), lambda i: (0, 0))],
        out_shape=[
            jax.ShapeDtypeStruct((shards, room, D), jnp.bfloat16),
            jax.ShapeDtypeStruct((8, D), jnp.float32),
        ],
        scratch_shapes=[
            pltpu.VMEM((4, shards, D // shards, D), jnp.bfloat16),
            pltpu.SemaphoreType.DMA((4,)),
        ],
        cost_estimate=SMALL_COST,
        compiler_params=pltpu.CompilerParams(vmem_limit_bytes=VMEM, dimension_semantics=("arbitrary",)),
        name="attn_grads",
    )(*operands)


MESH = pl.DeviceIdType.MESH
AHEAD = 3
OTHER = 2
GATHER_AT = 3


def reduce_kernel(count, seqs, sizes, parts, rule, *refs):
    number = len(sizes)
    extra = 5 if parts else 1
    give_ref, basis = refs[number], refs[number + 1 : number + extra]
    take_ref = refs[2 * number + extra]
    refs = refs[:number] + refs[number + extra : 2 * number + extra] + refs[2 * number + extra + 1 :]
    sources = refs[:number]
    outs = refs[number : 2 * number]
    bits = count.bit_length() - 1
    turns = seqs.bit_length() - 1
    levels = bits + turns
    held = refs[2 * number : 2 * number + levels]
    send_sem, recv_sem, give_sem, take_sem = refs[2 * number + levels : 2 * number + levels + 4]
    rest = refs[2 * number + levels + 4 :]
    me = lax.axis_index("shard")
    place = lax.axis_index("seq")

    def across(index, bit):
        return index + (1 - 2 * ((index // 2**bit) % 2)) * 2**bit

    partners = [{"shard": across(me, b)} for b in range(bits)] + [{"seq": across(place, t)} for t in range(turns)]
    others = [{"shard": lax.rem(me + k, count)} for k in range(1, count)]
    greeted = others + partners[bits:]
    barrier = pltpu.get_barrier_semaphore()
    for partner in greeted:
        pl.semaphore_signal(barrier, inc=1, device_id=partner, device_id_type=MESH)
    pl.semaphore_wait(barrier, len(greeted))

    pieces = []
    offset = 0
    for source, out, (rows, cut) in zip(sources, outs, sizes):
        for start in range(0, rows, cut):
            pieces.append((source, out, start, offset + start, cut))
        offset += rows
    orders = [list(range(bits)), list(range(bits))]
    if bits > 2:
        orders[1] = [0] + list(range(2, bits)) + [1]
    flights = {}

    def moves(piece, level):
        order = orders[1 if piece % 5 == OTHER else 0]
        if level >= bits:
            return [(0, 0)], partners[level]
        bit = order[level]
        left = sorted(order[level:])
        low = 2 ** left.index(bit)
        side = (me // 2**bit) % 2
        pairs = []
        for j in range(2 ** (bits - level - 1)):
            base = (j // low) * 2 * low + j % low
            pairs.append((base + side * low, base + (1 - side) * low))
        return pairs, partners[bit]

    def data(piece, level, index):
        source, _, start, spot, cut = pieces[piece]
        if level == 0:
            return source.at[index, pl.ds(start, cut)]
        return held[level - 1].at[index, pl.ds(spot, cut)]

    def launch(piece, level):
        pairs, partner = moves(piece, level)
        _, _, _, spot, cut = pieces[piece]
        copies = []
        for j, (_, sent) in enumerate(pairs):
            copies.append(
                pltpu.make_async_remote_copy(
                    src_ref=data(piece, level, sent),
                    dst_ref=held[level].at[j, pl.ds(spot, cut)],
                    send_sem=send_sem.at[piece, level, j],
                    recv_sem=recv_sem.at[piece, level, j],
                    device_id=partner,
                    device_id_type=MESH,
                )
            )
        for copy in copies:
            copy.start()
        flights[piece, level] = copies

    def absorb(piece, level):
        pairs, _ = moves(piece, level)
        _, out, start, spot, cut = pieces[piece]
        for j, (kept, _) in enumerate(pairs):
            flights[piece, level][j].wait()
            mine, other = data(piece, level, kept)[...], held[level][j, pl.ds(spot, cut)]
            if level == levels - 1:
                out[pl.ds(start, cut)] = mine.astype(jnp.float32) + other.astype(jnp.float32)
            else:
                held[level][j, pl.ds(spot, cut)] = mine + other

    def trade_all(source, target_ref, send, recv):
        copies = [pltpu.make_async_copy(source.at[me], target_ref.at[me], send.at[0])]
        for k in range(1, count):
            target = lax.rem(me + k, count)
            copies.append(
                pltpu.make_async_remote_copy(
                    src_ref=source.at[target],
                    dst_ref=target_ref.at[me],
                    send_sem=send.at[k],
                    recv_sem=recv.at[k],
                    device_id={"shard": target},
                    device_id_type=MESH,
                )
            )
        for copy in copies:
            copy.start()
        return copies

    def wait_all(copies):
        for copy in copies:
            copy.wait()

    if parts:
        left_ref, first_ref, second_ref, right_ref = basis
        held_rows, whole, turned_rows, near_send, near_recv, back_send, back_recv, other_rows, far_send, far_recv = rest
        part = lax.rem(me, parts)
        columns = give_ref.shape[2]

        def ask_far():
            wait_all(away[0])
            copy = pltpu.make_async_remote_copy(
                src_ref=held_rows,
                dst_ref=other_rows,
                send_sem=far_send,
                recv_sem=far_recv,
                device_id=partners[bits],
                device_id_type=MESH,
            )
            copy.start()
            away.append([copy])

        def gather_near():
            wait_all(away[1])
            total = held_rows[...].astype(jnp.float32) + other_rows[...].astype(jnp.float32)
            whole[part] = total.astype(jnp.bfloat16).reshape(D, columns)
            copies = []
            for j in range(1, parts):
                copies.append(
                    pltpu.make_async_remote_copy(
                        src_ref=whole.at[part],
                        dst_ref=whole.at[part],
                        send_sem=near_send.at[j],
                        recv_sem=near_recv.at[j],
                        device_id={"shard": me - part + lax.rem(part + j, parts)},
                        device_id_type=MESH,
                    )
                )
                copies[-1].start()
            away.append(copies)

        def own_columns(values):
            kept = values[:, 0:columns]
            for j in range(1, parts):
                kept = jnp.where(part == j, values[:, j * columns : (j + 1) * columns], kept)
            return kept.astype(jnp.bfloat16)

        def turn():
            wait_all(away[2])
            grad = jnp.concatenate([whole[j] for j in range(parts)], 1)
            left, right = left_ref[...], right_ref[...]
            rotated = mm(mm(left, grad).astype(jnp.bfloat16), right)
            share = rule(first_ref[...].astype(jnp.float32), second_ref[...].astype(jnp.float32), rotated)[0]
            back = own_columns(mm(share.astype(jnp.bfloat16), right, NT))
            turned_rows[:, 0] = own_columns(rotated).reshape(count, -1, columns)
            turned_rows[:, 1] = mm(turned(left), back).astype(jnp.bfloat16).reshape(count, -1, columns)
            away.append(trade_all(turned_rows, take_ref, back_send, back_recv))

        away = [trade_all(give_ref, held_rows, give_sem, take_sem)]
        between = {GATHER_AT: ask_far, GATHER_AT + 2: gather_near, GATHER_AT + 3: turn}
    else:
        away = [trade_all(give_ref, take_ref, give_sem, take_sem)]
        between = {}
    delay = [0, 1] + [1 + AHEAD * level for level in range(1, levels)]
    for wave in range(len(pieces) + delay[-1]):
        if wave in between:
            between[wave]()
        for level in range(levels, -1, -1):
            piece = wave - delay[level]
            if 0 <= piece < len(pieces):
                if level > 0:
                    absorb(piece, level - 1)
                if level < levels:
                    launch(piece, level)
    wait_all(away[-1])


def reduce_chunks(mesh_sizes, cuts, chunks, give, parts, rule, basis):
    count, seqs = mesh_sizes
    bits, turns = count.bit_length() - 1, seqs.bit_length() - 1
    lanes = chunks[0].shape[2]
    sizes = [(c.shape[1], cut) for c, cut in zip(chunks, cuts)]
    total = sum(rows for rows, _ in sizes)
    number = sum(rows // cut for rows, cut in sizes)
    slots = [2 ** (bits - 1 - level) for level in range(bits)] + [1] * turns
    spec = pl.BlockSpec(memory_space=pltpu.VMEM)
    scratch = [pltpu.VMEM((n, total, lanes), jnp.bfloat16) for n in slots]
    scratch += [pltpu.SemaphoreType.DMA((number, bits + turns, count // 2))] * 2
    scratch += [pltpu.SemaphoreType.DMA((count,))] * 2
    taken = give.shape
    if parts:
        _, depth, columns = give.shape
        taken = (count, 2, depth, columns)
        scratch += [
            pltpu.VMEM(give.shape, jnp.bfloat16),
            pltpu.VMEM((parts, D, columns), jnp.bfloat16),
            pltpu.VMEM(taken, jnp.bfloat16),
        ]
        scratch += [pltpu.SemaphoreType.DMA((parts,))] * 2 + [pltpu.SemaphoreType.DMA((count,))] * 2
        scratch += [pltpu.VMEM(give.shape, jnp.bfloat16)] + [pltpu.SemaphoreType.DMA] * 2
    return pl.pallas_call(
        functools.partial(reduce_kernel, count, seqs, sizes, parts, rule),
        in_specs=[spec] * (len(chunks) + 1 + len(basis)),
        out_specs=[spec] * (len(chunks) + 1),
        out_shape=[jax.ShapeDtypeStruct(c.shape[1:], jnp.float32) for c in chunks]
        + [jax.ShapeDtypeStruct(taken, give.dtype)],
        scratch_shapes=scratch,
        cost_estimate=SMALL_COST,
        compiler_params=pltpu.CompilerParams(collective_id=0, has_side_effects=True, vmem_limit_bytes=VMEM),
        name="reduce_chunks",
    )(*chunks, give, *basis)


def finish_kernel(rules, parts, shapes, *refs):
    number = len(shapes)
    small_ref, conv_sum_ref, take_ref = refs[:3]
    ins = [refs[3 + 3 * i : 6 + 3 * i] for i in range(number + 3)]
    outs = [refs[3 * number + 12 + 3 * i : 3 * number + 15 + 3 * i] for i in range(number + 3)]
    conv_rule, turned_rule, vector_rule, small_rules = rules

    def put(at, values):
        for ref, value in zip(outs[at], values):
            ref[...] = value

    put(0, conv_rule(ins[0][0][...], conv_sum_ref[...].T, ins[0][1][...], ins[0][2][...]))
    for m in range(ins[1][0].shape[0]):
        rotated = jnp.concatenate([take_ref[m * parts + j, 0] for j in range(parts)], 1).astype(jnp.float32)
        update = jnp.concatenate([take_ref[m * parts + j, 1] for j in range(parts)], 1).astype(jnp.float32)
        weight, first, second = turned_rule(ins[1][0][m], update, ins[1][1][m], ins[1][2][m], rotated)
        outs[1][0][m] = weight
        outs[1][1][m] = first
        outs[1][2][m] = second
    taps = small_ref.shape[1]
    start = 0
    for i, (depth, width) in enumerate(shapes):
        count = -(-width // taps)
        grad = jnp.concatenate([small_ref[start + j * depth : start + (j + 1) * depth, :] for j in range(count)], 1)
        start += count * depth
        put(3 + i, small_rules[i](ins[3 + i][0][...], grad[:, :width], ins[3 + i][1][...], ins[3 + i][2][...]))
    size = ins[2][0].shape[1]
    count = -(-size // taps)
    grad = jnp.concatenate([small_ref[start + j : start + j + 1, :] for j in range(count)], 1)[:, :size]
    put(2, vector_rule(ins[2][0][...], grad, ins[2][1][...], ins[2][2][...]))


def finish(rules, parts, small_sum, conv_sum, take, conv, attention, vector, small):
    vector = tuple(v.reshape(1, -1) for v in vector)
    operands = list(conv) + list(attention) + list(vector) + [item for triple in small for item in triple]
    shapes = [triple[0].shape for triple in small]
    results = pl.pallas_call(
        functools.partial(finish_kernel, rules, parts, shapes),
        out_shape=[jax.ShapeDtypeStruct(item.shape, jnp.float32) for item in operands],
        cost_estimate=SMALL_COST,
        compiler_params=pltpu.CompilerParams(vmem_limit_bytes=VMEM),
        name="finish",
    )(small_sum, conv_sum, take, *operands)
    triples = [tuple(results[3 * i : 3 * i + 3]) for i in range(len(results) // 3)]
    triples[2] = tuple(v.reshape(-1) for v in triples[2])
    return triples


def swap_moves(count, step):
    return [(i, (i - step) % count) for i in range(count)]


def gather_ring(block):
    count = lax.axis_size("seq")
    return [block] + [lax.ppermute(block, "seq", swap_moves(count, step)) for step in range(1, count)]


def return_ring(blocks):
    count = lax.axis_size("seq")
    return [lax.ppermute(block, "seq", swap_moves(count, -step)) for step, block in enumerate(blocks) if step > 0]


def seq_sum(values):
    if lax.axis_size("seq") > 2:
        return lax.psum(values, "seq").astype(jnp.float32)
    other = lax.ppermute(values, "seq", [(0, 1), (1, 0)])
    return values.astype(jnp.float32) + other.astype(jnp.float32)


def lowered(values):
    return values.astype(jnp.bfloat16)


def bdot(left_side, right_side):
    return jnp.dot(left_side, right_side, preferred_element_type=jnp.float32)


def turned_dot(left_side, right_side):
    return lax.dot_general(left_side, right_side, NT, preferred_element_type=jnp.float32)


def rows_dot(left_side, right_side):
    return lax.dot_general(left_side, right_side, (((0,), (0,)), ((), ())), preferred_element_type=jnp.float32)


def fdot(left_side, right_side):
    return jnp.dot(left_side, right_side, precision=lax.Precision.HIGHEST, preferred_element_type=jnp.float32)


def column_sum(values):
    return jnp.sum(values.astype(jnp.float32), 0, keepdims=True)


def norm_forward(values, gain_row, bias_row):
    centred = values - jnp.mean(values, -1, keepdims=True)
    spread = jnp.mean(centred * centred, -1, keepdims=True)
    scale = lax.rsqrt(spread + norm_epsilon)
    level = centred * scale
    return level * gain_row + bias_row, (level, scale, gain_row)


def norm_vectors(grad, kept):
    level = kept[0]
    return jnp.sum(grad * level, 0, keepdims=True), jnp.sum(grad, 0, keepdims=True)


def norm_backward(grad, kept):
    level, scale, gain_row = kept
    inside = grad * gain_row
    centred = inside - jnp.mean(inside, -1, keepdims=True) - level * jnp.mean(inside * level, -1, keepdims=True)
    return (scale * centred,) + norm_vectors(grad, kept)


def unit_rows(values):
    return values * lax.rsqrt(jnp.sum(values * values, -1, keepdims=True) + unit_epsilon)


def vector_pieces(vector):
    widths = [CIN, CIN, D, D, D, D, D] + [D, D, D, D, D, FF, D, D, D] * LAYERS + [PROJ, PROJ]
    pieces = []
    offset = 0
    for width in widths:
        pieces.append(vector[offset : offset + width])
        offset = offset + width
    return pieces


def with_halo(block, width):
    count = lax.axis_size("seq")
    forward = [(i, i + 1) for i in range(count - 1)]
    backward = [(i + 1, i) for i in range(count - 1)]
    low = lax.ppermute(block[:, block.shape[1] - width :], "seq", forward)
    high = lax.ppermute(block[:, :width], "seq", backward)
    return jnp.concatenate([low, block, high], axis=1)


def layer_forward(hidden, hidden_low, weights, pieces, clip_count, waiting):
    attn_w, expand_w, shrink_w = weights
    q_bias, v_bias, o_bias, gain_one, bias_one, expand_bias, shrink_bias, gain_two, bias_two = pieces
    entries = gather_ring(hidden_low)
    query = lowered(bdot(entries[0], attn_w[:, :D]) + q_bias)
    keys = [lowered(bdot(entry, attn_w[:, D : 2 * D])) for entry in entries]
    values = [lowered(bdot(entry, attn_w[:, 2 * D : 3 * D]) + v_bias) for entry in entries]
    mixed, stat = attend(query, keys, values, clip_count)
    if waiting is not None:
        mixed, waiting = fence(mixed, waiting)
    branch = bdot(mixed, attn_w[:, 3 * D :]) + o_bias
    middle, middle_kept = norm_forward(hidden + branch, gain_one, bias_one)
    middle_low = lowered(middle)
    inner = bdot(middle_low, expand_w) + expand_bias
    activated, slope = gelu_parts(inner)
    active_low = lowered(activated)
    slope_low = lowered(slope)
    outer = bdot(active_low, shrink_w) + shrink_bias
    result, final_kept = norm_forward(middle + outer, gain_two, bias_two)
    cache = (entries, query, keys, values, mixed, stat, middle_kept, middle_low, slope_low, active_low, final_kept)
    return result, lowered(result), cache, waiting


def feed_backward(grad_out, cache, expand_w, shrink_w):
    middle_low, slope_low, active_low, final_kept = cache[7:]
    grad_sum, grad_gain, grad_bias = norm_backward(grad_out, final_kept)
    grad_outer = lowered(grad_sum)
    grad_shrink = lowered(rows_dot(active_low, grad_outer))
    grad_inner = lowered(slope_low.astype(jnp.float32) * turned_dot(grad_outer, shrink_w))
    grad_expand = lowered(rows_dot(middle_low, grad_inner))
    grad_middle = grad_sum + turned_dot(grad_inner, expand_w)
    vectors = [column_sum(grad_inner), column_sum(grad_outer), grad_gain, grad_bias]
    return grad_middle, grad_expand, grad_shrink, vectors


def attend_backward(grad_middle, cache, attn_w, clip_count, *waiting):
    entries, query, keys, values, mixed, stat, middle_kept = cache[:7]
    grad_sum, grad_gain, grad_bias = norm_backward(grad_middle, middle_kept)
    grad_branch = lowered(grad_sum)
    grad_mixed = lowered(turned_dot(grad_branch, attn_w[:, 3 * D :]))
    results = attend_back(query, grad_mixed, stat, keys, values, clip_count)
    results, grad_branch, *waiting = fence(results, grad_branch, *waiting)
    grad_query, grad_keys, grad_values = results[0], results[1::2], results[2::2]
    back = [
        turned_dot(dk, attn_w[:, D : 2 * D]) + turned_dot(dv, attn_w[:, 2 * D : 3 * D])
        for dk, dv in zip(grad_keys, grad_values)
    ]
    arrived = return_ring([lowered(block) for block in back])
    grad_hidden = grad_sum + turned_dot(grad_query, attn_w[:, :D]) + back[0]
    for block in arrived:
        grad_hidden = grad_hidden + block.astype(jnp.float32)
    grads = [
        lowered(rows_dot(entries[0], grad_query)),
        lowered(sum(rows_dot(entry, dk) for entry, dk in zip(entries, grad_keys))),
        lowered(sum(rows_dot(entry, dv) for entry, dv in zip(entries, grad_values))),
        lowered(rows_dot(mixed, grad_branch)),
    ]
    vectors = [
        column_sum(grad_query),
        sum(column_sum(dv) for dv in grad_values),
        column_sum(grad_branch),
        grad_gain,
        grad_bias,
    ]
    return grad_hidden, grads, vectors, waiting


def fused_forward(hidden, hidden_low, weights, pieces, clip_count, waiting):
    attn_whole, feed_whole, first = weights
    place = 0
    none = jnp.zeros_like(pieces[0])
    entries = [hidden_low]
    packs = [project(hidden_low, attn_whole, place, [pieces[0], none, pieces[1]])]
    for entry in gather_ring(hidden_low)[1:]:
        entries.append(entry)
        packs.append(project(entry, attn_whole, place + 1, [none, pieces[1]]))
    query = (packs[0], 0)
    keys = [(pack, 1 if j == 0 else 0) for j, pack in enumerate(packs)]
    values = [(pack, 2 if j == 0 else 1) for j, pack in enumerate(packs)]
    mixed, stat = attend(query, keys, values, clip_count)
    if waiting is not None:
        mixed, waiting = fence(mixed, waiting)
    low, level1, scale1, active, slope, result, result_low, level2, scale2 = feed_forward(
        hidden, mixed, attn_whole, feed_whole, first, place, pieces[2:]
    )
    cache = (entries, query, keys, values, mixed, stat, (level1, scale1, low, slope, active, level2, scale2))
    return result, result_low, cache, waiting


def fused_backward(grads, cache, weights, pieces, clip_count, chunks, room, waiting):
    attn_whole, feed_whole, first = weights
    entries, query, keys, values, mixed, stat, kept = cache
    shards = lax.axis_size("shard")
    grad_sum, branch, grad_mixed, sums, grad_expand_bias, feed_chunks = feed_back(
        grads, kept, attn_whole, feed_whole, first, 0, pieces[3], pieces[7], chunks
    )
    if waiting is not None:
        grad_mixed, held = fence(grad_mixed, waiting[1])
        waiting = waiting[0](held)
    results = attend_back(query, grad_mixed, stat, keys, values, clip_count)
    if waiting is not None:
        results, waiting = fence(results, waiting)
    backs = entry_back(grad_sum, results[0], results[1:], attn_whole, 0)
    results, backs, branch = fence(results, backs, branch)
    arrived = return_ring(backs)
    attn_chunks, more = attn_grads(entries, results[0], mixed, branch, results[1:], shards, room)
    arrived, more = fence(arrived, more)
    vectors = [more[0:1], more[1:2], sums[0:1], sums[1:2], sums[2:3], grad_expand_bias, sums[3:4], sums[4:5], sums[5:6]]
    return [backs[0]] + arrived, feed_chunks, attn_chunks, vectors, waiting


def plain_backward(grads, cache, weights, pieces, clip_count, chunks, room, waiting):
    attn_w, expand_w, shrink_w = weights
    shards = lax.axis_size("shard")
    grad = grads[0]
    for part in grads[1:]:
        grad = grad + part.astype(jnp.float32)
    grad_middle, grad_expand, grad_shrink, feed_vectors = feed_backward(grad, cache, expand_w, shrink_w)
    rest = [] if waiting is None else [waiting[0](waiting[1])]
    grad_hidden, attn_list, attn_vectors, rest = attend_backward(grad_middle, cache, attn_w, clip_count, *rest)
    blocks = [] if chunks is None else [chunks]
    blocks += [grad_expand[:, j * D : (j + 1) * D].reshape(shards, -1, D) for j in range(FF // D)]
    blocks.append(grad_shrink.reshape(shards, -1, D))
    attn_chunks = jnp.concatenate([item.reshape(shards, -1, D) for item in attn_list], 1)
    vectors = attn_vectors + feed_vectors
    return [grad_hidden], jnp.concatenate(blocks, 1), attn_chunks, vectors, rest[0] if rest else None


def adam_update(weight, grad, first, second, rate, decay):
    first = beta_one * first + (1 - beta_one) * grad
    second = beta_two * second + (1 - beta_two) * grad * grad
    share_fraction = (
        first / (1 - beta_one**STEP) / (jnp.sqrt(second / (1 - beta_two**STEP)) + adam_epsilon)
    )
    return (weight - rate * (share_fraction + decay * weight), first, second)


def matrix_rule(weight, grad, first, second):
    return adam_update(weight, grad, first, second, rate_matrix, decay_rate)


def target_rule(weight, grad, first, second):
    return adam_update(weight, grad, first, second, rate_target, decay_rate)


def codebook_rule(weight, grad, first, second):
    return adam_update(weight, grad, first, second, rate_codebook, decay_rate)


def vector_rule(weight, grad, first, second):
    return adam_update(weight, grad, first, second, rate_vector, 0.0)


def rotated_adam(first, second, grad):
    first = beta_rotated * first + (1 - beta_rotated) * grad
    second = beta_rotated * second + (1 - beta_rotated) * grad * grad
    share = first / (1 - beta_rotated**STEP) / (jnp.sqrt(second / (1 - beta_rotated**STEP)) + adam_epsilon)
    return share, first, second


def attention_rule(weight, update, first, second, rotated):
    _, first, second = rotated_adam(first, second, rotated)
    return weight - rate_rotated * update, first, second


def gather_rows(block):
    whole = lax.all_gather(block, "shard", axis=0, tiled=True)
    return whole.reshape((-1,) + block.shape)


def pass_kernel(*refs):
    pass


def fence(*values):
    flat, tree = jax.tree.flatten(values)
    spec = pl.BlockSpec(memory_space=pl.ANY)
    flat = pl.pallas_call(
        pass_kernel,
        in_specs=[spec] * len(flat),
        out_specs=[spec] * len(flat),
        out_shape=[jax.ShapeDtypeStruct(v.shape, v.dtype) for v in flat],
        input_output_aliases={i: i for i in range(len(flat))},
        cost_estimate=SMALL_COST,
        name="fence",
    )(*flat)
    return jax.tree.unflatten(tree, flat)


def scatter_chunks(chunks):
    return lax.psum_scatter(chunks, "shard", scatter_dimension=0, tiled=False)


def trade(chunks):
    return lax.all_to_all(chunks, "shard", split_axis=0, concat_axis=0, tiled=True)


def on_device(
    features,
    time_mask,
    negatives,
    target_codes,
    feature_weight,
    feature_first,
    feature_second,
    conv_weight,
    conv_first,
    conv_second,
    attention_weight,
    attention_first,
    attention_second,
    left_basis_t,
    right_orthogonal_basis,
    expand_weight,
    expand_first,
    expand_second,
    shrink_weight,
    shrink_first,
    shrink_second,
    final_weight,
    final_first,
    final_second,
    target_weight,
    target_first,
    target_second,
    codebook_weight,
    codebook_first,
    codebook_second,
    vector_params,
    vector_first,
    vector_second,
):
    clip_count, frame_count = (features.shape[0], features.shape[1])
    row_count = clip_count * frame_count
    seq_count = lax.axis_size("seq")
    shards = lax.axis_size("shard")
    clip_frames = frame_count * seq_count
    taps = conv_weight.shape[0]
    small_items = [feature_weight, final_weight, target_weight, codebook_weight]

    def split_small(packed):
        blocks = []
        start = 0
        for item in small_items:
            depth, width = item.shape
            count = -(-width // taps)
            pieces = [packed[..., start + j * depth : start + (j + 1) * depth, :] for j in range(count)]
            blocks.append(jnp.concatenate(pieces, -1)[..., :width])
            start += count * depth
        size = vector_params.shape[0]
        count = -(-size // taps)
        vector = packed[..., start : start + count, :].reshape(packed.shape[:-2] + (-1,))[..., :size]
        return blocks, vector, packed[..., start + count, :2]

    parts = shards // (4 * LAYERS)
    rows = D // shards

    def own_attn(layer):
        return jnp.concatenate([lowered(attention_weight[4 * layer + i]) for i in range(4)])

    def own_feed(layer):
        expand_own = lowered(expand_weight[layer])
        return jnp.concatenate(
            [expand_own[:, j * D : (j + 1) * D] for j in range(FF // D)] + [lowered(shrink_weight[layer])]
        )

    first_all = gather_rows(pack_weights(conv_weight, small_items, vector_params, SMALL_ROWS))
    conv_w = first_all
    blocks, vector_low, _ = split_small(first_all[:, D:])
    feat_w, final_w, target_w, code_w = [block.reshape(-1, block.shape[-1]) for block in blocks]

    def cut_halves(block):
        number = block.shape[1]
        cut = block.reshape(4 * LAYERS, number, rows, parts, D // parts).transpose(0, 3, 1, 2, 4)
        return cut.reshape(shards, number, rows, D // parts)

    def spread_halves(block):
        return trade(cut_halves(block))

    def join_halves(got):
        number = got.shape[1]
        got = got.transpose(1, 0, 2, 3).reshape(number, D, D // parts)
        if parts != 2:
            groups = [[i * parts + j for j in range(parts)] for i in range(shards // parts)]
            return lax.all_gather(got, "shard", axis=2, tiled=True, axis_index_groups=groups)
        other = lax.ppermute(got, "shard", [(i, i ^ 1) for i in range(shards)])
        second = lax.axis_index("shard") % 2 == 1
        return jnp.concatenate([jnp.where(second, other, got), jnp.where(second, got, other)], 2)

    def plain_weights(attn_whole, feed_whole):
        blocks = [attn_whole[:, j * rows : (j + 1) * rows].reshape(D, D) for j in range(4)]
        columns = [feed_whole[:, j * rows : (j + 1) * rows].reshape(D, D) for j in range(FF // D)]
        shrink = feed_whole[:, FF // D * rows :].reshape(FF, D)
        return jnp.concatenate(blocks, 1), jnp.concatenate(columns, 1), shrink

    first_frame = lax.axis_index("seq") * frame_count
    ring_draws = (negatives - first_frame + clip_frames) % clip_frames
    counts = count_draws(ring_draws.transpose(0, 2, 1), clip_frames)
    held = jnp.stack([lowered(left_basis_t), lowered(attention_first), lowered(attention_second)], 1)
    counts, own_0 = fence(counts, jnp.concatenate([own_attn(0), own_feed(0)]))
    whole_0 = gather_rows(own_0)
    fused = rows % 16 == 0
    weights = [(whole_0, whole_0, 4) if fused else plain_weights(whole_0[:, : 4 * rows], whole_0[:, 4 * rows :])]

    pieces = vector_pieces(vector_low.reshape(-1).astype(jnp.float32))
    mask_on = (time_mask > 0).reshape(row_count, 1)
    feats = features.reshape(row_count, CIN).astype(jnp.float32)
    normed, norm_kept = norm_forward(feats, pieces[0], pieces[1])
    normed_low = lowered(normed)
    projected = bdot(normed_low, feat_w) + pieces[2]
    masked = jnp.where(mask_on, pieces[3][None, :], projected)
    padded = with_halo(lowered(masked).reshape(clip_count, frame_count, D), KW // 2)
    strip_rows = frame_count * clip_count // 16 // PACK
    strips = to_strips(padded, frame_count)
    conv_out = from_strips(conv_forward(strips, conv_w, 0, strip_rows, shards), clip_count) + pieces[4]
    conv_active, conv_slope = gelu_parts(conv_out)
    hidden, front_kept = norm_forward(masked + conv_active, pieces[5], pieces[6])

    hidden_low = lowered(hidden)
    codes = jnp.concatenate(gather_ring(target_codes), 1).reshape(clip_count * clip_frames, QGROUPS)
    width = PROJ // QGROUPS
    code_f = code_w.astype(jnp.float32)
    target_f = target_w.astype(jnp.float32)
    table = jnp.concatenate(
        [fdot(code_f[g * width : (g + 1) * width].T, target_f[g * width : (g + 1) * width]) for g in range(QGROUPS)]
    )
    choice = jnp.concatenate(
        [(codes[:, g : g + 1] == jnp.arange(CODES)[None, :]).astype(jnp.float32) for g in range(QGROUPS)], 1
    )
    raw_targets = fdot(choice, table) + pieces[-1]
    target_kept = lax.rsqrt(jnp.sum(raw_targets * raw_targets, -1, keepdims=True) + unit_epsilon)
    targets = raw_targets * target_kept
    forward = fused_forward if fused else layer_forward
    hidden, hidden_low, own_1 = fence(hidden, hidden_low, own_attn(1))
    attn_whole_1 = gather_rows(own_1)
    hidden, hidden_low, cache, own_1 = forward(hidden, hidden_low, weights[0], pieces[7:16], clip_count, own_feed(1))
    feed_whole_1 = gather_rows(own_1)
    caches = [cache]
    weights.append((attn_whole_1, feed_whole_1, 0) if fused else plain_weights(attn_whole_1, feed_whole_1))
    hidden, top_low, cache, (targets, target_kept) = forward(
        hidden, hidden_low, weights[1], pieces[16:25], clip_count, (targets, target_kept)
    )
    caches.append(cache)
    context, context_pull = jax.vjp(unit_rows, bdot(top_low, final_w) + pieces[-2])
    context_low = lowered(context).reshape(clip_count, frame_count, PROJ)

    counts = counts.astype(jnp.float32)
    targets_low = lowered(targets).reshape(clip_count, clip_frames, PROJ)
    similar = jnp.einsum("clp,cfp->clf", targets_low, context_low, preferred_element_type=jnp.float32)
    logits = similar / contrastive_sharpness
    place = jnp.arange(clip_frames)[:, None] == jnp.arange(frame_count)[None, :]
    own = place.astype(jnp.float32)[None]
    weight = counts + own
    largest = jnp.max(jnp.where(weight > 0, logits, -jnp.inf), 1, keepdims=True)
    power = weight * jnp.exp(jnp.where(weight > 0, logits - largest, 0.0))
    running_totals = jnp.sum(power, 1, keepdims=True)
    mask_as_floats = time_mask.astype(jnp.float32)
    own_logit = jnp.sum(own * logits, 1)
    row_loss = largest[:, 0] + jnp.log(running_totals[:, 0]) - own_logit
    loss_sum = jnp.sum(mask_as_floats * row_loss)
    mask_count = jnp.sum(mask_as_floats)
    derivative_multiplier = 1.0 / (clip_count * shards * clip_frames)
    grad_similar = lowered(
        mask_as_floats[:, None, :]
        * (power / running_totals - own)
        * (derivative_multiplier / contrastive_sharpness)
    )
    grad_context = jnp.einsum("clf,clp->cfp", grad_similar, targets_low, preferred_element_type=jnp.float32)
    grad_targets = jnp.einsum("clf,cfp->clp", grad_similar, context_low, preferred_element_type=jnp.float32)
    grad_targets = grad_targets.reshape(-1, PROJ)
    grad_raw = target_kept * (grad_targets - targets * jnp.sum(grad_targets * targets, -1, keepdims=True))
    grad_table = fdot(choice.T, grad_raw)
    tables = [grad_table[g * CODES : (g + 1) * CODES] for g in range(QGROUPS)]
    grad_target_w = jnp.concatenate([fdot(code_f[g * width : (g + 1) * width], tables[g]) for g in range(QGROUPS)])
    grad_codebook = jnp.concatenate(
        [fdot(target_f[g * width : (g + 1) * width], tables[g].T) for g in range(QGROUPS)]
    )
    grad_target_bias = column_sum(grad_raw)
    (grad_context_raw,) = context_pull(grad_context.reshape(row_count, PROJ))
    grad_context_low = lowered(grad_context_raw)
    grad_final_w = rows_dot(top_low, grad_context_low)
    grad_final_bias = column_sum(grad_context_low)
    grad_hidden = turned_dot(grad_context_low, final_w)

    columns = D // parts
    group = lax.axis_index("shard") // parts
    right_low = lowered(lax.dynamic_index_in_dim(right_orthogonal_basis, group, 0, keepdims=False))

    def rotate(whole_grad):
        left_low, first_low, second_low = traded[0], traded[1], traded[2]
        rotated = bdot(lowered(bdot(left_low, whole_grad)), right_low)
        direction = rotated_adam(first_low.astype(jnp.float32), second_low.astype(jnp.float32), rotated)[0]
        half_back = lowered(turned_dot(lowered(direction), right_low))
        part_start = (lax.axis_index("shard") % parts) * columns
        rotated_part = lax.dynamic_slice_in_dim(lowered(rotated), part_start, columns, 1)
        update_part = lowered(rows_dot(left_low, lax.dynamic_slice_in_dim(half_back, part_start, columns, 1)))
        sent = jnp.stack([rotated_part.reshape(shards, rows, columns), update_part.reshape(shards, rows, columns)], 1)
        return sent

    backward = fused_backward if fused else plain_backward
    grads, chunks, attn_chunks, vectors_1, _ = backward(
        [grad_hidden], caches[1], weights[1], pieces[16:25], clip_count, None, 4 * rows + 8 * rows * fused, None
    )
    (chunks,) = fence(chunks)
    sum_feed_1 = scatter_chunks(chunks)
    grads, chunks, attn_chunks, vectors_0, traded = backward(
        grads, caches[0], weights[0], pieces[7:16], clip_count, attn_chunks, 4 * rows, (spread_halves, held)
    )
    (chunks,) = fence(chunks)
    sum_feed_0 = scatter_chunks(chunks)
    (attn_chunks,) = fence(attn_chunks)
    sum_attn = scatter_chunks(attn_chunks)
    grad_hidden = grads[0]
    for part in grads[1:]:
        grad_hidden = grad_hidden + part.astype(jnp.float32)
    grad_sum, grad_gain_enc, grad_bias_enc = norm_backward(grad_hidden, front_kept)
    grad_conv_low = lowered(grad_sum * conv_slope)
    grad_strips = to_strips(with_halo(grad_conv_low.reshape(clip_count, frame_count, D), KW // 2), frame_count)
    conv_chunks = conv_weight_grad(strips, grad_strips, strip_rows, shards)
    grad_strips, conv_chunks, sum_feed_1 = fence(grad_strips, conv_chunks, sum_feed_1)
    grad_back = conv_input_grad(grad_strips, conv_w, 0, strip_rows, shards)
    traded = join_halves(traded)
    sum_feed_1 = seq_sum(sum_feed_1)
    grad_back, sum_feed_1, sum_feed_0, traded = fence(grad_back, sum_feed_1, sum_feed_0, traded)
    grad_masked = grad_sum + from_strips(grad_back, clip_count)
    grad_embedding = jnp.sum(jnp.where(mask_on, grad_masked, 0.0), 0, keepdims=True)
    grad_projected = lowered(jnp.where(mask_on, 0.0, grad_masked))
    grad_feat_w = rows_dot(normed_low, grad_projected)
    grad_gain_feat, grad_bias_feat = norm_vectors(turned_dot(grad_projected, feat_w), norm_kept)
    vector_grads = [
        grad_gain_feat,
        grad_bias_feat,
        column_sum(grad_projected),
        grad_embedding,
        column_sum(grad_conv_low),
        grad_gain_enc,
        grad_bias_enc,
    ]
    vector_grads += vectors_0 + vectors_1
    vector_grads += [grad_final_bias, grad_target_bias]
    extra = jnp.pad(jnp.stack([loss_sum, mask_count])[None], ((0, 0), (0, 126)))
    small_grads = [grad_feat_w, grad_final_w, grad_target_w, grad_codebook]
    small_chunks = pack_grads(small_grads, vector_grads, extra, shards, SMALL_ROWS, taps)
    inside = fused and seq_count == 2
    attn_1 = sum_feed_0[: 4 * rows]
    sum_feed_0 = seq_sum(sum_feed_0)
    small_chunks, sum_attn, sum_feed_0, attn_1 = fence(small_chunks, sum_attn, sum_feed_0, attn_1)
    if inside:
        attn_rows = jnp.concatenate([sum_attn, attn_1]).reshape(4 * LAYERS, 1, rows, D)
    else:
        attn_rows = jnp.concatenate([seq_sum(sum_attn), sum_feed_0[: 4 * rows]]).reshape(4 * LAYERS, 1, rows, D)
    mesh_sizes, cuts, last_chunks = (shards, seq_count), (SMALL_ROWS, 128), [small_chunks, conv_chunks]
    if inside:
        give = cut_halves(lowered(attn_rows)).reshape(shards, rows, columns)
        basis = [traded[0], traded[1], traded[2], right_low]
        small_sum, sum_conv, rotation = reduce_chunks(mesh_sizes, cuts, last_chunks, give, parts, rotated_adam, basis)
    else:
        sent = rotate(join_halves(spread_halves(lowered(attn_rows)))[0])
        small_sum, sum_conv, rotation = reduce_chunks(mesh_sizes, cuts, last_chunks, sent, 0, None, [])
    feed_sums = [sum_feed_0[4 * rows :], sum_feed_1]
    small_sums, sum_vector, sum_loss = split_small(small_sum)
    sum_expand = jnp.stack(
        [s[: -shrink_weight.shape[1]].reshape(FF // D, -1, D).transpose(1, 0, 2).reshape(-1, FF) for s in feed_sums]
    )
    sum_shrink = jnp.stack([s[-shrink_weight.shape[1] :] for s in feed_sums])
    expand_new = adam_update(expand_weight, sum_expand, expand_first, expand_second, rate_matrix, decay_rate)
    shrink_new = adam_update(shrink_weight, sum_shrink, shrink_first, shrink_second, rate_matrix, decay_rate)
    conv_all = (conv_weight, conv_first, conv_second)
    attention_all = (attention_weight, attention_first, attention_second)
    vector_all = (vector_params, vector_first, vector_second)
    small_all = [
        (feature_weight, feature_first, feature_second),
        (final_weight, final_first, final_second),
        (target_weight, target_first, target_second),
        (codebook_weight, codebook_first, codebook_second),
    ]
    small_rules = [matrix_rule, matrix_rule, target_rule, codebook_rule]
    if fused:
        rules = (matrix_rule, attention_rule, vector_rule, small_rules)
        results = finish(rules, parts, small_sum, sum_conv, rotation, conv_all, attention_all, vector_all, small_all)
        conv_new, attention_new, vector_new, feature_new, final_new, target_new, codebook_new = results
    else:
        arrived = rotation.reshape(4 * LAYERS, parts, 2, rows, columns).transpose(2, 0, 3, 1, 4)
        arrived = arrived.reshape(2, 4 * LAYERS, rows, D).astype(jnp.float32)
        attention_new = attention_rule(attention_weight, arrived[1], attention_first, attention_second, arrived[0])
        conv_new = turned_adam(matrix_rule, conv_weight, sum_conv, conv_first, conv_second)
        vector_new = vector_rule(vector_params, sum_vector, vector_first, vector_second)
        feature_new, final_new, target_new, codebook_new = [
            rule(triple[0], grad, triple[1], triple[2]) for rule, grad, triple in zip(small_rules, small_sums, small_all)
        ]
    return (
        (sum_loss,)
        + feature_new
        + conv_new
        + attention_new
        + expand_new
        + shrink_new
        + final_new
        + target_new
        + codebook_new
        + vector_new
    )


def solution(mesh):
    return jax.shard_map(
        on_device,
        mesh=mesh,
        in_specs=(
            P("shard", "seq", None),
            P("shard", "seq"),
            P("shard", "seq", None),
            P("shard", "seq", None),
            P("shard", None),
            P("shard", None),
            P("shard", None),
            P("shard", None),
            P("shard", None),
            P("shard", None),
            P(None, "shard", None),
            P(None, "shard", None),
            P(None, "shard", None),
            P(None, "shard", None),
            P(),
            P(None, "shard", None),
            P(None, "shard", None),
            P(None, "shard", None),
            P(None, "shard", None),
            P(None, "shard", None),
            P(None, "shard", None),
            P("shard", None),
            P("shard", None),
            P("shard", None),
            P("shard", None),
            P("shard", None),
            P("shard", None),
            P("shard", None),
            P("shard", None),
            P("shard", None),
            P("shard"),
            P("shard"),
            P("shard"),
        ),
        out_specs=(
            P(),
            P("shard", None),
            P("shard", None),
            P("shard", None),
            P("shard", None),
            P("shard", None),
            P("shard", None),
            P(None, "shard", None),
            P(None, "shard", None),
            P(None, "shard", None),
            P(None, "shard", None),
            P(None, "shard", None),
            P(None, "shard", None),
            P(None, "shard", None),
            P(None, "shard", None),
            P(None, "shard", None),
            P("shard", None),
            P("shard", None),
            P("shard", None),
            P("shard", None),
            P("shard", None),
            P("shard", None),
            P("shard", None),
            P("shard", None),
            P("shard", None),
            P("shard"),
            P("shard"),
            P("shard"),
        ),
        check_vma=False,
    )
```
